32 devices in a mesh: wide: 8 (over z, y), narrow: 4 (over x, core).
Axes of the slice: x: 2, y: 2, z: 4, core: 2. Of those that a mesh axis runs over, the one named last changes fastest.
Arguments:
- first_input: bfloat16 [3, 32, 32, 512], P(None, ('wide', 'narrow')), may hold values from -24 to 24
- second_input: bfloat16 [2, 64, 16, 512], P(None, ('wide', 'narrow')), may hold values from -24 to 24
- first_cotangent: bfloat16 [3, 32, 32, 512], P(None, ('wide', 'narrow')), may hold values from -6 to 6
- second_cotangent: bfloat16 [2, 64, 16, 512], P(None, ('wide', 'narrow')), may hold values from -6 to 6
- entry_gain: bfloat16 [512], P('narrow'), may hold values from 0.099609375 to 1.8984375
- entry_shift: bfloat16 [512], P('narrow'), may hold values from -3 to 3
- entry_kernel: bfloat16 [27, 512, 512], P(None, None, 'narrow'), may hold values from -0.0546875 to 0.0546875
- entry_bias: bfloat16 [512], P('narrow'), may hold values from -3 to 3
- exit_gain: bfloat16 [512], P('narrow'), may hold values from 0.099609375 to 1.8984375
- exit_shift: bfloat16 [512], P('narrow'), may hold values from -3 to 3
- exit_kernel: bfloat16 [27, 512, 512], P(None, None, 'narrow'), may hold values from -0.15625 to 0.15625
- exit_bias: bfloat16 [512], P('narrow'), may hold values from -3 to 3
Outputs:
- first_output: bfloat16 [3, 32, 32, 512], P(None, ('wide', 'narrow'))
- second_output: bfloat16 [2, 64, 16, 512], P(None, ('wide', 'narrow'))
- first_input_grad: bfloat16 [3, 32, 32, 512], P(None, ('wide', 'narrow'))
- second_input_grad: bfloat16 [2, 64, 16, 512], P(None, ('wide', 'narrow'))
- entry_gain_grad: float32 [512], P('narrow')
- entry_shift_grad: float32 [512], P('narrow')
- entry_kernel_grad: float32 [27, 512, 512], P(None, None, 'narrow')
- entry_bias_grad: float32 [512], P('narrow')
- exit_gain_grad: float32 [512], P('narrow')
- exit_shift_grad: float32 [512], P('narrow')
- exit_kernel_grad: float32 [27, 512, 512], P(None, None, 'narrow')
- exit_bias_grad: float32 [512], P('narrow')
The draws below stay inside these ranges and needn't reach their ends.
All inputs are finite; a program needn't handle non-finite values.
Results may differ from the reference program's by a relative error of at most 0.013.
Values may be sent and summed in bfloat16 or wider, within the bound.
A program may use at most 256 MiB of HBM per device.

```python
import jax
import jax.numpy as jnp
from jax import lax

CHANNELS = 512
GROUPS = 32
FRAMES_ONE = 3
HEIGHT_ONE = 32
WIDTH_ONE = 32
FRAMES_TWO = 2
HEIGHT_TWO = 16
WIDTH_TWO = 16
CLIPS_ONE = 1
CLIPS_TWO = 4


def shaped(key, noise, clip_height, offset_scale, rise):
    offset = jnp.clip(offset_scale * jax.random.normal(jax.random.fold_in(key, 5), (noise.shape[3],), jnp.float32), -2.0, 2.0)
    position = (jnp.arange(noise.shape[1]) % clip_height).astype(jnp.float32) / (clip_height - 1)
    factor = 1.0 + (rise - 1.0) * position
    return (noise + offset[None, None, None, :]) * factor[None, :, None, None]


def draw_first_input(key, part):
    key = jax.random.fold_in(key, 11)
    grid_shape = (FRAMES_ONE, CLIPS_ONE * HEIGHT_ONE, WIDTH_ONE, CHANNELS)
    noise = jnp.clip(jax.random.normal(key, grid_shape, jnp.float32), -4.0, 4.0)
    return shaped(key, noise, HEIGHT_ONE, 0.4, 3.0).astype(jnp.bfloat16)


def draw_second_input(key, part):
    key = jax.random.fold_in(key, 12)
    grid_shape = (FRAMES_TWO, CLIPS_TWO * HEIGHT_TWO, WIDTH_TWO, CHANNELS)
    noise = jnp.clip(jax.random.normal(key, grid_shape, jnp.float32), -4.0, 4.0)
    return shaped(key, noise, HEIGHT_TWO, 0.4, 3.0).astype(jnp.bfloat16)


def shard_levels(rng, extent, shards, smallest, largest):
    def one(dim, blocks):
        draws = jax.random.uniform(jax.random.fold_in(jax.random.fold_in(rng, 6), dim), (blocks,), jnp.float32, smallest / len(shards), largest / len(shards))
        return jnp.repeat(jnp.exp(draws), extent[dim] // blocks).reshape((-1,) + (1,) * (len(extent) - dim - 1))

    factor_of = one(*shards[0])
    for cut in shards[1:]:
        factor_of = factor_of * one(*cut)
    return factor_of


def bell_draw(stream_key, dims, spread, limit, shards=(), dtype=jnp.bfloat16):
    entries = spread * jax.random.normal(stream_key, dims, jnp.float32)
    if shards:
        entries = entries * shard_levels(stream_key, dims, shards, -0.22, 0.18)
    return jnp.clip(entries, -limit, limit).astype(dtype)


def setup_inputs(seed: int = 0) -> dict:
    arg_keys = jax.random.split(jax.random.key(seed), 13)
    return {
        "first_input": draw_first_input(jax.random.fold_in(arg_keys[12], 71), 0),
        "second_input": draw_second_input(jax.random.fold_in(arg_keys[12], 71), 0),
        "first_cotangent": bell_draw(arg_keys[2], (FRAMES_ONE, CLIPS_ONE * HEIGHT_ONE, WIDTH_ONE, CHANNELS), 1.0, 6.0, ((1, 32),)),
        "second_cotangent": bell_draw(arg_keys[3], (FRAMES_TWO, CLIPS_TWO * HEIGHT_TWO, WIDTH_TWO, CHANNELS), 1.0, 6.0, ((1, 32),)),
        "entry_gain": jnp.clip(1.0 + 0.18 * jax.random.normal(arg_keys[4], (CHANNELS,), jnp.float32), 0.099609375, 1.8984375).astype(jnp.bfloat16),
        "entry_shift": bell_draw(arg_keys[5], (CHANNELS,), 0.5, 3.0, ((0, 4),)),
        "entry_kernel": bell_draw(arg_keys[6], (27, CHANNELS, CHANNELS), (27 * CHANNELS) ** -0.5, 0.0546875, ((2, 4),)),
        "entry_bias": bell_draw(arg_keys[7], (CHANNELS,), 0.5, 3.0, ((0, 4),)),
        "exit_gain": jnp.clip(1.0 + 0.18 * jax.random.normal(arg_keys[8], (CHANNELS,), jnp.float32), 0.099609375, 1.8984375).astype(jnp.bfloat16),
        "exit_shift": bell_draw(arg_keys[9], (CHANNELS,), 0.5, 3.0, ((0, 4),)),
        "exit_kernel": bell_draw(arg_keys[10], (27, CHANNELS, CHANNELS), (27 * CHANNELS // 8) ** -0.5, 0.15625, ((2, 4),)),
        "exit_bias": bell_draw(arg_keys[11], (CHANNELS,), 0.5, 3.0, ((0, 4),)),
    }


epsilon = 1e-06

@jax.custom_vjp
def low(v):
    return lax.optimization_barrier(v.astype(jnp.bfloat16)).astype(jnp.float32)

@jax.custom_vjp
def low_back(v):
    return v

def low_keep(v):
    return (low(v), None)

def low_pass(kept, grad):
    return (grad,)

def back_keep(v):
    return (v, None)

def back_low(kept, grad):
    return (low(grad),)
low.defvjp(low_keep, low_pass)
low_back.defvjp(back_keep, back_low)

def swish(values):
    return values * jax.nn.sigmoid(values)

def group_norm(values, gain, shift, clip_count, clip_height):
    frame_count, all_rows, col_count, channels = values.shape
    grouped = values.reshape(frame_count, clip_count, clip_height, col_count, GROUPS, channels // GROUPS)
    group_mean = lax.optimization_barrier(jnp.mean(grouped, axis=(0, 2, 3, 5), keepdims=True))
    centered = grouped - group_mean
    variance = lax.optimization_barrier(jnp.mean(centered * centered, axis=(0, 2, 3, 5), keepdims=True))
    return (centered * lax.rsqrt(variance + epsilon)).reshape(values.shape) * gain + shift

def convolve(values, kernel, clip_count, clip_height):
    frame_count, all_rows, col_count, channels = values.shape
    clipped = values.reshape(frame_count, clip_count, clip_height, col_count, channels).transpose(1, 0, 2, 3, 4)
    result = lax.conv_general_dilated(clipped, kernel.reshape(3, 3, 3, channels, channels), (1, 1, 1), ((1, 1), (1, 1), (1, 1)), dimension_numbers=('NDHWC', 'DHWIO', 'NDHWC'), precision=lax.Precision.HIGHEST)
    return result.transpose(1, 0, 2, 3, 4).reshape(values.shape)

def residual_block(block_input, clip_count, clip_height, weights):
    entry_gain, entry_shift, entry_kernel, entry_bias, exit_gain, exit_shift, exit_kernel, exit_bias = weights
    active_one = low(swish(group_norm(block_input, entry_gain, entry_shift, clip_count, clip_height)))
    mid_values = low_back(convolve(active_one, entry_kernel, clip_count, clip_height) + entry_bias)
    active_two = low(swish(group_norm(mid_values, exit_gain, exit_shift, clip_count, clip_height)))
    return block_input + convolve(active_two, exit_kernel, clip_count, clip_height) + exit_bias

def reference(first_input, second_input, first_cotangent, second_cotangent, entry_gain, entry_shift, entry_kernel, entry_bias, exit_gain, exit_shift, exit_kernel, exit_bias):
    weights = tuple((weight.astype(jnp.float32) for weight in (entry_gain, entry_shift, entry_kernel, entry_bias, exit_gain, exit_shift, exit_kernel, exit_bias)))

    def forward(first_values, second_values, *params):
        return (residual_block(first_values, CLIPS_ONE, HEIGHT_ONE, params), residual_block(second_values, CLIPS_TWO, HEIGHT_TWO, params))
    outputs, pullback = jax.vjp(forward, first_input.astype(jnp.float32), second_input.astype(jnp.float32), *weights)
    grads = pullback((first_cotangent.astype(jnp.float32), second_cotangent.astype(jnp.float32)))
    return (outputs[0].astype(jnp.bfloat16), outputs[1].astype(jnp.bfloat16), grads[0].astype(jnp.bfloat16), grads[1].astype(jnp.bfloat16), grads[2], grads[3], grads[4], grads[5], grads[6], grads[7], grads[8], grads[9])
```

```python
import functools

import jax
import jax.numpy as jnp
from jax import lax
from jax.experimental import pallas as pl
from jax.experimental.pallas import tpu as pltpu
from jax.sharding import PartitionSpec as P

GROUPS = 32
HEIGHT_ONE = 32
HEIGHT_TWO = 16
CHANNELS = 512
NARROW = 4
BANDS = 8
SLICE = 128
FRAMES = 5
FIRST = 3
BAND = 128
OWN = 32
LONG = 192

EPS = 1e-06
F32 = jnp.float32
BF16 = jnp.bfloat16
MESH = pl.DeviceIdType.MESH

FORWARD = {
    1: ((0, 3, 0), (3, 5, 3)),
    0: ((0, 2, 1), (3, 4, 4)),
    2: ((1, 3, 0), (4, 5, 3)),
}
BACKWARD = {
    1: ((0, 3, 0), (3, 5, 3)),
    0: ((1, 3, 0), (4, 5, 3)),
    2: ((0, 2, 1), (3, 4, 4)),
}


TWO = {"x": True, "a2": False}
ORDER = (
    "prep",
    "st0",
    "xh1",
    "gown",
    "gstart",
    "xsend",
    "xh2",
    "T2",
    "T2b",
    "z g 1",
    "xown",
    "act",
    "T2c",
    "C1",
    "z g 2",
    "C1b",
    "C1c",
    "rs0",
    "S2",
    "a2start",
    "z g 3",
    "padg 0",
    "z a2 1",
    "padg 1",
    "gh2",
    "S3",
    "padg 2",
    "a2own",
    "padg 3",
    "y a2 0",
    "xbulk",
    "T1",
    "y a2 1",
    "o a2 0 1",
    "T1b",
    "o a2 1 0",
    "z a2 2",
    "prepa 0",
    "wx 0 0 0",
    "wx 0 0 1",
    "wx 0 0 2",
    "wx 0 0 3",
    "wx 0 0 4",
    "z x 1",
    "T1c",
    "wx 0 1 0",
    "z a2 3",
    "wx 0 1 1",
    "wx 0 1 2",
    "wx 0 1 3",
    "wx 0 1 4",
    "wx 0 2 0",
    "wx 0 2 1",
    "wx 0 2 2",
    "o a2 1 1",
    "y a2 2",
    "wx 0 2 3",
    "wx 0 2 4",
    "mstart",
    "o a2 2 0",
    "prepa 1",
    "wx 1 0 0",
    "wx 1 0 1",
    "wx 1 0 2",
    "wx 1 0 3",
    "rt",
    "wx 1 0 4",
    "wx 1 1 0",
    "wx 1 1 1",
    "wx 1 1 2",
    "wx 1 1 3",
    "z x 2",
    "y a2 3",
    "wx 1 1 4",
    "wx 1 2 0",
    "wx 1 2 1",
    "o a2 2 1",
    "y x 0",
    "wx 1 2 2",
    "wx 1 2 3",
    "wx 1 2 4",
    "y x 1",
    "prepa 2",
    "wx 2 0 0",
    "C2",
    "wx 2 0 1",
    "z m 1",
    "wx 2 0 2",
    "o a2 3 0",
    "wx 2 0 3",
    "wx 2 0 4",
    "wx 2 1 0",
    "wx 2 1 1",
    "padm 0",
    "wx 2 1 2",
    "wx 2 1 3",
    "wx 2 1 4",
    "z x 3",
    "wx 2 2 0",
    "wx 2 2 1",
    "wx 2 2 2",
    "wx 2 2 3",
    "wx 2 2 4",
    "y x 2",
    "o a2 3 1",
    "z m 2",
    "C2b",
    "gh1",
    "o x 1 1",
    "C2c",
    "prepa 3",
    "wx 3 0 0",
    "wx 3 0 1",
    "y x 3",
    "o x 0 1",
    "z m 3",
    "wx 3 0 2",
    "S4",
    "wx 3 0 3",
    "wx 3 0 4",
    "wx 3 1 0",
    "wx 3 1 1",
    "wx 3 1 2",
    "wx 3 1 3",
    "o x 2 1",
    "padm 1",
    "wx 3 1 4",
    "wx 3 2 0",
    "wx 3 2 1",
    "padm 2",
    "prepx 0",
    "prepx 1",
    "prepx 2",
    "o x 3 1",
    "wx 3 2 2",
    "wx 3 2 3",
    "out",
    "wx 3 2 4",
    "S5",
    "padm 3",
    "prepx 3",
    "fin",
)
REAPS = (47, 71, 94, 118, 136)


def sigmoid_of(values):
    return 0.5 * jnp.tanh(0.5 * values) + 0.5


def group_sum(tile):
    lanes = lax.broadcasted_iota(jnp.int32, tile.shape, 1)
    for step in (1, 2, 4, 8):
        up = pltpu.roll(tile, step, 1)
        down = pltpu.roll(tile, SLICE - step, 1)
        tile = tile + jnp.where((lanes & step) != 0, up, down)
    return tile


def column_ids(rows, width):
    return lax.broadcasted_iota(jnp.int32, (rows, SLICE), 0) % width


def shifted(values, width, k):
    if k == 1:
        return values
    rows = values.shape[0]
    cols = column_ids(rows, width)
    if k == 0:
        return jnp.where(cols == width - 1, 0.0, pltpu.roll(values, rows - 1, 0))
    return jnp.where(cols == 0, 0.0, pltpu.roll(values, 1, 0))


def three_shifts(values, width):
    wide = values.astype(F32)
    return jnp.concatenate([shifted(wide, width, k).astype(BF16) for k in range(3)], axis=1)


def taken(ref, spans, start_one, start_two):
    (a, b, _), (c, d, _) = spans
    one = ref[a:b, start_one : start_one + BAND, :]
    two = ref[c:d, start_two : start_two + BAND, :]
    lanes = ref.shape[2]
    return jnp.concatenate(
        [one.reshape((b - a) * BAND, lanes), two.reshape((d - c) * BAND, lanes)], axis=0
    )


def spread(out, spans, result, fresh):
    (a, b, o), (c, d, p) = spans
    cut = (b - a) * BAND
    one = result[:cut].reshape(b - a, BAND, -1)
    two = result[cut:].reshape(d - c, BAND, -1)
    if fresh:
        out[o : o + b - a] = one
        out[p : p + d - c] = two
    else:
        out[o : o + b - a] += one
        out[p : p + d - c] += two


PARTS = (1, 0, 2)


def conv_forward(act, weights, sums, part):
    i = PARTS[part]
    spans = FORWARD[i]
    rows = jnp.concatenate([taken(act, spans, 32 * j, 16 + 16 * j) for j in range(3)], axis=1)
    taps = weights[3 * i : 3 * i + 3].reshape(3 * CHANNELS, 3 * SLICE)
    spread(sums, spans, jnp.dot(rows, taps, preferred_element_type=F32), part == 0)


def conv_columns(sums, frame, width):
    total = sums[frame, :, SLICE : 2 * SLICE]
    total = total + shifted(sums[frame, :, 0:SLICE], width, 2)
    return total + shifted(sums[frame, :, 2 * SLICE : 3 * SLICE], width, 0)


def conv_backward(grads, weights, sums, part):
    i = PARTS[part]
    spans = BACKWARD[i]
    rows = jnp.concatenate(
        [taken(grads, spans, 64 - 32 * j, 48 - 16 * j) for j in range(3)], axis=1
    )
    taps = jnp.concatenate([weights[3 * i + j] for j in range(3)], axis=1)
    result = lax.dot_general(rows, taps, (((1,), (1,)), ((), ())), preferred_element_type=F32)
    spread(sums, spans, result, part == 0)


def moments(values):
    total = jnp.sum(values, axis=0, keepdims=True)
    off = values - total / values.shape[0]
    return total, jnp.sum(off * off, axis=0, keepdims=True)


def merge(totals, squares, count):
    total = functools.reduce(jnp.add, totals)
    mean = total / (count * len(totals))
    square = functools.reduce(jnp.add, squares)
    for part in totals:
        off = part / count - mean
        square = square + count * off * off
    return total, square


def group_merge(total, square, count):
    mean = total / count
    group_total = group_sum(total)
    off = mean - group_total / (16 * count)
    return group_total, group_sum(square + count * off * off)


def long_row(tile, row):
    return jnp.concatenate([tile[row + k : row + k + 1, :] for k in range(NARROW)], axis=1)


def lanes_of(m):
    if isinstance(m, int):
        return pl.ds(m * SLICE, SLICE)
    return pl.ds(pl.multiple_of(m * SLICE, SLICE), SLICE)


def place_of(k):
    return k % 2 * 2 + k // 2


def store_taps(out, taps, result, fresh):
    for number, tap in enumerate(taps):
        for k in range(NARROW):
            start = place_of(k) * SLICE
            piece = result[start : start + SLICE, number * SLICE : (number + 1) * SLICE]
            rows = slice(k * SLICE, (k + 1) * SLICE)
            if fresh:
                out[tap, rows, :] = piece
            else:
                out[tap, rows, :] += piece


def rows_of(m, offset=0):
    return pl.ds(pl.multiple_of(offset + m * OWN, OWN), OWN)


def clear_pads(three_one, three_two):
    for start in (0, three_one.shape[1] - 32):
        three_one[:, start : start + 32, :] = jnp.zeros((FIRST, 32, 3 * SLICE), BF16)
    for start in (0, three_two.shape[2] - 16):
        three_two[:, :, start : start + 16, :] = jnp.zeros((FRAMES - FIRST, 4, 16, 3 * SLICE), BF16)


def pad_pair(grad_ref, three_one, three_two, pair):
    @pl.loop(0, 2)
    def _(half):
        first = pl.multiple_of(half * BAND, BAND)

        @pl.loop(0, FIRST)
        def _(f):
            start = pl.multiple_of(32 + pair * 2 * BAND + first, 32)
            three_one[f, pl.ds(start, BAND), :] = three_shifts(grad_ref[2 * pair + half, f], 32)

        @pl.loop(0, FRAMES - FIRST)
        def _(f):
            start = pl.multiple_of(16 + first, 16)
            three_two[f, pair, pl.ds(start, BAND), :] = three_shifts(grad_ref[2 * pair + half, FIRST + f], 16)


PAIRS = {
    0: ((0, 1), (1, 2), (3, 4)),
    1: ((0, 0), (1, 1), (2, 2), (3, 3), (4, 4)),
    2: ((1, 0), (2, 1), (4, 3)),
}
TAP_GROUPS = ((0, 1), (2, 3), (4, 5), (6, 7), (8,))


def tap_rows(three_one, three_two, t, tap):
    j, k = tap // 3, tap % 3
    cut = slice(k * SLICE, (k + 1) * SLICE)
    if t < FIRST:
        return three_one[t, (2 - j) * 32 : (2 - j) * 32 + 1024, cut]
    return three_two[t - FIRST, :, (2 - j) * 16 : (2 - j) * 16 + 256, cut].reshape(1024, SLICE)


def weight_terms(act_t, three_one, three_two, i, pairs, group, out, fresh):
    left = jnp.concatenate([act_t[c, s] for s, _ in pairs for c in range(BANDS)], axis=1)
    right = jnp.concatenate(
        [
            jnp.concatenate([tap_rows(three_one, three_two, t, tap) for tap in group], axis=1)
            for _, t in pairs
        ],
        axis=0,
    )
    result = jnp.dot(left, right, preferred_element_type=F32)
    store_taps(out, [9 * i + tap for tap in group], result, fresh)


def pair_weight_terms(act_t, three_one, three_two, pair, i, group, out, fresh):
    def rows(t, tap):
        j, cut = tap // 3, slice(tap % 3 * SLICE, (tap % 3 + 1) * SLICE)
        if t < FIRST:
            start = pl.multiple_of((2 - j) * 32 + pair * 2 * BAND, 32)
            return three_one[t, pl.ds(start, 2 * BAND), cut]
        return three_two[t - FIRST, pair, (2 - j) * 16 : (2 - j) * 16 + 2 * BAND, cut]

    left = jnp.concatenate([act_t[2 * pair + half, s] for s, _ in PAIRS[i] for half in range(2)], axis=1)
    right = jnp.concatenate(
        [jnp.concatenate([rows(t, tap) for tap in group], axis=1) for _, t in PAIRS[i]], axis=0
    )
    result = jnp.dot(left, right, preferred_element_type=F32)
    store_taps(out, [9 * i + tap for tap in group], result, fresh)


def block_kernel(
    x_one, x_two, g_one, g_two, gain_one, shift_one, bias_one, gain_two, shift_two, bias_two,
    entry_hbm, exit_hbm,
    out_one, out_two, back_one, back_two, smalls, act_out, wide_one_out, wide_two_out, exit_grad,
    act_t1, act_t2, g_all, gm_all, three_one, three_two, wide_one, wide_two, exit_sum,
    entry_w, exit_w, own_x, own_g, band_x, band_a, long_g, long_m, params,
    stat_a, stat_b, stat_c, stat_d, stat_e, stat_f, few,
    sums, partial, grad_three, mid, grad_two, grad_one, part_send, part_recv, tail_send, tail_recv, out_send,
    w_sem, send_sem, x_sem, g_sem, p_sem, halo_sem, stat_sem, ga_sem, gm_sem, a1_sem, a2_sem, rs_sem, o_sem, store_sem,
):
    w = lax.axis_index("wide")
    n = lax.axis_index("narrow")
    base = w // BANDS * BANDS
    b = w - base
    z, y = b // 2, b % 2
    has_up, has_down = b > 0, b < BANDS - 1
    pair_up, pair_down = y == 1, y == 0
    flags = lambda f: (has_up, has_down) if f < FIRST else (pair_up, pair_down)
    width_of = lambda f: 32 if f < FIRST else 16
    sub_of = lambda f: 0 if f < FIRST else 1

    sends = []
    used = [0]

    def both(first, second):
        if first is None or second is None:
            return second if first is None else first
        return jnp.logical_and(first, second)

    def under(flag, act):
        if flag is None:
            act()
        else:
            pl.when(flag)(act)

    def make(src, dst, recv, device):
        used[0] += 1
        return pltpu.make_async_remote_copy(
            src_ref=src,
            dst_ref=dst,
            send_sem=send_sem.at[used[0] - 1],
            recv_sem=recv,
            device_id=device,
            device_id_type=MESH,
        )

    def start(copies):
        for copy in copies:
            copy.start()

    def launch(copies, flag=None):
        under(flag, lambda: start(copies))
        sends.append((flag, copies))

    def send(src, dst, recv, device, flag=None):
        launch([make(src, dst, recv, device)], flag)

    def reap(count):
        for flag, copies in sends[:count]:

            def wait_all(copies=copies):
                for copy in copies:
                    copy.wait_send()

            under(flag, wait_all)
        del sends[:count]

    def arrived(dst, recv, flag=None):
        wait = pltpu.make_async_remote_copy(
            src_ref=dst,
            dst_ref=dst,
            send_sem=send_sem.at[0],
            recv_sem=recv,
            device_id=(w, n),
            device_id_type=MESH,
        ).wait_recv
        under(flag, wait)

    def beside(m):
        return (w, m)

    def band_of(c):
        return (base + c, n)

    others = [lax.rem(n + d, NARROW) for d in (1, 2, 3)]
    far = [lax.rem(b + d, BANDS) for d in range(1, BANDS)]
    sib, opp, cross = n ^ 1, n ^ 2, n ^ 3
    beyond = b + 1 - 2 * y
    slant = b - 1 + 2 * y
    above = lax.rem(b + BANDS - 1, BANDS)
    below = lax.rem(b + 1, BANDS)
    up_chip = lax.rem(b + BANDS - 2, BANDS)
    down_chip = lax.rem(b + 2, BANDS)
    pairs_by_distance = [z, z + 1 - 2 * (z % 2), 2 - z // 2, 3 - 3 * (z // 2)]
    mine, mine_long = rows_of(n), rows_of(n, 32)

    sem_of = {"x": a1_sem, "a2": a2_sem, "g": ga_sem, "m": gm_sem}
    array_of = {"x": act_t1, "a2": act_t2, "g": g_all, "m": gm_all}

    def block(name, c, k):
        if name in ("g", "m"):
            return array_of[name].at[c]
        return array_of[name].at[c, :, lanes_of(place_of(k)), :]

    def couple(name, c, k):
        rows = pl.ds(pl.multiple_of(k % 2 * 2 * SLICE, 2 * SLICE), 2 * SLICE)
        return array_of[name].at[c, :, rows, :]

    def sem(name, c, kind):
        return sem_of[name].at[c] if name in ("g", "m") else sem_of[name].at[c, kind]

    def own(name, c):
        return couple(name, c, n) if TWO.get(name) else block(name, c, n)

    def to(ref, name, c, kind, device):
        return make(ref, ref, sem(name, c, kind), device)

    def to_opp(name, c):
        return to(block(name, c, n), name, c, 1, beside(opp))

    def to_sib(name, c):
        return to(couple(name, c, n), name, c, 2, beside(sib))

    def to_beyond(name, c):
        return to(block(name, c, n), name, c, 0, band_of(beyond))

    def at_distance(step, line):
        for sign in (-1, 1) if step else (1,):
            there = None if step == 0 else (z >= step if sign < 0 else z + step <= 3)
            c = lax.rem(b + 2 * sign * step + BANDS, BANDS)
            yield sign, there, c if line == 0 else c + 1 - 2 * y

    def z_step(name, step):
        for sign, there, c in at_distance(step, 0):
            arrived(own(name, c), sem(name, c, 0), there)
            copies = [to_beyond(name, c)]
            if name in ("x", "a2"):
                copies.append(to_sib(name, c) if TWO[name] else to_opp(name, c))
            if step < 3:
                onward, target = (z < 3, down_chip) if sign < 0 else (z > 0, up_chip)
                launch([to(own(name, c), name, c, 0, band_of(target))], both(there, onward))
            launch(copies, there)

    def y_step(name, step):
        for _, there, c in at_distance(step, 1):
            arrived(block(name, c, n), sem(name, c, 0), there)
            launch([to_opp(name, c)], there)

    def o_step(name, step, line):
        for _, there, c in at_distance(step, line):
            arrived(block(name, c, opp), sem(name, c, 1), there)
            launch([to_sib(name, c)], there)

    def begin(name):
        launch([to(own(name, b), name, b, 0, band_of(down_chip))], z < 3)
        launch([to(own(name, b), name, b, 0, band_of(up_chip))], z > 0)
        launch([to_beyond(name, b)])

    def await_sib(name, c):
        arrived(couple(name, c, sib), sem(name, c, 2))

    def to_bands(stat, number):
        for c in far:
            send(stat.at[b], stat.at[b], stat_sem.at[number, b], band_of(c))

    def from_bands(stat, number):
        for c in far:
            arrived(stat.at[b], stat_sem.at[number, c])

    def to_narrow(stat, number):
        for m in others:
            send(stat.at[n], stat.at[n], stat_sem.at[number, n], beside(m))

    def from_narrow(stat, number):
        for m in others:
            arrived(stat.at[n], stat_sem.at[number, m])

    def exchange_rims(ref, first_sem):
        send(ref.at[0:3, 128:160, :], ref.at[0:3, 0:32, :], halo_sem.at[first_sem], band_of(below), has_down)
        send(ref.at[0:3, 32:64, :], ref.at[0:3, 160:192, :], halo_sem.at[first_sem + 1], band_of(above), has_up)
        send(ref.at[3:5, 144:160, :], ref.at[3:5, 16:32, :], halo_sem.at[first_sem + 2], band_of(beyond), pair_down)
        send(ref.at[3:5, 32:48, :], ref.at[3:5, 160:176, :], halo_sem.at[first_sem + 3], band_of(beyond), pair_up)

    def await_rims(ref, first_sem):
        arrived(ref.at[0:3, 0:32, :], halo_sem.at[first_sem], has_up)
        arrived(ref.at[0:3, 160:192, :], halo_sem.at[first_sem + 1], has_down)
        arrived(ref.at[3:5, 16:32, :], halo_sem.at[first_sem + 2], pair_up)
        arrived(ref.at[3:5, 160:176, :], halo_sem.at[first_sem + 3], pair_down)

    kept = {}
    count_one = 3 * BAND * BANDS
    count_two = 2 * BAND * 2

    def prep():
        loads = []
        for number, (source, target) in enumerate(((exit_hbm, exit_w), (entry_hbm, entry_w))):
            for k in range(3):
                load = pltpu.make_async_copy(
                    source.at[:, k],
                    target.at[:, :, k * SLICE : (k + 1) * SLICE],
                    w_sem.at[number, k],
                )
                load.start()
                loads.append(load)
        kept["loads"] = loads
        own_x[0:FIRST] = x_one[...]
        own_x[FIRST:FRAMES] = x_two[...]
        own_g[0:FIRST] = g_one[...]
        own_g[FIRST:FRAMES] = g_two[...]
        for ref in (params, stat_c, stat_d, stat_f, smalls):
            ref[...] = jnp.zeros_like(ref)
        for ref in (band_x, long_g, long_m):
            for start in (0, 160):
                ref[:, start : start + 32, :] = jnp.zeros((FRAMES, 32, ref.shape[2]), BF16)
        for row, ref in enumerate((gain_one, shift_one, bias_one, gain_two, shift_two, bias_two)):
            params[n, row : row + 1, :] = ref[...].astype(F32)
        band_x[:, mine_long, :] = own_x[...]
        long_g[:, mine_long, :] = own_g[:, :, lanes_of(n)]

        barrier = pltpu.get_barrier_semaphore()
        for m in others:
            pl.semaphore_signal(barrier, inc=1, device_id=beside(m), device_id_type=MESH)
        for c in far:
            pl.semaphore_signal(barrier, inc=1, device_id=band_of(c), device_id_type=MESH)
        for sub, (start, stop) in enumerate(((0, FIRST), (FIRST, FRAMES))):
            values = own_x[start:stop].astype(F32).reshape((stop - start) * OWN, CHANNELS)
            total, square = moments(values)
            cuts = [slice(k * SLICE, (k + 1) * SLICE) for k in range(NARROW)]
            t, s = group_merge(
                jnp.concatenate([total[:, cut] for cut in cuts], axis=0),
                jnp.concatenate([square[:, cut] for cut in cuts], axis=0),
                float(values.shape[0]),
            )
            stat_a[n, 8 * sub : 8 * sub + 4, :] = t
            stat_a[n, 8 * sub + 4 : 8 * sub + 8, :] = s
        pl.semaphore_wait(barrier, NARROW - 1 + BANDS - 1)
        to_narrow(stat_a, 0)
        rims_out()
        for m in others:
            send(own_g.at[:, :, lanes_of(m)], long_g.at[:, mine_long, :], g_sem.at[n], beside(m))
            send(params.at[n], params.at[n], p_sem.at[n], beside(m))
        clear_pads(wide_one, wide_two)
        clear_pads(three_one, three_two)

    def xsend():
        for m in (opp, sib):
            send(own_x, band_x.at[:, mine_long, :], x_sem.at[n], beside(m))

    def st0():
        from_narrow(stat_a, 0)
        for sub, count in ((0, 3 * OWN * 16.0), (1, 2 * OWN * 16.0)):
            t, s = merge(
                [stat_a[m, 8 * sub : 8 * sub + 4, :] for m in range(NARROW)],
                [stat_a[m, 8 * sub + 4 : 8 * sub + 8, :] for m in range(NARROW)],
                count,
            )
            stat_b[b, 8 * sub : 8 * sub + 4, :] = t
            stat_b[b, 8 * sub + 4 : 8 * sub + 8, :] = s
        to_bands(stat_b, 1)

    def gown():
        for m in others:
            arrived(long_g.at[:, mine_long, :], g_sem.at[m])
        exchange_rims(long_g, 4)
        g_all[b] = long_g[:, 32:160, :]

    def rim_parts():
        return (
            (band_x.at[0:3, 0:32, :], 0, own_x.at[0:3], below, has_down, has_up, 3),
            (band_x.at[3:5, 16:32, :], 2, own_x.at[3:5, 16:32, :], beyond, pair_down, pair_up, 3),
            (band_x.at[0:3, 160:192, :], 1, own_x.at[0:3], above, has_up, has_down, 0),
            (band_x.at[3:5, 160:176, :], 3, own_x.at[3:5, 0:16, :], beyond, pair_up, pair_down, 0),
        )

    def rims_out():
        for ref, number, own, target, gives, _, owner in rim_parts():
            send(own, ref, halo_sem.at[number], band_of(target), both(gives, n == owner))

    def xh1():
        for ref, number, _, _, _, takes, owner in rim_parts():
            flag = both(takes, n == owner)
            arrived(ref, halo_sem.at[number], flag)
            send(ref, ref, halo_sem.at[number], beside(opp), flag)
            send(ref, ref, halo_sem.at[number], beside(sib), flag)

    def xh2():
        for ref, number, _, _, _, takes, owner in rim_parts():
            flag = both(takes, n == (owner + 2) % 4)
            arrived(ref, halo_sem.at[number], flag)
            send(ref, ref, halo_sem.at[number], beside(sib), flag)

    def xh3():
        for ref, number, _, _, _, takes, owner in rim_parts():
            arrived(ref, halo_sem.at[number], both(takes, n % 2 != owner % 2))

    def xown():
        arrived(band_x.at[:, mine_long, :], x_sem.at[opp])
        theirs = band_x.at[:, rows_of(opp, 32), :]
        send(theirs, theirs, x_sem.at[opp], beside(sib))
        arrived(band_x.at[:, mine_long, :], x_sem.at[sib])
        arrived(band_x.at[:, mine_long, :], x_sem.at[cross])

    def first_hidden(values, sub):
        normed = (values - kept["mean_one"][sub]) * kept["inv_one"][sub]
        return normed, normed * kept["gain_long"] + kept["shift_long"]

    def first_active(f, start, stop):
        _, hidden = first_hidden(band_x[f, start:stop].astype(F32), sub_of(f))
        return (hidden * sigmoid_of(hidden)).astype(BF16)

    def act():
        for m in others:
            arrived(params.at[n], p_sem.at[m])
        from_bands(stat_b, 1)
        one_total, one_square = merge(
            [stat_b[c, 0:4, :] for c in range(BANDS)],
            [stat_b[c, 4:8, :] for c in range(BANDS)],
            3 * BAND * 16.0,
        )
        two_total, two_square = merge(
            [stat_b[b, 8:12, :], stat_b[beyond, 8:12, :]],
            [stat_b[b, 12:16, :], stat_b[beyond, 12:16, :]],
            2 * BAND * 16.0,
        )
        kept["mean_one"] = [
            long_row(one_total / (16.0 * count_one), 0),
            long_row(two_total / (16.0 * count_two), 0),
        ]
        kept["inv_one"] = [
            long_row(lax.rsqrt(one_square / (16.0 * count_one) + EPS), 0),
            long_row(lax.rsqrt(two_square / (16.0 * count_two) + EPS), 0),
        ]
        kept["gain_long"] = jnp.concatenate([params[m, 0:1, :] for m in range(NARROW)], axis=1)
        kept["shift_long"] = jnp.concatenate([params[m, 1:2, :] for m in range(NARROW)], axis=1)
        for f in range(FRAMES):
            active = first_active(f, 32, 160)
            band_a[f, 32:160, :] = active
            for k in range(NARROW):
                cut = slice(k * SLICE, (k + 1) * SLICE)
                act_t1[b, f, lanes_of(place_of(k)), :] = active[:, cut].T

    def lay_out(long):
        for start, stop in ((0, FIRST), (FIRST, FRAMES)):

            @pl.loop(start, stop)
            def _(f, start=start):
                grad_three[f] = three_shifts(long[f], width_of(start))

    def t2():
        await_rims(long_g, 4)
        lay_out(long_g)
        for load in kept["loads"][:3]:
            load.wait()
        conv_backward(grad_three, exit_w, partial, 0)

    def t2c():
        conv_backward(grad_three, exit_w, partial, 2)
        part_send[0] = partial[:, :, lanes_of(sib)].astype(BF16)
        part_send[1] = partial[:, :, lanes_of(cross)].astype(BF16)
        for k in range(2):
            send(part_send.at[k], part_recv.at[k], rs_sem.at[0, k], beside(sib))

    def rs0():
        for k in range(2):
            arrived(part_recv.at[k], rs_sem.at[0, k])
        part_send[2] = (partial[:, :, lanes_of(opp)] + part_recv[1].astype(F32)).astype(BF16)
        send(part_send.at[2], part_recv.at[2], rs_sem.at[0, 2], beside(opp))

    def c1():
        xh3()
        for f in range(FRAMES):
            width = width_of(f)
            up, down = flags(f)
            row = first_active(f, 32 - width, 32)
            band_a[f, 32 - width : 32, :] = jnp.where(up, row, jnp.zeros_like(row))
            row = first_active(f, 160, 160 + width)
            band_a[f, 160 : 160 + width, :] = jnp.where(down, row, jnp.zeros_like(row))
        for load in kept["loads"][3:]:
            load.wait()
        conv_forward(band_a, entry_w, sums, 0)

    def c1c():
        conv_forward(band_a, entry_w, sums, 2)
        for f in range(FRAMES):
            mid[f] = conv_columns(sums, f, width_of(f)) + params[n, 2:3, :]
        for sub, (start, stop) in enumerate(((0, FIRST), (FIRST, FRAMES))):
            values = mid[start:stop].reshape((stop - start) * BAND, SLICE)
            total, square = moments(values)
            t, s = group_merge(total, square, float(values.shape[0]))
            stat_c[b, 2 * sub : 2 * sub + 1, :] = t
            stat_c[b, 2 * sub + 1 : 2 * sub + 2, :] = s
        to_bands(stat_c, 2)

    def s2():
        from_bands(stat_c, 2)
        one_total, one_square = merge(
            [stat_c[c, 0:1, :] for c in range(BANDS)],
            [stat_c[c, 1:2, :] for c in range(BANDS)],
            3 * BAND * 16.0,
        )
        two_total, two_square = merge(
            [stat_c[b, 2:3, :], stat_c[beyond, 2:3, :]],
            [stat_c[b, 3:4, :], stat_c[beyond, 3:4, :]],
            2 * BAND * 16.0,
        )
        mean_two = [one_total / (16.0 * count_one), two_total / (16.0 * count_two)]
        kept["inv_two"] = [
            lax.rsqrt(one_square / (16.0 * count_one) + EPS),
            lax.rsqrt(two_square / (16.0 * count_two) + EPS),
        ]
        kept["gain_own"], kept["shift_own"] = params[n, 3:4, :], params[n, 4:5, :]
        for f in range(FRAMES):
            normed = (mid[f] - mean_two[sub_of(f)]) * kept["inv_two"][sub_of(f)]
            mid[f] = normed
            hidden = normed * kept["gain_own"] + kept["shift_own"]
            act_t2[b, f, lanes_of(place_of(n)), :] = (hidden * sigmoid_of(hidden)).astype(BF16).T

    def gh2():
        arrived(part_recv.at[2], rs_sem.at[0, 2])
        rows_sum = [[0.0, 0.0], [0.0, 0.0]]
        for f in range(FRAMES):
            sub = sub_of(f)
            grad = partial[f, :, lanes_of(n)] + part_recv[0, f].astype(F32) + part_recv[2, f].astype(F32)
            hidden = mid[f] * kept["gain_own"] + kept["shift_own"]
            sigmoid = sigmoid_of(hidden)
            grad = grad * (sigmoid * (1.0 + hidden * (1.0 - sigmoid)))
            grad_two[f] = grad
            rows_sum[sub][0] += jnp.sum(grad, axis=0, keepdims=True)
            rows_sum[sub][1] += jnp.sum(grad * mid[f], axis=0, keepdims=True)
        for sub in range(2):
            stat_d[b, 2 * sub : 2 * sub + 1, :] = rows_sum[sub][0]
            stat_d[b, 2 * sub + 1 : 2 * sub + 2, :] = rows_sum[sub][1]
        own = g_all[b].astype(F32).reshape(FRAMES * BAND, SLICE)
        stat_d[b, 4:5, :] = jnp.sum(own, axis=0, keepdims=True)
        to_bands(stat_d, 3)

    def a2start():
        begin("a2")
        launch([to_opp("a2", b)])

    def a2own():
        o_step("a2", 0, 0)

    def s3():
        from_bands(stat_d, 3)
        gain_own = kept["gain_own"]
        all_rows = [
            functools.reduce(jnp.add, [stat_d[c, r : r + 1, :] for c in range(BANDS)]) for r in range(5)
        ]
        smalls[3:4, :] = all_rows[1] + all_rows[3]
        smalls[4:5, :] = all_rows[0] + all_rows[2]
        smalls[5:6, :] = all_rows[4]
        pair_rows = [stat_d[b, r : r + 1, :] + stat_d[beyond, r : r + 1, :] for r in range(4)]
        p_two = [
            group_sum(gain_own * all_rows[0]) / (16.0 * count_one),
            group_sum(gain_own * pair_rows[2]) / (16.0 * count_two),
        ]
        q_two = [
            group_sum(gain_own * all_rows[1]) / (16.0 * count_one),
            group_sum(gain_own * pair_rows[3]) / (16.0 * count_two),
        ]
        bias_sum = 0.0
        for f in range(FRAMES):
            sub = sub_of(f)
            grad = (grad_two[f] * gain_own - p_two[sub] - mid[f] * q_two[sub]) * kept["inv_two"][sub]
            grad = grad.astype(BF16)
            gm_all[b, f] = grad
            long_m[f, 32:160, :] = grad
            bias_sum = bias_sum + jnp.sum(grad.astype(F32), axis=0, keepdims=True)
        stat_f[b, 16:17, :] = bias_sum
        exchange_rims(long_m, 8)

    def t1():
        await_rims(long_m, 8)
        lay_out(long_m)
        conv_backward(grad_three, entry_w, partial, 0)

    def t1c():
        conv_backward(grad_three, entry_w, partial, 2)
        tail_send[0] = partial[:, rows_of(sib), :].astype(BF16)
        tail_send[1] = partial[:, rows_of(cross), :].astype(BF16)
        for k in range(2):
            send(tail_send.at[k], tail_recv.at[k], rs_sem.at[1, k], beside(sib))

    def rt():
        for k in range(2):
            arrived(tail_recv.at[k], rs_sem.at[1, k])
        tail_send[2] = (partial[:, rows_of(opp), :] + tail_recv[1].astype(F32)).astype(BF16)
        send(tail_send.at[2], tail_recv.at[2], rs_sem.at[1, 2], beside(opp))

    def gh1():
        arrived(tail_recv.at[2], rs_sem.at[1, 2])
        for sub, (start, stop) in enumerate(((0, FIRST), (FIRST, FRAMES))):
            first_sum, second_sum = 0.0, 0.0
            for f in range(start, stop):
                grad = partial[f, mine, :] + tail_recv[0, f].astype(F32) + tail_recv[2, f].astype(F32)
                normed, hidden = first_hidden(own_x[f].astype(F32), sub)
                sigmoid = sigmoid_of(hidden)
                grad = grad * (sigmoid * (1.0 + hidden * (1.0 - sigmoid)))
                grad_one[f] = grad
                first_sum = first_sum + jnp.sum(grad, axis=0, keepdims=True)
                second_sum = second_sum + jnp.sum(grad * normed, axis=0, keepdims=True)
            for k in range(NARROW):
                cut = slice(k * SLICE, (k + 1) * SLICE)
                stat_e[n, 8 * sub + k : 8 * sub + k + 1, :] = first_sum[:, cut]
                stat_e[n, 8 * sub + 4 + k : 8 * sub + 5 + k, :] = second_sum[:, cut]
        to_narrow(stat_e, 4)

    def s4():
        from_narrow(stat_e, 4)
        stat_f[b, 0:16, :] = stat_e[0] + stat_e[1] + stat_e[2] + stat_e[3]
        to_bands(stat_f, 5)

    def s5():
        from_bands(stat_f, 5)
        all_sums = functools.reduce(jnp.add, [stat_f[c] for c in range(BANDS)])
        pair_sums = stat_f[b] + stat_f[beyond]
        few[0, 0:4, :] = all_sums[0:4] + all_sums[8:12]
        few[1, 0:4, :] = all_sums[4:8] + all_sums[12:16]
        smalls[0:1, :] = few[1, pl.ds(n, 1), :]
        smalls[1:2, :] = few[0, pl.ds(n, 1), :]
        smalls[2:3, :] = all_sums[16:17]
        gain_rows = jnp.concatenate([params[m, 0:1, :] for m in range(NARROW)], axis=0)
        p_one = [
            long_row(group_sum(gain_rows * all_sums[0:4]) / (16.0 * count_one), 0),
            long_row(group_sum(gain_rows * pair_sums[8:12]) / (16.0 * count_two), 0),
        ]
        q_one = [
            long_row(group_sum(gain_rows * all_sums[4:8]) / (16.0 * count_one), 0),
            long_row(group_sum(gain_rows * pair_sums[12:16]) / (16.0 * count_two), 0),
        ]
        for f in range(FRAMES):
            sub = sub_of(f)
            normed, _ = first_hidden(own_x[f].astype(F32), sub)
            grad = grad_one[f] * kept["gain_long"] - p_one[sub] - normed * q_one[sub]
            grad = (own_g[f].astype(F32) + grad * kept["inv_one"][sub]).astype(BF16)
            if sub == 0:
                back_one[f] = grad
            else:
                back_two[f - FIRST] = grad

    stores = []

    def store(source, target, number):
        copy = pltpu.make_async_copy(source, target, store_sem.at[number])
        copy.start()
        stores.append(copy)

    def prepa(number):
        first = 2 * pairs_by_distance[number]
        await_sib("a2", first)
        await_sib("a2", first + 1)

    def pad(name, number, array, one, two):
        pair = pairs_by_distance[number]
        c = 2 * pair + 1 - y
        arrived(block(name, c, n), sem(name, c, 0))
        pad_pair(array, one, two, pair)

    def padg(number):
        pad("g", number, g_all, wide_one, wide_two)

    def c2():
        @pl.loop(0, NARROW)
        def _(k):
            cut = lanes_of(k)
            rows = lanes_of(place_of(k))
            for f in range(FRAMES):
                width = width_of(f)
                up, down = flags(f)
                band_a[f, 32:160, cut] = act_t2[b, f, rows, :].T
                row = act_t2[b - (b + 7) // 8, f, rows, :].T[BAND - width : BAND]
                band_a[f, 32 - width : 32, cut] = jnp.where(up, row, jnp.zeros_like(row))
                row = act_t2[b + (14 - b) // 8, f, rows, :].T[0:width]
                band_a[f, 160 : 160 + width, cut] = jnp.where(down, row, jnp.zeros_like(row))

        conv_forward(band_a, exit_w, sums, 0)

    def c2c():
        conv_forward(band_a, exit_w, sums, 2)
        for f in range(FRAMES):
            total = conv_columns(sums, f, width_of(f)) + params[n, 5:6, :]
            total = total + band_x[f, 32:160, lanes_of(n)].astype(F32)
            out_send[f] = total.astype(BF16)
        for m in others:
            send(out_send.at[0:3, rows_of(m), :], out_one.at[:, :, lanes_of(n)], o_sem.at[0, n], beside(m))
            send(out_send.at[3:5, rows_of(m), :], out_two.at[:, :, lanes_of(n)], o_sem.at[1, n], beside(m))
        out_one[:, :, lanes_of(n)] = out_send[0:3, mine, :]
        out_two[:, :, lanes_of(n)] = out_send[3:5, mine, :]

    def out():
        for m in others:
            arrived(out_one.at[:, :, lanes_of(m)], o_sem.at[0, m])
            arrived(out_two.at[:, :, lanes_of(m)], o_sem.at[1, m])

    def wx(number, place, group):
        i = PARTS[place]
        taps = TAP_GROUPS[group]
        pair = pairs_by_distance[number]
        pair_weight_terms(act_t2, wide_one, wide_two, pair, i, taps, exit_sum, number == 0)
        if number == 3 and group == len(TAP_GROUPS) - 1:
            cut = slice(9 * i, 9 * i + 9)
            store(exit_sum.at[cut], exit_grad.at[cut], 6 + i)

    def prepx(number):
        first = 2 * pairs_by_distance[number]
        if number == 0:
            await_sib("x", beyond)
        else:
            await_sib("x", first)
            await_sib("x", first + 1)
        store(act_t1.at[pl.ds(first, 2)], act_out.at[pl.ds(first, 2)], number)

    def padm(number):
        pad("m", number, gm_all, three_one, three_two)
        if number == 3:
            store(three_one, wide_one_out, 4)
            store(three_two, wide_two_out, 5)

    def fin():
        reap(len(sends))
        for copy in stores:
            copy.wait()

    backward = lambda weights, part: lambda: conv_backward(grad_three, weights, partial, part)
    forward = lambda weights, part: lambda: conv_forward(band_a, weights, sums, part)
    steps = {
        "prep": prep, "xsend": xsend, "st0": st0, "gown": gown, "xown": xown, "xh1": xh1, "xh2": xh2, "act": act,
        "T2": t2, "T2b": backward(exit_w, 1), "T2c": t2c, "rs0": rs0,
        "C1": c1, "C1b": forward(entry_w, 1), "C1c": c1c,
        "S2": s2, "gh2": gh2, "a2start": a2start, "a2own": a2own, "S3": s3,
        "T1": t1, "T1b": backward(entry_w, 1), "T1c": t1c, "rt": rt, "gh1": gh1, "S4": s4, "S5": s5,
        "C2": c2, "C2b": forward(exit_w, 1), "C2c": c2c, "out": out,
        "padg": padg, "padm": padm, "fin": fin,
        "gstart": lambda: begin("g"),
        "mstart": lambda: begin("m"),
        "xbulk": lambda: begin("x"),
        "z": z_step, "y": y_step, "o": o_step, "wx": wx, "prepx": prepx, "prepa": prepa,
    }
    before = 0
    for number, item in enumerate(ORDER):
        if number in REAPS:
            count, before = before, len(sends) - before
            reap(count)
        word, *rest = item.split()
        steps[word](*[int(r) if r.isdigit() else r for r in rest])


def run_block(args):
    vmem = pl.BlockSpec(memory_space=pltpu.VMEM)
    hbm = pl.BlockSpec(memory_space=pl.ANY)
    dma = pltpu.SemaphoreType.DMA
    shape = jax.ShapeDtypeStruct
    everyone = (BANDS, FRAMES, CHANNELS, BAND)
    wide_one = (FIRST, 34 * 32, 3 * SLICE)
    wide_two = (FRAMES - FIRST, 4, 18 * 16, 3 * SLICE)
    return pl.pallas_call(
        block_kernel,
        out_shape=(
            shape((FIRST, OWN, CHANNELS), BF16),
            shape((FRAMES - FIRST, OWN, CHANNELS), BF16),
            shape((FIRST, OWN, CHANNELS), BF16),
            shape((FRAMES - FIRST, OWN, CHANNELS), BF16),
            shape((8, SLICE), F32),
            shape(everyone, BF16),
            shape(wide_one, BF16),
            shape(wide_two, BF16),
            shape((27, CHANNELS, SLICE), F32),
        ),
        in_specs=[vmem] * 10 + [hbm] * 2,
        out_specs=(vmem,) * 5 + (hbm,) * 4,
        scratch_shapes=[
            pltpu.VMEM(everyone, BF16),
            pltpu.VMEM(everyone, BF16),
            pltpu.VMEM((BANDS, FRAMES, BAND, SLICE), BF16),
            pltpu.VMEM((BANDS, FRAMES, BAND, SLICE), BF16),
            pltpu.VMEM(wide_one, BF16),
            pltpu.VMEM(wide_two, BF16),
            pltpu.VMEM(wide_one, BF16),
            pltpu.VMEM(wide_two, BF16),
            pltpu.VMEM((27, CHANNELS, SLICE), F32),
            pltpu.VMEM((9, CHANNELS, 3 * SLICE), BF16),
            pltpu.VMEM((9, CHANNELS, 3 * SLICE), BF16),
            pltpu.VMEM((FRAMES, OWN, CHANNELS), BF16),
            pltpu.VMEM((FRAMES, OWN, CHANNELS), BF16),
            pltpu.VMEM((FRAMES, LONG, CHANNELS), BF16),
            pltpu.VMEM((FRAMES, LONG, CHANNELS), BF16),
            pltpu.VMEM((FRAMES, LONG, SLICE), BF16),
            pltpu.VMEM((FRAMES, LONG, SLICE), BF16),
            pltpu.VMEM((NARROW, 8, SLICE), F32),
            pltpu.VMEM((NARROW, 16, SLICE), F32),
            pltpu.VMEM((BANDS, 16, SLICE), F32),
            pltpu.VMEM((BANDS, 8, SLICE), F32),
            pltpu.VMEM((BANDS, 8, SLICE), F32),
            pltpu.VMEM((NARROW, 16, SLICE), F32),
            pltpu.VMEM((BANDS, 24, SLICE), F32),
            pltpu.VMEM((2, 8, SLICE), F32),
            pltpu.VMEM((FRAMES, BAND, 3 * SLICE), F32),
            pltpu.VMEM((FRAMES, BAND, CHANNELS), F32),
            pltpu.VMEM((FRAMES, LONG, 3 * SLICE), BF16),
            pltpu.VMEM((FRAMES, BAND, SLICE), F32),
            pltpu.VMEM((FRAMES, BAND, SLICE), F32),
            pltpu.VMEM((FRAMES, OWN, CHANNELS), F32),
            pltpu.VMEM((3, FRAMES, BAND, SLICE), BF16),
            pltpu.VMEM((3, FRAMES, BAND, SLICE), BF16),
            pltpu.VMEM((3, FRAMES, OWN, CHANNELS), BF16),
            pltpu.VMEM((3, FRAMES, OWN, CHANNELS), BF16),
            pltpu.VMEM((FRAMES, BAND, SLICE), BF16),
            dma((2, 3)),
            dma((288,)),
            dma((NARROW,)),
            dma((NARROW,)),
            dma((NARROW,)),
            dma((12,)),
            dma((6, BANDS)),
            dma((BANDS,)),
            dma((BANDS,)),
            dma((BANDS, 3)),
            dma((BANDS, 3)),
            dma((2, 3)),
            dma((2, NARROW)),
            dma((9,)),
        ],
        compiler_params=pltpu.CompilerParams(
            collective_id=0, has_side_effects=True, vmem_limit_bytes=62 * 1024 * 1024
        ),
        cost_estimate=pl.CostEstimate(flops=20 * 10**9, bytes_accessed=3 * 10**7, transcendentals=0),
        name="block",
    )(*args)


def last_kernel(act_hbm, one_hbm, two_hbm, exit_hbm, smalls, *refs):
    rows, (entry_out, exit_out, *vectors), rest = refs[:4], refs[4:12], refs[12:]
    row_outs, (act_t, wide_one, wide_two, entry_sum, exit_sum, load_sem, store_sem) = rest[:4], rest[4:]

    loads = []
    for f in range(FRAMES):
        first = pltpu.make_async_copy(act_hbm.at[:, f], act_t.at[:, f], load_sem.at[f])
        if f < FIRST:
            second = pltpu.make_async_copy(one_hbm.at[f], wide_one.at[f], load_sem.at[FRAMES + f])
        else:
            place = f - FIRST
            second = pltpu.make_async_copy(two_hbm.at[place], wide_two.at[place], load_sem.at[FRAMES + f])
        first.start()
        second.start()
        loads.append((first, second))
    through = pltpu.make_async_copy(exit_hbm, exit_sum, load_sem.at[2 * FRAMES])
    through.start()
    for row, ref in enumerate(vectors):
        ref[...] = smalls[row : row + 1, :]
    for source, target in zip(rows, row_outs):
        target[...] = source[...]

    stores = []

    def store(source, target):
        copy = pltpu.make_async_copy(source, target, store_sem.at[len(stores)])
        copy.start()
        stores.append(copy)

    def terms(i, pairs, fresh, last):
        for group in TAP_GROUPS[:4]:
            weight_terms(act_t, wide_one, wide_two, i, pairs, group, entry_sum, fresh)
            if last:
                taps = slice(9 * i + group[0], 9 * i + group[-1] + 1)
                store(entry_sum.at[taps], entry_out.at[taps])

    for parts, pairs in ((loads[:2], PAIRS[1][:2]), (loads[2:], PAIRS[1][2:])):
        for first, second in parts:
            first.wait()
            second.wait()
        terms(1, pairs, pairs[0][0] == 0, pairs[-1][0] == FRAMES - 1)
    through.wait()
    store(exit_sum, exit_out)
    terms(0, PAIRS[0], True, True)
    seen = set()
    for s in range(FRAMES):
        meets = [(i, t) for i in range(3) for other, t in PAIRS[i] if other == s]
        right = jnp.concatenate([tap_rows(wide_one, wide_two, t, 8) for _, t in meets], axis=1)
        left = jnp.concatenate([act_t[c, s] for c in range(BANDS)], axis=1)
        result = jnp.dot(left, right, preferred_element_type=F32)
        for place, (i, _) in enumerate(meets):
            part = result[:, place * SLICE : (place + 1) * SLICE]
            store_taps(entry_sum, [9 * i + 8], part, i not in seen)
            seen.add(i)
    for i in range(3):
        store(entry_sum.at[9 * i + 8 : 9 * i + 9], entry_out.at[9 * i + 8 : 9 * i + 9])
    terms(2, PAIRS[2], True, True)
    for copy in stores:
        copy.wait()


def run_last(act, wide_one, wide_two, smalls, rows, exit_grad):
    vmem = pl.BlockSpec(memory_space=pltpu.VMEM)
    hbm = pl.BlockSpec(memory_space=pl.ANY)
    shape = jax.ShapeDtypeStruct
    taps = shape((27, CHANNELS, SLICE), F32)
    return pl.pallas_call(
        last_kernel,
        out_shape=(taps, taps, *[shape((1, SLICE), F32)] * 6, *[shape(r.shape, r.dtype) for r in rows]),
        in_specs=[hbm] * 4 + [vmem] * 5,
        out_specs=(hbm, hbm, *[vmem] * 10),
        scratch_shapes=[
            pltpu.VMEM(act.shape, BF16),
            pltpu.VMEM(wide_one.shape, BF16),
            pltpu.VMEM(wide_two.shape, BF16),
            pltpu.VMEM(taps.shape, F32),
            pltpu.VMEM(taps.shape, F32),
            pltpu.SemaphoreType.DMA((2 * FRAMES + 1,)),
            pltpu.SemaphoreType.DMA((16,)),
        ],
        compiler_params=pltpu.CompilerParams(vmem_limit_bytes=60 * 1024 * 1024),
        cost_estimate=pl.CostEstimate(flops=14 * 10**9, bytes_accessed=35 * 10**6, transcendentals=0),
        name="last",
    )(act, wide_one, wide_two, exit_grad, smalls, *rows)


def local(
    first_input,
    second_input,
    first_cotangent,
    second_cotangent,
    entry_gain,
    entry_shift,
    entry_kernel,
    entry_bias,
    exit_gain,
    exit_shift,
    exit_kernel,
    exit_bias,
):
    def rows(values):
        return values.reshape(values.shape[0], OWN, CHANNELS)

    vectors = [
        v.reshape(1, SLICE) for v in (entry_gain, entry_shift, entry_bias, exit_gain, exit_shift, exit_bias)
    ]
    taps = [k.reshape(9, 3, CHANNELS, SLICE) for k in (entry_kernel, exit_kernel)]
    *home, smalls, act_one, wide_one, wide_two, exit_grad = run_block(
        [
            rows(first_input),
            rows(second_input),
            rows(first_cotangent),
            rows(second_cotangent),
            *vectors,
            *taps,
        ]
    )
    entry_grad, exit_grad, *rest = run_last(act_one, wide_one, wide_two, smalls, home, exit_grad)
    small, (out_one, out_two, back_one, back_two) = rest[:6], rest[6:]
    totals = (*small, entry_grad, exit_grad)
    groups = lax.axis_size("wide") // BANDS
    if groups > 1:
        totals = tuple(lax.psum(t, "wide") / BANDS for t in totals)
    *small, entry_grad, exit_grad = totals
    small = [t.reshape(SLICE) for t in small]
    return (
        out_one.reshape(first_input.shape),
        out_two.reshape(second_input.shape),
        back_one.reshape(first_input.shape),
        back_two.reshape(second_input.shape),
        small[0],
        small[1],
        entry_grad,
        small[2],
        small[3],
        small[4],
        exit_grad,
        small[5],
    )


def solution(mesh):
    banded = P(None, ("wide", "narrow"), None, None)
    vector = P("narrow")
    kernel = P(None, None, "narrow")
    return jax.shard_map(
        local,
        mesh=mesh,
        in_specs=(banded,) * 4 + (vector, vector, kernel, vector) * 2,
        out_specs=(banded,) * 4 + (vector, vector, kernel, vector) * 2,
        check_vma=False,
    )
```

```python
import functools

import jax
import jax.numpy as jnp
from jax import lax
from jax.experimental import pallas as pl
from jax.experimental.pallas import tpu as pltpu
from jax.sharding import PartitionSpec as P

GROUPS = 32
HEIGHT_ONE = 32
HEIGHT_TWO = 16
CHANNELS = 512
NARROW = 4
BANDS = 8
SLICE = 128
FRAMES = 5
FIRST = 3
BAND = 128
OWN = 32
LONG = 192

EPS = 1e-06
F32 = jnp.float32
BF16 = jnp.bfloat16
MESH = pl.DeviceIdType.MESH

FORWARD = {
    1: ((0, 3, 0), (3, 5, 3)),
    0: ((0, 2, 1), (3, 4, 4)),
    2: ((1, 3, 0), (4, 5, 3)),
}
BACKWARD = {
    1: ((0, 3, 0), (3, 5, 3)),
    0: ((1, 3, 0), (4, 5, 3)),
    2: ((0, 2, 1), (3, 4, 4)),
}


TWO = {"x": True, "a2": False}
ORDER = (
    "prep",
    "st0",
    "xh1",
    "gown",
    "xsend",
    "gstart",
    "xh2",
    "T2",
    "T2b",
    "z g 1",
    "xown",
    "act",
    "T2c",
    "C1",
    "xbulk",
    "rs0",
    "C1b",
    "C1c",
    "S2",
    "a2start",
    "y a2 0",
    "z g 2",
    "a2own",
    "gh2",
    "z a2 1",
    "o a2 0 1",
    "padg 0",
    "padg 1",
    "padg 2",
    "S3",
    "z g 3",
    "prepa 0",
    "z a2 2",
    "wx 0 0 0",
    "wx 0 0 1",
    "wx 0 0 2",
    "wx 0 0 3",
    "o a2 1 0",
    "wx 0 0 4",
    "wx 0 1 0",
    "wx 0 1 1",
    "z x 1",
    "y a2 1",
    "wx 0 1 2",
    "wx 0 1 3",
    "wx 0 1 4",
    "wx 0 2 0",
    "z a2 3",
    "T1",
    "T1b",
    "wx 0 2 1",
    "T1c",
    "wx 0 2 2",
    "wx 0 2 3",
    "mstart",
    "o a2 1 1",
    "y a2 2",
    "wx 0 2 4",
    "padg 3",
    "o a2 2 0",
    "z x 2",
    "prepa 1",
    "wx 1 0 0",
    "wx 1 0 1",
    "wx 1 0 2",
    "rt",
    "wx 1 0 3",
    "wx 1 0 4",
    "wx 1 1 0",
    "wx 1 1 1",
    "wx 1 1 2",
    "wx 1 1 3",
    "wx 1 1 4",
    "o a2 3 0",
    "wx 1 2 0",
    "wx 1 2 1",
    "wx 1 2 2",
    "o a2 2 1",
    "wx 1 2 3",
    "y x 0",
    "y a2 3",
    "wx 1 2 4",
    "z m 1",
    "prepa 2",
    "C2",
    "y x 1",
    "wx 2 0 0",
    "wx 2 0 1",
    "gh1",
    "wx 2 0 2",
    "wx 2 0 3",
    "wx 2 0 4",
    "z x 3",
    "wx 2 1 0",
    "C2b",
    "padm 0",
    "y x 2",
    "wx 2 1 1",
    "o a2 3 1",
    "z m 2",
    "wx 2 1 2",
    "wx 2 1 3",
    "wx 2 1 4",
    "wx 2 2 0",
    "wx 2 2 1",
    "wx 2 2 2",
    "wx 2 2 3",
    "prepa 3",
    "wx 2 2 4",
    "wx 3 0 0",
    "o x 0 1",
    "wx 3 0 1",
    "wx 3 0 2",
    "y x 3",
    "o x 1 1",
    "padm 1",
    "prepx 0",
    "z m 3",
    "wx 3 0 3",
    "wx 3 0 4",
    "wx 3 1 0",
    "wx 3 1 1",
    "wx 3 1 2",
    "wx 3 1 3",
    "wx 3 1 4",
    "o x 2 1",
    "S4",
    "wx 3 2 0",
    "wx 3 2 1",
    "wx 3 2 2",
    "o x 3 1",
    "prepx 1",
    "prepx 2",
    "C2c",
    "prepx 3",
    "wx 3 2 3",
    "wx 3 2 4",
    "padm 2",
    "padm 3",
    "S5",
    "out",
    "fin",
)
REAPS = (47, 71, 94, 118, 136)


def sigmoid_of(values):
    return 0.5 * jnp.tanh(0.5 * values) + 0.5


def group_sum(tile):
    lanes = lax.broadcasted_iota(jnp.int32, tile.shape, 1)
    for step in (1, 2, 4, 8):
        up = pltpu.roll(tile, step, 1)
        down = pltpu.roll(tile, SLICE - step, 1)
        tile = tile + jnp.where((lanes & step) != 0, up, down)
    return tile


def column_ids(rows, width):
    return lax.broadcasted_iota(jnp.int32, (rows, SLICE), 0) % width


def shifted(values, width, k):
    if k == 1:
        return values
    rows = values.shape[0]
    cols = column_ids(rows, width)
    if k == 0:
        return jnp.where(cols == width - 1, 0.0, pltpu.roll(values, rows - 1, 0))
    return jnp.where(cols == 0, 0.0, pltpu.roll(values, 1, 0))


def three_shifts(values, width):
    wide = values.astype(F32)
    return jnp.concatenate([shifted(wide, width, k).astype(BF16) for k in range(3)], axis=1)


def taken(ref, spans, start_one, start_two):
    (a, b, _), (c, d, _) = spans
    one = ref[a:b, start_one : start_one + BAND, :]
    two = ref[c:d, start_two : start_two + BAND, :]
    lanes = ref.shape[2]
    return jnp.concatenate(
        [one.reshape((b - a) * BAND, lanes), two.reshape((d - c) * BAND, lanes)], axis=0
    )


def spread(out, spans, result, fresh):
    (a, b, o), (c, d, p) = spans
    cut = (b - a) * BAND
    one = result[:cut].reshape(b - a, BAND, -1)
    two = result[cut:].reshape(d - c, BAND, -1)
    if fresh:
        out[o : o + b - a] = one
        out[p : p + d - c] = two
    else:
        out[o : o + b - a] += one
        out[p : p + d - c] += two


PARTS = (1, 0, 2)


def conv_forward(act, weights, sums, part):
    i = PARTS[part]
    spans = FORWARD[i]
    rows = jnp.concatenate([taken(act, spans, 32 * j, 16 + 16 * j) for j in range(3)], axis=1)
    taps = weights[3 * i : 3 * i + 3].reshape(3 * CHANNELS, 3 * SLICE)
    spread(sums, spans, jnp.dot(rows, taps, preferred_element_type=F32), part == 0)


def conv_columns(sums, frame, width):
    total = sums[frame, :, SLICE : 2 * SLICE]
    total = total + shifted(sums[frame, :, 0:SLICE], width, 2)
    return total + shifted(sums[frame, :, 2 * SLICE : 3 * SLICE], width, 0)


def conv_backward(grads, weights, sums, part):
    i = PARTS[part]
    spans = BACKWARD[i]
    rows = jnp.concatenate(
        [taken(grads, spans, 64 - 32 * j, 48 - 16 * j) for j in range(3)], axis=1
    )
    taps = jnp.concatenate([weights[3 * i + j] for j in range(3)], axis=1)
    result = lax.dot_general(rows, taps, (((1,), (1,)), ((), ())), preferred_element_type=F32)
    spread(sums, spans, result, part == 0)


def moments(values):
    total = jnp.sum(values, axis=0, keepdims=True)
    off = values - total / values.shape[0]
    return total, jnp.sum(off * off, axis=0, keepdims=True)


def merge(totals, squares, count):
    total = functools.reduce(jnp.add, totals)
    mean = total / (count * len(totals))
    square = functools.reduce(jnp.add, squares)
    for part in totals:
        off = part / count - mean
        square = square + count * off * off
    return total, square


def group_merge(total, square, count):
    mean = total / count
    group_total = group_sum(total)
    off = mean - group_total / (16 * count)
    return group_total, group_sum(square + count * off * off)


def long_row(tile, row):
    return jnp.concatenate([tile[row + k : row + k + 1, :] for k in range(NARROW)], axis=1)


def lanes_of(m):
    if isinstance(m, int):
        return pl.ds(m * SLICE, SLICE)
    return pl.ds(pl.multiple_of(m * SLICE, SLICE), SLICE)


def place_of(k):
    return k % 2 * 2 + k // 2


def store_taps(out, taps, result, fresh):
    for number, tap in enumerate(taps):
        for k in range(NARROW):
            start = place_of(k) * SLICE
            piece = result[start : start + SLICE, number * SLICE : (number + 1) * SLICE]
            rows = slice(k * SLICE, (k + 1) * SLICE)
            if fresh:
                out[tap, rows, :] = piece
            else:
                out[tap, rows, :] += piece


def rows_of(m, offset=0):
    return pl.ds(pl.multiple_of(offset + m * OWN, OWN), OWN)


def clear_pads(three_one, three_two):
    for start in (0, three_one.shape[1] - 32):
        three_one[:, start : start + 32, :] = jnp.zeros((FIRST, 32, 3 * SLICE), BF16)
    for start in (0, three_two.shape[2] - 16):
        three_two[:, :, start : start + 16, :] = jnp.zeros((FRAMES - FIRST, 4, 16, 3 * SLICE), BF16)


def pad_pair(grad_ref, three_one, three_two, pair):
    @pl.loop(0, 2)
    def _(half):
        first = pl.multiple_of(half * BAND, BAND)

        @pl.loop(0, FIRST)
        def _(f):
            start = pl.multiple_of(32 + pair * 2 * BAND + first, 32)
            three_one[f, pl.ds(start, BAND), :] = three_shifts(grad_ref[2 * pair + half, f], 32)

        @pl.loop(0, FRAMES - FIRST)
        def _(f):
            start = pl.multiple_of(16 + first, 16)
            three_two[f, pair, pl.ds(start, BAND), :] = three_shifts(grad_ref[2 * pair + half, FIRST + f], 16)


PAIRS = {
    0: ((0, 1), (1, 2), (3, 4)),
    1: ((0, 0), (1, 1), (2, 2), (3, 3), (4, 4)),
    2: ((1, 0), (2, 1), (4, 3)),
}
TAP_GROUPS = ((0, 1), (2, 3), (4, 5), (6, 7), (8,))


def tap_rows(three_one, three_two, t, tap):
    j, k = tap // 3, tap % 3
    cut = slice(k * SLICE, (k + 1) * SLICE)
    if t < FIRST:
        return three_one[t, (2 - j) * 32 : (2 - j) * 32 + 1024, cut]
    return three_two[t - FIRST, :, (2 - j) * 16 : (2 - j) * 16 + 256, cut].reshape(1024, SLICE)


def weight_terms(act_t, three_one, three_two, i, pairs, group, out, fresh):
    left = jnp.concatenate([act_t[c, s] for s, _ in pairs for c in range(BANDS)], axis=1)
    right = jnp.concatenate(
        [
            jnp.concatenate([tap_rows(three_one, three_two, t, tap) for tap in group], axis=1)
            for _, t in pairs
        ],
        axis=0,
    )
    result = jnp.dot(left, right, preferred_element_type=F32)
    store_taps(out, [9 * i + tap for tap in group], result, fresh)


def pair_weight_terms(act_t, three_one, three_two, pair, i, group, out, fresh):
    def rows(t, tap):
        j, cut = tap // 3, slice(tap % 3 * SLICE, (tap % 3 + 1) * SLICE)
        if t < FIRST:
            start = pl.multiple_of((2 - j) * 32 + pair * 2 * BAND, 32)
            return three_one[t, pl.ds(start, 2 * BAND), cut]
        return three_two[t - FIRST, pair, (2 - j) * 16 : (2 - j) * 16 + 2 * BAND, cut]

    left = jnp.concatenate([act_t[2 * pair + half, s] for s, _ in PAIRS[i] for half in range(2)], axis=1)
    right = jnp.concatenate(
        [jnp.concatenate([rows(t, tap) for tap in group], axis=1) for _, t in PAIRS[i]], axis=0
    )
    result = jnp.dot(left, right, preferred_element_type=F32)
    store_taps(out, [9 * i + tap for tap in group], result, fresh)


def block_kernel(
    x_one, x_two, g_one, g_two, gain_one, shift_one, bias_one, gain_two, shift_two, bias_two,
    entry_hbm, exit_hbm,
    out_one, out_two, back_one, back_two, smalls, act_out, wide_one_out, wide_two_out, exit_grad,
    act_t1, act_t2, g_all, gm_all, three_one, three_two, wide_one, wide_two, exit_sum,
    entry_w, exit_w, own_x, own_g, band_x, band_a, long_g, long_m, params,
    stat_a, stat_b, stat_c, stat_d, stat_e, stat_f, few,
    sums, partial, grad_three, mid, grad_two, grad_one, part_send, part_recv, tail_send, tail_recv, out_send,
    w_sem, send_sem, x_sem, g_sem, p_sem, halo_sem, stat_sem, ga_sem, gm_sem, a1_sem, a2_sem, rs_sem, o_sem, store_sem,
):
    w = lax.axis_index("wide")
    n = lax.axis_index("narrow")
    base = w // BANDS * BANDS
    b = w - base
    z, y = b // 2, b % 2
    has_up, has_down = b > 0, b < BANDS - 1
    pair_up, pair_down = y == 1, y == 0
    flags = lambda f: (has_up, has_down) if f < FIRST else (pair_up, pair_down)
    width_of = lambda f: 32 if f < FIRST else 16
    sub_of = lambda f: 0 if f < FIRST else 1

    sends = []
    used = [0]

    def both(first, second):
        if first is None or second is None:
            return second if first is None else first
        return jnp.logical_and(first, second)

    def under(flag, act):
        if flag is None:
            act()
        else:
            pl.when(flag)(act)

    def make(src, dst, recv, device):
        used[0] += 1
        return pltpu.make_async_remote_copy(
            src_ref=src,
            dst_ref=dst,
            send_sem=send_sem.at[used[0] - 1],
            recv_sem=recv,
            device_id=device,
            device_id_type=MESH,
        )

    def start(copies):
        for copy in copies:
            copy.start()

    def launch(copies, flag=None):
        under(flag, lambda: start(copies))
        sends.append((flag, copies))

    def send(src, dst, recv, device, flag=None):
        launch([make(src, dst, recv, device)], flag)

    def reap(count):
        for flag, copies in sends[:count]:

            def wait_all(copies=copies):
                for copy in copies:
                    copy.wait_send()

            under(flag, wait_all)
        del sends[:count]

    def arrived(dst, recv, flag=None):
        wait = pltpu.make_async_remote_copy(
            src_ref=dst,
            dst_ref=dst,
            send_sem=send_sem.at[0],
            recv_sem=recv,
            device_id=(w, n),
            device_id_type=MESH,
        ).wait_recv
        under(flag, wait)

    def beside(m):
        return (w, m)

    def band_of(c):
        return (base + c, n)

    others = [lax.rem(n + d, NARROW) for d in (1, 2, 3)]
    far = [lax.rem(b + d, BANDS) for d in range(1, BANDS)]
    sib, opp, cross = n ^ 1, n ^ 2, n ^ 3
    beyond = b + 1 - 2 * y
    slant = b - 1 + 2 * y
    above = lax.rem(b + BANDS - 1, BANDS)
    below = lax.rem(b + 1, BANDS)
    up_chip = lax.rem(b + BANDS - 2, BANDS)
    down_chip = lax.rem(b + 2, BANDS)
    pairs_by_distance = [z, z + 1 - 2 * (z % 2), 2 - z // 2, 3 - 3 * (z // 2)]
    mine, mine_long = rows_of(n), rows_of(n, 32)

    sem_of = {"x": a1_sem, "a2": a2_sem, "g": ga_sem, "m": gm_sem}
    array_of = {"x": act_t1, "a2": act_t2, "g": g_all, "m": gm_all}

    def block(name, c, k):
        if name in ("g", "m"):
            return array_of[name].at[c]
        return array_of[name].at[c, :, lanes_of(place_of(k)), :]

    def couple(name, c, k):
        rows = pl.ds(pl.multiple_of(k % 2 * 2 * SLICE, 2 * SLICE), 2 * SLICE)
        return array_of[name].at[c, :, rows, :]

    def sem(name, c, kind):
        return sem_of[name].at[c] if name in ("g", "m") else sem_of[name].at[c, kind]

    def own(name, c):
        return couple(name, c, n) if TWO.get(name) else block(name, c, n)

    def to(ref, name, c, kind, device):
        return make(ref, ref, sem(name, c, kind), device)

    def to_opp(name, c):
        return to(block(name, c, n), name, c, 1, beside(opp))

    def to_sib(name, c):
        return to(couple(name, c, n), name, c, 2, beside(sib))

    def to_beyond(name, c):
        return to(block(name, c, n), name, c, 0, band_of(beyond))

    def at_distance(step, line):
        for sign in (-1, 1) if step else (1,):
            there = None if step == 0 else (z >= step if sign < 0 else z + step <= 3)
            c = lax.rem(b + 2 * sign * step + BANDS, BANDS)
            yield sign, there, c if line == 0 else c + 1 - 2 * y

    def z_step(name, step):
        for sign, there, c in at_distance(step, 0):
            arrived(own(name, c), sem(name, c, 0), there)
            copies = [to_beyond(name, c)]
            if name in ("x", "a2"):
                copies.append(to_sib(name, c) if TWO[name] else to_opp(name, c))
            if step < 3:
                onward, target = (z < 3, down_chip) if sign < 0 else (z > 0, up_chip)
                launch([to(own(name, c), name, c, 0, band_of(target))], both(there, onward))
            launch(copies, there)

    def y_step(name, step):
        for _, there, c in at_distance(step, 1):
            arrived(block(name, c, n), sem(name, c, 0), there)
            launch([to_opp(name, c)], there)

    def o_step(name, step, line):
        for _, there, c in at_distance(step, line):
            arrived(block(name, c, opp), sem(name, c, 1), there)
            launch([to_sib(name, c)], there)

    def begin(name):
        launch([to(own(name, b), name, b, 0, band_of(down_chip))], z < 3)
        launch([to(own(name, b), name, b, 0, band_of(up_chip))], z > 0)
        launch([to_beyond(name, b)])

    def await_sib(name, c):
        arrived(couple(name, c, sib), sem(name, c, 2))

    def to_bands(stat, number):
        for c in far:
            send(stat.at[b], stat.at[b], stat_sem.at[number, b], band_of(c))

    def from_bands(stat, number):
        for c in far:
            arrived(stat.at[b], stat_sem.at[number, c])

    def to_narrow(stat, number):
        for m in others:
            send(stat.at[n], stat.at[n], stat_sem.at[number, n], beside(m))

    def from_narrow(stat, number):
        for m in others:
            arrived(stat.at[n], stat_sem.at[number, m])

    def exchange_rims(ref, first_sem):
        send(ref.at[0:3, 128:160, :], ref.at[0:3, 0:32, :], halo_sem.at[first_sem], band_of(below), has_down)
        send(ref.at[0:3, 32:64, :], ref.at[0:3, 160:192, :], halo_sem.at[first_sem + 1], band_of(above), has_up)
        send(ref.at[3:5, 144:160, :], ref.at[3:5, 16:32, :], halo_sem.at[first_sem + 2], band_of(beyond), pair_down)
        send(ref.at[3:5, 32:48, :], ref.at[3:5, 160:176, :], halo_sem.at[first_sem + 3], band_of(beyond), pair_up)

    def await_rims(ref, first_sem):
        arrived(ref.at[0:3, 0:32, :], halo_sem.at[first_sem], has_up)
        arrived(ref.at[0:3, 160:192, :], halo_sem.at[first_sem + 1], has_down)
        arrived(ref.at[3:5, 16:32, :], halo_sem.at[first_sem + 2], pair_up)
        arrived(ref.at[3:5, 160:176, :], halo_sem.at[first_sem + 3], pair_down)

    stores = []

    def store(source, target, number):
        copy = pltpu.make_async_copy(source, target, store_sem.at[number])
        copy.start()
        stores.append(copy)

    kept = {}
    count_one = 3 * BAND * BANDS
    count_two = 2 * BAND * 2

    def prep():
        loads = []
        for number, (source, target) in enumerate(((exit_hbm, exit_w), (entry_hbm, entry_w))):
            for k in range(3):
                load = pltpu.make_async_copy(
                    source.at[:, k],
                    target.at[:, :, k * SLICE : (k + 1) * SLICE],
                    w_sem.at[number, k],
                )
                load.start()
                loads.append(load)
        kept["loads"] = loads
        own_x[0:FIRST] = x_one[...]
        own_x[FIRST:FRAMES] = x_two[...]
        own_g[0:FIRST] = g_one[...]
        own_g[FIRST:FRAMES] = g_two[...]
        for ref in (params, stat_c, stat_d, stat_f, smalls):
            ref[...] = jnp.zeros_like(ref)
        for ref in (band_x, long_g, long_m):
            for start in (0, 160):
                ref[:, start : start + 32, :] = jnp.zeros((FRAMES, 32, ref.shape[2]), BF16)
        for row, ref in enumerate((gain_one, shift_one, bias_one, gain_two, shift_two, bias_two)):
            params[n, row : row + 1, :] = ref[...].astype(F32)
        band_x[:, mine_long, :] = own_x[...]
        long_g[:, mine_long, :] = own_g[:, :, lanes_of(n)]

        barrier = pltpu.get_barrier_semaphore()
        for m in others:
            pl.semaphore_signal(barrier, inc=1, device_id=beside(m), device_id_type=MESH)
        for c in far:
            pl.semaphore_signal(barrier, inc=1, device_id=band_of(c), device_id_type=MESH)
        for sub, (start, stop) in enumerate(((0, FIRST), (FIRST, FRAMES))):
            values = own_x[start:stop].astype(F32).reshape((stop - start) * OWN, CHANNELS)
            total, square = moments(values)
            cuts = [slice(k * SLICE, (k + 1) * SLICE) for k in range(NARROW)]
            t, s = group_merge(
                jnp.concatenate([total[:, cut] for cut in cuts], axis=0),
                jnp.concatenate([square[:, cut] for cut in cuts], axis=0),
                float(values.shape[0]),
            )
            stat_a[n, 8 * sub : 8 * sub + 4, :] = t
            stat_a[n, 8 * sub + 4 : 8 * sub + 8, :] = s
        pl.semaphore_wait(barrier, NARROW - 1 + BANDS - 1)
        to_narrow(stat_a, 0)
        rims_out()
        for m in others:
            send(own_g.at[:, :, lanes_of(m)], long_g.at[:, mine_long, :], g_sem.at[n], beside(m))
            send(params.at[n], params.at[n], p_sem.at[n], beside(m))
        clear_pads(wide_one, wide_two)
        clear_pads(three_one, three_two)

    def xsend():
        for number, start in enumerate((0, three_one.shape[1] - 32)):
            rows = slice(start, start + 32)
            store(three_one.at[:, rows, :], wide_one_out.at[:, rows, :], 12 + number)
        for m in (opp, sib):
            send(own_x, band_x.at[:, mine_long, :], x_sem.at[n], beside(m))

    def st0():
        from_narrow(stat_a, 0)
        for sub, count in ((0, 3 * OWN * 16.0), (1, 2 * OWN * 16.0)):
            t, s = merge(
                [stat_a[m, 8 * sub : 8 * sub + 4, :] for m in range(NARROW)],
                [stat_a[m, 8 * sub + 4 : 8 * sub + 8, :] for m in range(NARROW)],
                count,
            )
            stat_b[b, 8 * sub : 8 * sub + 4, :] = t
            stat_b[b, 8 * sub + 4 : 8 * sub + 8, :] = s
        to_bands(stat_b, 1)

    def gown():
        for m in others:
            arrived(long_g.at[:, mine_long, :], g_sem.at[m])
        exchange_rims(long_g, 4)
        g_all[b] = long_g[:, 32:160, :]

    def rim_parts():
        return (
            (band_x.at[0:3, 0:32, :], 0, own_x.at[0:3], below, has_down, has_up, 3),
            (band_x.at[3:5, 16:32, :], 2, own_x.at[3:5, 16:32, :], beyond, pair_down, pair_up, 3),
            (band_x.at[0:3, 160:192, :], 1, own_x.at[0:3], above, has_up, has_down, 0),
            (band_x.at[3:5, 160:176, :], 3, own_x.at[3:5, 0:16, :], beyond, pair_up, pair_down, 0),
        )

    def rims_out():
        for ref, number, own, target, gives, _, owner in rim_parts():
            send(own, ref, halo_sem.at[number], band_of(target), both(gives, n == owner))

    def xh1():
        for ref, number, _, _, _, takes, owner in rim_parts():
            flag = both(takes, n == owner)
            arrived(ref, halo_sem.at[number], flag)
            send(ref, ref, halo_sem.at[number], beside(opp), flag)
            send(ref, ref, halo_sem.at[number], beside(sib), flag)

    def xh2():
        for ref, number, _, _, _, takes, owner in rim_parts():
            flag = both(takes, n == (owner + 2) % 4)
            arrived(ref, halo_sem.at[number], flag)
            send(ref, ref, halo_sem.at[number], beside(sib), flag)

    def xh3():
        for ref, number, _, _, _, takes, owner in rim_parts():
            arrived(ref, halo_sem.at[number], both(takes, n % 2 != owner % 2))

    def xown():
        arrived(band_x.at[:, mine_long, :], x_sem.at[opp])
        theirs = band_x.at[:, rows_of(opp, 32), :]
        send(theirs, theirs, x_sem.at[opp], beside(sib))
        arrived(band_x.at[:, mine_long, :], x_sem.at[sib])
        arrived(band_x.at[:, mine_long, :], x_sem.at[cross])

    def first_hidden(values, sub):
        normed = (values - kept["mean_one"][sub]) * kept["inv_one"][sub]
        return normed, normed * kept["gain_long"] + kept["shift_long"]

    def first_active(f, start, stop):
        _, hidden = first_hidden(band_x[f, start:stop].astype(F32), sub_of(f))
        return (hidden * sigmoid_of(hidden)).astype(BF16)

    def act():
        for m in others:
            arrived(params.at[n], p_sem.at[m])
        from_bands(stat_b, 1)
        one_total, one_square = merge(
            [stat_b[c, 0:4, :] for c in range(BANDS)],
            [stat_b[c, 4:8, :] for c in range(BANDS)],
            3 * BAND * 16.0,
        )
        two_total, two_square = merge(
            [stat_b[b, 8:12, :], stat_b[beyond, 8:12, :]],
            [stat_b[b, 12:16, :], stat_b[beyond, 12:16, :]],
            2 * BAND * 16.0,
        )
        kept["mean_one"] = [
            long_row(one_total / (16.0 * count_one), 0),
            long_row(two_total / (16.0 * count_two), 0),
        ]
        kept["inv_one"] = [
            long_row(lax.rsqrt(one_square / (16.0 * count_one) + EPS), 0),
            long_row(lax.rsqrt(two_square / (16.0 * count_two) + EPS), 0),
        ]
        kept["gain_long"] = jnp.concatenate([params[m, 0:1, :] for m in range(NARROW)], axis=1)
        kept["shift_long"] = jnp.concatenate([params[m, 1:2, :] for m in range(NARROW)], axis=1)
        for f in range(FRAMES):
            active = first_active(f, 32, 160)
            band_a[f, 32:160, :] = active
            for k in range(NARROW):
                cut = slice(k * SLICE, (k + 1) * SLICE)
                act_t1[b, f, lanes_of(place_of(k)), :] = active[:, cut].T

    def lay_out(long):
        for f in range(FRAMES):
            grad_three[f] = three_shifts(long[f], width_of(f))

    def t2():
        await_rims(long_g, 4)
        lay_out(long_g)
        for load in kept["loads"][:3]:
            load.wait()
        conv_backward(grad_three, exit_w, partial, 0)

    def t2c():
        conv_backward(grad_three, exit_w, partial, 2)
        part_send[0] = partial[:, :, lanes_of(sib)].astype(BF16)
        part_send[1] = partial[:, :, lanes_of(cross)].astype(BF16)
        for k in range(2):
            send(part_send.at[k], part_recv.at[k], rs_sem.at[0, k], beside(sib))

    def rs0():
        for k in range(2):
            arrived(part_recv.at[k], rs_sem.at[0, k])
        part_send[2] = (partial[:, :, lanes_of(opp)] + part_recv[1].astype(F32)).astype(BF16)
        send(part_send.at[2], part_recv.at[2], rs_sem.at[0, 2], beside(opp))

    def c1():
        xh3()
        for f in range(FRAMES):
            width = width_of(f)
            up, down = flags(f)
            row = first_active(f, 32 - width, 32)
            band_a[f, 32 - width : 32, :] = jnp.where(up, row, jnp.zeros_like(row))
            row = first_active(f, 160, 160 + width)
            band_a[f, 160 : 160 + width, :] = jnp.where(down, row, jnp.zeros_like(row))
        for load in kept["loads"][3:]:
            load.wait()
        conv_forward(band_a, entry_w, sums, 0)

    def c1c():
        conv_forward(band_a, entry_w, sums, 2)
        for f in range(FRAMES):
            mid[f] = conv_columns(sums, f, width_of(f)) + params[n, 2:3, :]
        for sub, (start, stop) in enumerate(((0, FIRST), (FIRST, FRAMES))):
            values = mid[start:stop].reshape((stop - start) * BAND, SLICE)
            total, square = moments(values)
            t, s = group_merge(total, square, float(values.shape[0]))
            stat_c[b, 2 * sub : 2 * sub + 1, :] = t
            stat_c[b, 2 * sub + 1 : 2 * sub + 2, :] = s
        to_bands(stat_c, 2)

    def s2():
        from_bands(stat_c, 2)
        one_total, one_square = merge(
            [stat_c[c, 0:1, :] for c in range(BANDS)],
            [stat_c[c, 1:2, :] for c in range(BANDS)],
            3 * BAND * 16.0,
        )
        two_total, two_square = merge(
            [stat_c[b, 2:3, :], stat_c[beyond, 2:3, :]],
            [stat_c[b, 3:4, :], stat_c[beyond, 3:4, :]],
            2 * BAND * 16.0,
        )
        mean_two = [one_total / (16.0 * count_one), two_total / (16.0 * count_two)]
        kept["inv_two"] = [
            lax.rsqrt(one_square / (16.0 * count_one) + EPS),
            lax.rsqrt(two_square / (16.0 * count_two) + EPS),
        ]
        kept["gain_own"], kept["shift_own"] = params[n, 3:4, :], params[n, 4:5, :]
        for f in range(FRAMES):
            normed = (mid[f] - mean_two[sub_of(f)]) * kept["inv_two"][sub_of(f)]
            mid[f] = normed
            hidden = normed * kept["gain_own"] + kept["shift_own"]
            act_t2[b, f, lanes_of(place_of(n)), :] = (hidden * sigmoid_of(hidden)).astype(BF16).T

    def gh2():
        arrived(part_recv.at[2], rs_sem.at[0, 2])
        rows_sum = [[0.0, 0.0], [0.0, 0.0]]
        for f in range(FRAMES):
            sub = sub_of(f)
            grad = partial[f, :, lanes_of(n)] + part_recv[0, f].astype(F32) + part_recv[2, f].astype(F32)
            hidden = mid[f] * kept["gain_own"] + kept["shift_own"]
            sigmoid = sigmoid_of(hidden)
            grad = grad * (sigmoid * (1.0 + hidden * (1.0 - sigmoid)))
            grad_two[f] = grad
            rows_sum[sub][0] += jnp.sum(grad, axis=0, keepdims=True)
            rows_sum[sub][1] += jnp.sum(grad * mid[f], axis=0, keepdims=True)
        for sub in range(2):
            stat_d[b, 2 * sub : 2 * sub + 1, :] = rows_sum[sub][0]
            stat_d[b, 2 * sub + 1 : 2 * sub + 2, :] = rows_sum[sub][1]
        own = g_all[b].astype(F32).reshape(FRAMES * BAND, SLICE)
        stat_d[b, 4:5, :] = jnp.sum(own, axis=0, keepdims=True)
        to_bands(stat_d, 3)

    def a2start():
        begin("a2")
        launch([to_opp("a2", b)])

    def a2own():
        o_step("a2", 0, 0)

    def s3():
        from_bands(stat_d, 3)
        gain_own = kept["gain_own"]
        all_rows = [
            functools.reduce(jnp.add, [stat_d[c, r : r + 1, :] for c in range(BANDS)]) for r in range(5)
        ]
        smalls[3:4, :] = all_rows[1] + all_rows[3]
        smalls[4:5, :] = all_rows[0] + all_rows[2]
        smalls[5:6, :] = all_rows[4]
        pair_rows = [stat_d[b, r : r + 1, :] + stat_d[beyond, r : r + 1, :] for r in range(4)]
        p_two = [
            group_sum(gain_own * all_rows[0]) / (16.0 * count_one),
            group_sum(gain_own * pair_rows[2]) / (16.0 * count_two),
        ]
        q_two = [
            group_sum(gain_own * all_rows[1]) / (16.0 * count_one),
            group_sum(gain_own * pair_rows[3]) / (16.0 * count_two),
        ]
        bias_sum = 0.0
        for f in range(FRAMES):
            sub = sub_of(f)
            grad = (grad_two[f] * gain_own - p_two[sub] - mid[f] * q_two[sub]) * kept["inv_two"][sub]
            grad = grad.astype(BF16)
            gm_all[b, f] = grad
            long_m[f, 32:160, :] = grad
            bias_sum = bias_sum + jnp.sum(grad.astype(F32), axis=0, keepdims=True)
        stat_f[b, 16:17, :] = bias_sum
        exchange_rims(long_m, 8)

    def t1():
        await_rims(long_m, 8)
        lay_out(long_m)
        conv_backward(grad_three, entry_w, partial, 0)

    def t1c():
        conv_backward(grad_three, entry_w, partial, 2)
        tail_send[0] = partial[:, rows_of(sib), :].astype(BF16)
        tail_send[1] = partial[:, rows_of(cross), :].astype(BF16)
        for k in range(2):
            send(tail_send.at[k], tail_recv.at[k], rs_sem.at[1, k], beside(sib))

    def rt():
        for k in range(2):
            arrived(tail_recv.at[k], rs_sem.at[1, k])
        tail_send[2] = (partial[:, rows_of(opp), :] + tail_recv[1].astype(F32)).astype(BF16)
        send(tail_send.at[2], tail_recv.at[2], rs_sem.at[1, 2], beside(opp))

    def gh1():
        arrived(tail_recv.at[2], rs_sem.at[1, 2])
        for sub, (start, stop) in enumerate(((0, FIRST), (FIRST, FRAMES))):
            first_sum, second_sum = 0.0, 0.0
            for f in range(start, stop):
                grad = partial[f, mine, :] + tail_recv[0, f].astype(F32) + tail_recv[2, f].astype(F32)
                normed, hidden = first_hidden(own_x[f].astype(F32), sub)
                sigmoid = sigmoid_of(hidden)
                grad = grad * (sigmoid * (1.0 + hidden * (1.0 - sigmoid)))
                grad_one[f] = grad
                first_sum = first_sum + jnp.sum(grad, axis=0, keepdims=True)
                second_sum = second_sum + jnp.sum(grad * normed, axis=0, keepdims=True)
            for k in range(NARROW):
                cut = slice(k * SLICE, (k + 1) * SLICE)
                stat_e[n, 8 * sub + k : 8 * sub + k + 1, :] = first_sum[:, cut]
                stat_e[n, 8 * sub + 4 + k : 8 * sub + 5 + k, :] = second_sum[:, cut]
        to_narrow(stat_e, 4)

    def s4():
        from_narrow(stat_e, 4)
        stat_f[b, 0:16, :] = stat_e[0] + stat_e[1] + stat_e[2] + stat_e[3]
        to_bands(stat_f, 5)

    def s5():
        from_bands(stat_f, 5)
        all_sums = functools.reduce(jnp.add, [stat_f[c] for c in range(BANDS)])
        pair_sums = stat_f[b] + stat_f[beyond]
        few[0, 0:4, :] = all_sums[0:4] + all_sums[8:12]
        few[1, 0:4, :] = all_sums[4:8] + all_sums[12:16]
        smalls[0:1, :] = few[1, pl.ds(n, 1), :]
        smalls[1:2, :] = few[0, pl.ds(n, 1), :]
        smalls[2:3, :] = all_sums[16:17]
        gain_rows = jnp.concatenate([params[m, 0:1, :] for m in range(NARROW)], axis=0)
        p_one = [
            long_row(group_sum(gain_rows * all_sums[0:4]) / (16.0 * count_one), 0),
            long_row(group_sum(gain_rows * pair_sums[8:12]) / (16.0 * count_two), 0),
        ]
        q_one = [
            long_row(group_sum(gain_rows * all_sums[4:8]) / (16.0 * count_one), 0),
            long_row(group_sum(gain_rows * pair_sums[12:16]) / (16.0 * count_two), 0),
        ]
        for f in range(FRAMES):
            sub = sub_of(f)
            normed, _ = first_hidden(own_x[f].astype(F32), sub)
            grad = grad_one[f] * kept["gain_long"] - p_one[sub] - normed * q_one[sub]
            grad = (own_g[f].astype(F32) + grad * kept["inv_one"][sub]).astype(BF16)
            if sub == 0:
                back_one[f] = grad
            else:
                back_two[f - FIRST] = grad

    def prepa(number):
        first = 2 * pairs_by_distance[number]
        await_sib("a2", first)
        await_sib("a2", first + 1)

    def pad(name, number, array, one, two):
        pair = pairs_by_distance[number]
        c = 2 * pair + 1 - y
        arrived(block(name, c, n), sem(name, c, 0))
        pad_pair(array, one, two, pair)

    def padg(number):
        pad("g", number, g_all, wide_one, wide_two)

    def c2():
        @pl.loop(0, NARROW)
        def _(k):
            cut = lanes_of(k)
            rows = lanes_of(place_of(k))
            for f in range(FRAMES):
                width = width_of(f)
                up, down = flags(f)
                band_a[f, 32:160, cut] = act_t2[b, f, rows, :].T
                row = act_t2[b - (b + 7) // 8, f, rows, :].T[BAND - width : BAND]
                band_a[f, 32 - width : 32, cut] = jnp.where(up, row, jnp.zeros_like(row))
                row = act_t2[b + (14 - b) // 8, f, rows, :].T[0:width]
                band_a[f, 160 : 160 + width, cut] = jnp.where(down, row, jnp.zeros_like(row))

        conv_forward(band_a, exit_w, sums, 0)

    def c2c():
        conv_forward(band_a, exit_w, sums, 2)
        for f in range(FRAMES):
            total = conv_columns(sums, f, width_of(f)) + params[n, 5:6, :]
            total = total + band_x[f, 32:160, lanes_of(n)].astype(F32)
            out_send[f] = total.astype(BF16)
        for m in others:
            send(out_send.at[0:3, rows_of(m), :], out_one.at[:, :, lanes_of(n)], o_sem.at[0, n], beside(m))
            send(out_send.at[3:5, rows_of(m), :], out_two.at[:, :, lanes_of(n)], o_sem.at[1, n], beside(m))
        out_one[:, :, lanes_of(n)] = out_send[0:3, mine, :]
        out_two[:, :, lanes_of(n)] = out_send[3:5, mine, :]

    def out():
        for m in others:
            arrived(out_one.at[:, :, lanes_of(m)], o_sem.at[0, m])
            arrived(out_two.at[:, :, lanes_of(m)], o_sem.at[1, m])

    def wx(number, place, group):
        i = PARTS[place]
        taps = TAP_GROUPS[group]
        pair = pairs_by_distance[number]
        pair_weight_terms(act_t2, wide_one, wide_two, pair, i, taps, exit_sum, number == 0)
        if number == 3 and group == len(TAP_GROUPS) - 1:
            cut = slice(9 * i, 9 * i + 9)
            store(exit_sum.at[cut], exit_grad.at[cut], 14 + i)

    def prepx(number):
        first = 2 * pairs_by_distance[number]
        if number == 0:
            await_sib("x", beyond)
        else:
            await_sib("x", first)
            await_sib("x", first + 1)
        store(act_t1.at[pl.ds(first, 2)], act_out.at[pl.ds(first, 2)], number)

    def padm(number):
        pad("m", number, gm_all, three_one, three_two)
        pair = pairs_by_distance[number]
        rows = pl.ds(pl.multiple_of(32 + pair * 2 * BAND, 32), 2 * BAND)
        store(three_one.at[:, rows, :], wide_one_out.at[:, rows, :], 4 + number)
        store(three_two.at[:, pair], wide_two_out.at[:, pair], 8 + number)

    def fin():
        reap(len(sends))
        for copy in stores:
            copy.wait()

    backward = lambda weights, part: lambda: conv_backward(grad_three, weights, partial, part)
    forward = lambda weights, part: lambda: conv_forward(band_a, weights, sums, part)
    steps = {
        "prep": prep, "xsend": xsend, "st0": st0, "gown": gown, "xown": xown, "xh1": xh1, "xh2": xh2, "act": act,
        "T2": t2, "T2b": backward(exit_w, 1), "T2c": t2c, "rs0": rs0,
        "C1": c1, "C1b": forward(entry_w, 1), "C1c": c1c,
        "S2": s2, "gh2": gh2, "a2start": a2start, "a2own": a2own, "S3": s3,
        "T1": t1, "T1b": backward(entry_w, 1), "T1c": t1c, "rt": rt, "gh1": gh1, "S4": s4, "S5": s5,
        "C2": c2, "C2b": forward(exit_w, 1), "C2c": c2c, "out": out,
        "padg": padg, "padm": padm, "fin": fin,
        "gstart": lambda: begin("g"),
        "mstart": lambda: begin("m"),
        "xbulk": lambda: begin("x"),
        "z": z_step, "y": y_step, "o": o_step, "wx": wx, "prepx": prepx, "prepa": prepa,
    }
    before = 0
    for number, item in enumerate(ORDER):
        if number in REAPS:
            count, before = before, len(sends) - before
            reap(count)
        word, *rest = item.split()
        steps[word](*[int(r) if r.isdigit() else r for r in rest])


def run_block(args):
    vmem = pl.BlockSpec(memory_space=pltpu.VMEM)
    hbm = pl.BlockSpec(memory_space=pl.ANY)
    dma = pltpu.SemaphoreType.DMA
    shape = jax.ShapeDtypeStruct
    everyone = (BANDS, FRAMES, CHANNELS, BAND)
    wide_one = (FIRST, 34 * 32, 3 * SLICE)
    wide_two = (FRAMES - FIRST, 4, 18 * 16, 3 * SLICE)
    return pl.pallas_call(
        block_kernel,
        out_shape=(
            shape((FIRST, OWN, CHANNELS), BF16),
            shape((FRAMES - FIRST, OWN, CHANNELS), BF16),
            shape((FIRST, OWN, CHANNELS), BF16),
            shape((FRAMES - FIRST, OWN, CHANNELS), BF16),
            shape((8, SLICE), F32),
            shape(everyone, BF16),
            shape(wide_one, BF16),
            shape(wide_two, BF16),
            shape((27, CHANNELS, SLICE), F32),
        ),
        in_specs=[vmem] * 10 + [hbm] * 2,
        out_specs=(vmem,) * 5 + (hbm,) * 4,
        scratch_shapes=[
            pltpu.VMEM(everyone, BF16),
            pltpu.VMEM(everyone, BF16),
            pltpu.VMEM((BANDS, FRAMES, BAND, SLICE), BF16),
            pltpu.VMEM((BANDS, FRAMES, BAND, SLICE), BF16),
            pltpu.VMEM(wide_one, BF16),
            pltpu.VMEM(wide_two, BF16),
            pltpu.VMEM(wide_one, BF16),
            pltpu.VMEM(wide_two, BF16),
            pltpu.VMEM((27, CHANNELS, SLICE), F32),
            pltpu.VMEM((9, CHANNELS, 3 * SLICE), BF16),
            pltpu.VMEM((9, CHANNELS, 3 * SLICE), BF16),
            pltpu.VMEM((FRAMES, OWN, CHANNELS), BF16),
            pltpu.VMEM((FRAMES, OWN, CHANNELS), BF16),
            pltpu.VMEM((FRAMES, LONG, CHANNELS), BF16),
            pltpu.VMEM((FRAMES, LONG, CHANNELS), BF16),
            pltpu.VMEM((FRAMES, LONG, SLICE), BF16),
            pltpu.VMEM((FRAMES, LONG, SLICE), BF16),
            pltpu.VMEM((NARROW, 8, SLICE), F32),
            pltpu.VMEM((NARROW, 16, SLICE), F32),
            pltpu.VMEM((BANDS, 16, SLICE), F32),
            pltpu.VMEM((BANDS, 8, SLICE), F32),
            pltpu.VMEM((BANDS, 8, SLICE), F32),
            pltpu.VMEM((NARROW, 16, SLICE), F32),
            pltpu.VMEM((BANDS, 24, SLICE), F32),
            pltpu.VMEM((2, 8, SLICE), F32),
            pltpu.VMEM((FRAMES, BAND, 3 * SLICE), F32),
            pltpu.VMEM((FRAMES, BAND, CHANNELS), F32),
            pltpu.VMEM((FRAMES, LONG, 3 * SLICE), BF16),
            pltpu.VMEM((FRAMES, BAND, SLICE), F32),
            pltpu.VMEM((FRAMES, BAND, SLICE), F32),
            pltpu.VMEM((FRAMES, OWN, CHANNELS), F32),
            pltpu.VMEM((3, FRAMES, BAND, SLICE), BF16),
            pltpu.VMEM((3, FRAMES, BAND, SLICE), BF16),
            pltpu.VMEM((3, FRAMES, OWN, CHANNELS), BF16),
            pltpu.VMEM((3, FRAMES, OWN, CHANNELS), BF16),
            pltpu.VMEM((FRAMES, BAND, SLICE), BF16),
            dma((2, 3)),
            dma((288,)),
            dma((NARROW,)),
            dma((NARROW,)),
            dma((NARROW,)),
            dma((12,)),
            dma((6, BANDS)),
            dma((BANDS,)),
            dma((BANDS,)),
            dma((BANDS, 3)),
            dma((BANDS, 3)),
            dma((2, 3)),
            dma((2, NARROW)),
            dma((17,)),
        ],
        compiler_params=pltpu.CompilerParams(
            collective_id=0, has_side_effects=True, vmem_limit_bytes=62 * 1024 * 1024
        ),
        cost_estimate=pl.CostEstimate(flops=20 * 10**9, bytes_accessed=3 * 10**7, transcendentals=0),
        name="block",
    )(*args)


def last_kernel(act_hbm, one_hbm, two_hbm, exit_hbm, smalls, *refs):
    rows, (entry_out, exit_out, *vectors), rest = refs[:4], refs[4:12], refs[12:]
    row_outs, (act_t, wide_one, wide_two, entry_sum, exit_sum, load_sem, store_sem) = rest[:4], rest[4:]

    loads = []
    for f in range(FRAMES):
        first = pltpu.make_async_copy(act_hbm.at[:, f], act_t.at[:, f], load_sem.at[f])
        if f < FIRST:
            second = pltpu.make_async_copy(one_hbm.at[f], wide_one.at[f], load_sem.at[FRAMES + f])
        else:
            place = f - FIRST
            second = pltpu.make_async_copy(two_hbm.at[place], wide_two.at[place], load_sem.at[FRAMES + f])
        first.start()
        second.start()
        loads.append((first, second))
    through = pltpu.make_async_copy(exit_hbm, exit_sum, load_sem.at[2 * FRAMES])
    through.start()
    for row, ref in enumerate(vectors):
        ref[...] = smalls[row : row + 1, :]
    for source, target in zip(rows, row_outs):
        target[...] = source[...]

    stores = []

    def store(source, target):
        copy = pltpu.make_async_copy(source, target, store_sem.at[len(stores)])
        copy.start()
        stores.append(copy)

    def terms(i, pairs, fresh, last):
        for group in TAP_GROUPS[:4]:
            weight_terms(act_t, wide_one, wide_two, i, pairs, group, entry_sum, fresh)
            if last:
                taps = slice(9 * i + group[0], 9 * i + group[-1] + 1)
                store(entry_sum.at[taps], entry_out.at[taps])

    for parts, pairs in ((loads[:2], PAIRS[1][:2]), (loads[2:], PAIRS[1][2:])):
        for first, second in parts:
            first.wait()
            second.wait()
        terms(1, pairs, pairs[0][0] == 0, pairs[-1][0] == FRAMES - 1)
    through.wait()
    store(exit_sum, exit_out)
    terms(0, PAIRS[0], True, True)
    seen = set()
    for s in range(FRAMES):
        meets = [(i, t) for i in range(3) for other, t in PAIRS[i] if other == s]
        right = jnp.concatenate([tap_rows(wide_one, wide_two, t, 8) for _, t in meets], axis=1)
        left = jnp.concatenate([act_t[c, s] for c in range(BANDS)], axis=1)
        result = jnp.dot(left, right, preferred_element_type=F32)
        for place, (i, _) in enumerate(meets):
            part = result[:, place * SLICE : (place + 1) * SLICE]
            store_taps(entry_sum, [9 * i + 8], part, i not in seen)
            seen.add(i)
    for i in range(3):
        store(entry_sum.at[9 * i + 8 : 9 * i + 9], entry_out.at[9 * i + 8 : 9 * i + 9])
    terms(2, PAIRS[2], True, True)
    for copy in stores:
        copy.wait()


def run_last(act, wide_one, wide_two, smalls, rows, exit_grad):
    vmem = pl.BlockSpec(memory_space=pltpu.VMEM)
    hbm = pl.BlockSpec(memory_space=pl.ANY)
    shape = jax.ShapeDtypeStruct
    taps = shape((27, CHANNELS, SLICE), F32)
    return pl.pallas_call(
        last_kernel,
        out_shape=(taps, taps, *[shape((1, SLICE), F32)] * 6, *[shape(r.shape, r.dtype) for r in rows]),
        in_specs=[hbm] * 4 + [vmem] * 5,
        out_specs=(hbm, hbm, *[vmem] * 10),
        scratch_shapes=[
            pltpu.VMEM(act.shape, BF16),
            pltpu.VMEM(wide_one.shape, BF16),
            pltpu.VMEM(wide_two.shape, BF16),
            pltpu.VMEM(taps.shape, F32),
            pltpu.VMEM(taps.shape, F32),
            pltpu.SemaphoreType.DMA((2 * FRAMES + 1,)),
            pltpu.SemaphoreType.DMA((16,)),
        ],
        compiler_params=pltpu.CompilerParams(vmem_limit_bytes=60 * 1024 * 1024),
        cost_estimate=pl.CostEstimate(flops=14 * 10**9, bytes_accessed=35 * 10**6, transcendentals=0),
        name="last",
    )(act, wide_one, wide_two, exit_grad, smalls, *rows)


def local(
    first_input,
    second_input,
    first_cotangent,
    second_cotangent,
    entry_gain,
    entry_shift,
    entry_kernel,
    entry_bias,
    exit_gain,
    exit_shift,
    exit_kernel,
    exit_bias,
):
    def rows(values):
        return values.reshape(values.shape[0], OWN, CHANNELS)

    vectors = [
        v.reshape(1, SLICE) for v in (entry_gain, entry_shift, entry_bias, exit_gain, exit_shift, exit_bias)
    ]
    taps = [k.reshape(9, 3, CHANNELS, SLICE) for k in (entry_kernel, exit_kernel)]
    *home, smalls, act_one, wide_one, wide_two, exit_grad = run_block(
        [
            rows(first_input),
            rows(second_input),
            rows(first_cotangent),
            rows(second_cotangent),
            *vectors,
            *taps,
        ]
    )
    entry_grad, exit_grad, *rest = run_last(act_one, wide_one, wide_two, smalls, home, exit_grad)
    small, (out_one, out_two, back_one, back_two) = rest[:6], rest[6:]
    totals = (*small, entry_grad, exit_grad)
    groups = lax.axis_size("wide") // BANDS
    if groups > 1:
        totals = tuple(lax.psum(t, "wide") / BANDS for t in totals)
    *small, entry_grad, exit_grad = totals
    small = [t.reshape(SLICE) for t in small]
    return (
        out_one.reshape(first_input.shape),
        out_two.reshape(second_input.shape),
        back_one.reshape(first_input.shape),
        back_two.reshape(second_input.shape),
        small[0],
        small[1],
        entry_grad,
        small[2],
        small[3],
        small[4],
        exit_grad,
        small[5],
    )


def solution(mesh):
    banded = P(None, ("wide", "narrow"), None, None)
    vector = P("narrow")
    kernel = P(None, None, "narrow")
    return jax.shard_map(
        local,
        mesh=mesh,
        in_specs=(banded,) * 4 + (vector, vector, kernel, vector) * 2,
        out_specs=(banded,) * 4 + (vector, vector, kernel, vector) * 2,
        check_vma=False,
    )
```

```python
import functools

import jax
import jax.numpy as jnp
from jax import lax
from jax.experimental import pallas as pl
from jax.experimental.pallas import tpu as pltpu
from jax.sharding import PartitionSpec as P

GROUPS = 32
HEIGHT_ONE = 32
HEIGHT_TWO = 16
CHANNELS = 512
NARROW = 4
BANDS = 8
SLICE = 128
FRAMES = 5
FIRST = 3
BAND = 128
OWN = 32
LONG = 192

EPS = 1e-06
F32 = jnp.float32
BF16 = jnp.bfloat16
MESH = pl.DeviceIdType.MESH

FORWARD = {
    1: ((0, 3, 0), (3, 5, 3)),
    0: ((0, 2, 1), (3, 4, 4)),
    2: ((1, 3, 0), (4, 5, 3)),
}
BACKWARD = {
    1: ((0, 3, 0), (3, 5, 3)),
    0: ((1, 3, 0), (4, 5, 3)),
    2: ((0, 2, 1), (3, 4, 4)),
}


TWO = {"x": True, "a2": False}
ORDER = (
    "prep",
    "st0",
    "xsend",
    "xh1",
    "gown",
    "gstart",
    "T2",
    "T2b",
    "z g 1",
    "xh2",
    "xown",
    "act",
    "xbulk",
    "T2c",
    "C1",
    "C1b",
    "C1c",
    "z g 2",
    "rs0",
    "S2",
    "a2start",
    "gh2",
    "padg 0",
    "y a2 0",
    "a2own",
    "S3",
    "padg 1",
    "padg 2",
    "z a2 1",
    "T1",
    "mstart",
    "o a2 0 1",
    "T1b",
    "T1c",
    "y a2 1",
    "prepa 0",
    "z a2 2",
    "wx 0 0 0",
    "wx 0 0 1",
    "wx 0 0 2",
    "o a2 1 0",
    "z g 3",
    "z x 1",
    "wx 0 0 3",
    "wx 0 0 4",
    "wx 0 1 0",
    "wx 0 1 1",
    "wx 0 1 2",
    "wx 0 1 3",
    "wx 0 1 4",
    "wx 0 2 0",
    "wx 0 2 1",
    "wx 0 2 2",
    "padm 0",
    "o a2 1 1",
    "y a2 2",
    "wx 0 2 3",
    "wx 0 2 4",
    "z a2 3",
    "prepa 1",
    "wx 1 0 0",
    "wx 1 0 1",
    "wx 1 0 2",
    "wx 1 0 3",
    "z m 1",
    "wx 1 0 4",
    "padg 3",
    "wx 1 1 0",
    "rt",
    "wx 1 1 1",
    "wx 1 1 2",
    "o a2 2 0",
    "wx 1 1 3",
    "wx 1 1 4",
    "wx 1 2 0",
    "z x 2",
    "wx 1 2 1",
    "wx 1 2 2",
    "o a2 2 1",
    "y a2 3",
    "prepa 2",
    "y x 0",
    "C2",
    "wx 1 2 3",
    "wx 1 2 4",
    "wx 2 0 0",
    "y x 1",
    "wx 2 0 1",
    "wx 2 0 2",
    "o a2 3 0",
    "wx 2 0 3",
    "wx 2 0 4",
    "wx 2 1 0",
    "wx 2 1 1",
    "wx 2 1 2",
    "z x 3",
    "gh1",
    "o a2 3 1",
    "wx 2 1 3",
    "C2b",
    "z m 2",
    "prepa 3",
    "y x 2",
    "o x 0 1",
    "wx 2 1 4",
    "padm 1",
    "wx 2 2 0",
    "wx 2 2 1",
    "wx 2 2 2",
    "wx 2 2 3",
    "wx 2 2 4",
    "wx 3 0 0",
    "y x 3",
    "wx 3 0 1",
    "wx 3 0 2",
    "o x 1 1",
    "wx 3 0 3",
    "z m 3",
    "wx 3 0 4",
    "S4",
    "C2c",
    "prepx 0",
    "prepx 1",
    "o x 2 1",
    "wx 3 1 0",
    "wx 3 1 1",
    "o x 3 1",
    "wx 3 1 2",
    "wx 3 1 3",
    "wx 3 1 4",
    "wx 3 2 0",
    "prepx 2",
    "prepx 3",
    "wx 3 2 1",
    "wx 3 2 2",
    "wx 3 2 3",
    "wx 3 2 4",
    "padm 2",
    "padm 3",
    "S5",
    "out",
    "fin",
)
REAPS = (47, 71, 94, 118, 136)


def sigmoid_of(values):
    return 0.5 * jnp.tanh(0.5 * values) + 0.5


def group_sum(tile):
    lanes = lax.broadcasted_iota(jnp.int32, tile.shape, 1)
    for step in (1, 2, 4, 8):
        up = pltpu.roll(tile, step, 1)
        down = pltpu.roll(tile, SLICE - step, 1)
        tile = tile + jnp.where((lanes & step) != 0, up, down)
    return tile


def column_ids(rows, width):
    return lax.broadcasted_iota(jnp.int32, (rows, SLICE), 0) % width


def shifted(values, width, k):
    if k == 1:
        return values
    rows = values.shape[0]
    cols = column_ids(rows, width)
    if k == 0:
        return jnp.where(cols == width - 1, 0.0, pltpu.roll(values, rows - 1, 0))
    return jnp.where(cols == 0, 0.0, pltpu.roll(values, 1, 0))


def three_shifts(values, width):
    wide = values.astype(F32)
    return jnp.concatenate([shifted(wide, width, k).astype(BF16) for k in range(3)], axis=1)


def taken(ref, spans, start_one, start_two):
    (a, b, _), (c, d, _) = spans
    one = ref[a:b, start_one : start_one + BAND, :]
    two = ref[c:d, start_two : start_two + BAND, :]
    lanes = ref.shape[2]
    return jnp.concatenate(
        [one.reshape((b - a) * BAND, lanes), two.reshape((d - c) * BAND, lanes)], axis=0
    )


def spread(out, spans, result, fresh):
    (a, b, o), (c, d, p) = spans
    cut = (b - a) * BAND
    one = result[:cut].reshape(b - a, BAND, -1)
    two = result[cut:].reshape(d - c, BAND, -1)
    if fresh:
        out[o : o + b - a] = one
        out[p : p + d - c] = two
    else:
        out[o : o + b - a] += one
        out[p : p + d - c] += two


PARTS = (1, 0, 2)


def conv_forward(act, weights, sums, part):
    i = PARTS[part]
    spans = FORWARD[i]
    rows = jnp.concatenate([taken(act, spans, 32 * j, 16 + 16 * j) for j in range(3)], axis=1)
    taps = weights[3 * i : 3 * i + 3].reshape(3 * CHANNELS, 3 * SLICE)
    spread(sums, spans, jnp.dot(rows, taps, preferred_element_type=F32), part == 0)


def conv_columns(sums, frame, width):
    total = sums[frame, :, SLICE : 2 * SLICE]
    total = total + shifted(sums[frame, :, 0:SLICE], width, 2)
    return total + shifted(sums[frame, :, 2 * SLICE : 3 * SLICE], width, 0)


def conv_backward(grads, weights, sums, part):
    i = PARTS[part]
    spans = BACKWARD[i]
    rows = jnp.concatenate(
        [taken(grads, spans, 64 - 32 * j, 48 - 16 * j) for j in range(3)], axis=1
    )
    taps = jnp.concatenate([weights[3 * i + j] for j in range(3)], axis=1)
    result = lax.dot_general(rows, taps, (((1,), (1,)), ((), ())), preferred_element_type=F32)
    spread(sums, spans, result, part == 0)


def moments(values):
    total = jnp.sum(values, axis=0, keepdims=True)
    off = values - total / values.shape[0]
    return total, jnp.sum(off * off, axis=0, keepdims=True)


def merge(totals, squares, count):
    total = functools.reduce(jnp.add, totals)
    mean = total / (count * len(totals))
    square = functools.reduce(jnp.add, squares)
    for part in totals:
        off = part / count - mean
        square = square + count * off * off
    return total, square


def group_merge(total, square, count):
    mean = total / count
    group_total = group_sum(total)
    off = mean - group_total / (16 * count)
    return group_total, group_sum(square + count * off * off)


def long_row(tile, row):
    return jnp.concatenate([tile[row + k : row + k + 1, :] for k in range(NARROW)], axis=1)


def lanes_of(m):
    if isinstance(m, int):
        return pl.ds(m * SLICE, SLICE)
    return pl.ds(pl.multiple_of(m * SLICE, SLICE), SLICE)


def place_of(k):
    return k % 2 * 2 + k // 2


def store_taps(out, taps, result, fresh):
    for number, tap in enumerate(taps):
        for k in range(NARROW):
            start = place_of(k) * SLICE
            piece = result[start : start + SLICE, number * SLICE : (number + 1) * SLICE]
            rows = slice(k * SLICE, (k + 1) * SLICE)
            if fresh:
                out[tap, rows, :] = piece
            else:
                out[tap, rows, :] += piece


def rows_of(m, offset=0):
    return pl.ds(pl.multiple_of(offset + m * OWN, OWN), OWN)


def clear_pads(three_one, three_two):
    for start in (0, three_one.shape[1] - 32):
        three_one[:, start : start + 32, :] = jnp.zeros((FIRST, 32, 3 * SLICE), BF16)
    for start in (0, three_two.shape[2] - 16):
        three_two[:, :, start : start + 16, :] = jnp.zeros((FRAMES - FIRST, 4, 16, 3 * SLICE), BF16)


def pad_pair(grad_ref, three_one, three_two, pair):
    @pl.loop(0, 2)
    def _(half):
        first = pl.multiple_of(half * BAND, BAND)

        @pl.loop(0, FIRST)
        def _(f):
            start = pl.multiple_of(32 + pair * 2 * BAND + first, 32)
            three_one[f, pl.ds(start, BAND), :] = three_shifts(grad_ref[2 * pair + half, f], 32)

        @pl.loop(0, FRAMES - FIRST)
        def _(f):
            start = pl.multiple_of(16 + first, 16)
            three_two[f, pair, pl.ds(start, BAND), :] = three_shifts(grad_ref[2 * pair + half, FIRST + f], 16)


PAIRS = {
    0: ((0, 1), (1, 2), (3, 4)),
    1: ((0, 0), (1, 1), (2, 2), (3, 3), (4, 4)),
    2: ((1, 0), (2, 1), (4, 3)),
}
TAP_GROUPS = ((0, 1), (2, 3), (4, 5), (6, 7), (8,))


def tap_rows(three_one, three_two, t, tap):
    j, k = tap // 3, tap % 3
    cut = slice(k * SLICE, (k + 1) * SLICE)
    if t < FIRST:
        return three_one[t, (2 - j) * 32 : (2 - j) * 32 + 1024, cut]
    return three_two[t - FIRST, :, (2 - j) * 16 : (2 - j) * 16 + 256, cut].reshape(1024, SLICE)


def weight_terms(act_t, three_one, three_two, i, pairs, group, out, fresh):
    left = jnp.concatenate([act_t[c, s] for s, _ in pairs for c in range(BANDS)], axis=1)
    right = jnp.concatenate(
        [
            jnp.concatenate([tap_rows(three_one, three_two, t, tap) for tap in group], axis=1)
            for _, t in pairs
        ],
        axis=0,
    )
    result = jnp.dot(left, right, preferred_element_type=F32)
    store_taps(out, [9 * i + tap for tap in group], result, fresh)


def pair_weight_terms(act_t, three_one, three_two, pair, i, group, out, fresh):
    def rows(t, tap):
        j, cut = tap // 3, slice(tap % 3 * SLICE, (tap % 3 + 1) * SLICE)
        if t < FIRST:
            start = pl.multiple_of((2 - j) * 32 + pair * 2 * BAND, 32)
            return three_one[t, pl.ds(start, 2 * BAND), cut]
        return three_two[t - FIRST, pair, (2 - j) * 16 : (2 - j) * 16 + 2 * BAND, cut]

    left = jnp.concatenate([act_t[2 * pair + half, s] for s, _ in PAIRS[i] for half in range(2)], axis=1)
    right = jnp.concatenate(
        [jnp.concatenate([rows(t, tap) for tap in group], axis=1) for _, t in PAIRS[i]], axis=0
    )
    result = jnp.dot(left, right, preferred_element_type=F32)
    store_taps(out, [9 * i + tap for tap in group], result, fresh)


def block_kernel(
    x_one, x_two, g_one, g_two, gain_one, shift_one, bias_one, gain_two, shift_two, bias_two,
    entry_hbm, exit_hbm,
    out_one, out_two, back_one, back_two, smalls, act_out, wide_one_out, wide_two_out, exit_grad,
    act_t1, act_t2, g_all, gm_all, three_one, three_two, wide_one, wide_two, exit_sum,
    entry_w, exit_w, own_x, own_g, band_x, band_a, long_g, long_m, params,
    stat_a, stat_b, stat_c, stat_d, stat_e, stat_f, few,
    sums, partial, grad_three, mid, grad_two, grad_one, part_send, part_recv, tail_send, tail_recv, out_send,
    w_sem, send_sem, x_sem, g_sem, p_sem, halo_sem, stat_sem, ga_sem, gm_sem, a1_sem, a2_sem, rs_sem, o_sem, store_sem,
):
    w = lax.axis_index("wide")
    n = lax.axis_index("narrow")
    base = w // BANDS * BANDS
    b = w - base
    z, y = b // 2, b % 2
    has_up, has_down = b > 0, b < BANDS - 1
    pair_up, pair_down = y == 1, y == 0
    flags = lambda f: (has_up, has_down) if f < FIRST else (pair_up, pair_down)
    width_of = lambda f: 32 if f < FIRST else 16
    sub_of = lambda f: 0 if f < FIRST else 1

    sends = []
    used = [0]

    def both(first, second):
        if first is None or second is None:
            return second if first is None else first
        return jnp.logical_and(first, second)

    def under(flag, act):
        if flag is None:
            act()
        else:
            pl.when(flag)(act)

    def make(src, dst, recv, device):
        used[0] += 1
        return pltpu.make_async_remote_copy(
            src_ref=src,
            dst_ref=dst,
            send_sem=send_sem.at[used[0] - 1],
            recv_sem=recv,
            device_id=device,
            device_id_type=MESH,
        )

    def start(copies):
        for copy in copies:
            copy.start()

    def launch(copies, flag=None):
        under(flag, lambda: start(copies))
        sends.append((flag, copies))

    def send(src, dst, recv, device, flag=None):
        launch([make(src, dst, recv, device)], flag)

    def reap(count):
        for flag, copies in sends[:count]:

            def wait_all(copies=copies):
                for copy in copies:
                    copy.wait_send()

            under(flag, wait_all)
        del sends[:count]

    def arrived(dst, recv, flag=None):
        wait = pltpu.make_async_remote_copy(
            src_ref=dst,
            dst_ref=dst,
            send_sem=send_sem.at[0],
            recv_sem=recv,
            device_id=(w, n),
            device_id_type=MESH,
        ).wait_recv
        under(flag, wait)

    def beside(m):
        return (w, m)

    def band_of(c):
        return (base + c, n)

    others = [lax.rem(n + d, NARROW) for d in (1, 2, 3)]
    far = [lax.rem(b + d, BANDS) for d in range(1, BANDS)]
    sib, opp, cross = n ^ 1, n ^ 2, n ^ 3
    beyond = b + 1 - 2 * y
    slant = b - 1 + 2 * y
    above = lax.rem(b + BANDS - 1, BANDS)
    below = lax.rem(b + 1, BANDS)
    up_chip = lax.rem(b + BANDS - 2, BANDS)
    down_chip = lax.rem(b + 2, BANDS)
    pairs_by_distance = [z, z + 1 - 2 * (z % 2), 2 - z // 2, 3 - 3 * (z // 2)]
    mine, mine_long = rows_of(n), rows_of(n, 32)

    sem_of = {"x": a1_sem, "a2": a2_sem, "g": ga_sem, "m": gm_sem}
    array_of = {"x": act_t1, "a2": act_t2, "g": g_all, "m": gm_all}

    def block(name, c, k):
        if name in ("g", "m"):
            return array_of[name].at[c]
        return array_of[name].at[c, :, lanes_of(place_of(k)), :]

    def couple(name, c, k):
        rows = pl.ds(pl.multiple_of(k % 2 * 2 * SLICE, 2 * SLICE), 2 * SLICE)
        return array_of[name].at[c, :, rows, :]

    def sem(name, c, kind):
        return sem_of[name].at[c] if name in ("g", "m") else sem_of[name].at[c, kind]

    def own(name, c):
        return couple(name, c, n) if TWO.get(name) else block(name, c, n)

    def to(ref, name, c, kind, device):
        return make(ref, ref, sem(name, c, kind), device)

    def to_opp(name, c):
        return to(block(name, c, n), name, c, 1, beside(opp))

    def to_sib(name, c):
        return to(couple(name, c, n), name, c, 2, beside(sib))

    def to_beyond(name, c):
        return to(block(name, c, n), name, c, 0, band_of(beyond))

    def at_distance(step, line):
        for sign in (-1, 1) if step else (1,):
            there = None if step == 0 else (z >= step if sign < 0 else z + step <= 3)
            c = lax.rem(b + 2 * sign * step + BANDS, BANDS)
            yield sign, there, c if line == 0 else c + 1 - 2 * y

    def z_step(name, step):
        for sign, there, c in at_distance(step, 0):
            arrived(own(name, c), sem(name, c, 0), there)
            copies = [to_beyond(name, c)]
            if name in ("x", "a2"):
                copies.append(to_sib(name, c) if TWO[name] else to_opp(name, c))
            if step < 3:
                onward, target = (z < 3, down_chip) if sign < 0 else (z > 0, up_chip)
                launch([to(own(name, c), name, c, 0, band_of(target))], both(there, onward))
            launch(copies, there)

    def y_step(name, step):
        for _, there, c in at_distance(step, 1):
            arrived(block(name, c, n), sem(name, c, 0), there)
            launch([to_opp(name, c)], there)

    def o_step(name, step, line):
        for _, there, c in at_distance(step, line):
            arrived(block(name, c, opp), sem(name, c, 1), there)
            launch([to_sib(name, c)], there)

    def begin(name):
        launch([to(own(name, b), name, b, 0, band_of(down_chip))], z < 3)
        launch([to(own(name, b), name, b, 0, band_of(up_chip))], z > 0)
        launch([to_beyond(name, b)])

    def await_sib(name, c):
        arrived(couple(name, c, sib), sem(name, c, 2))

    def to_bands(stat, number):
        for c in far:
            send(stat.at[b], stat.at[b], stat_sem.at[number, b], band_of(c))

    def from_bands(stat, number):
        for c in far:
            arrived(stat.at[b], stat_sem.at[number, c])

    def to_narrow(stat, number):
        for m in others:
            send(stat.at[n], stat.at[n], stat_sem.at[number, n], beside(m))

    def from_narrow(stat, number):
        for m in others:
            arrived(stat.at[n], stat_sem.at[number, m])

    def exchange_rims(ref, first_sem):
        send(ref.at[0:3, 128:160, :], ref.at[0:3, 0:32, :], halo_sem.at[first_sem], band_of(below), has_down)
        send(ref.at[0:3, 32:64, :], ref.at[0:3, 160:192, :], halo_sem.at[first_sem + 1], band_of(above), has_up)
        send(ref.at[3:5, 144:160, :], ref.at[3:5, 16:32, :], halo_sem.at[first_sem + 2], band_of(beyond), pair_down)
        send(ref.at[3:5, 32:48, :], ref.at[3:5, 160:176, :], halo_sem.at[first_sem + 3], band_of(beyond), pair_up)

    def await_rims(ref, first_sem):
        arrived(ref.at[0:3, 0:32, :], halo_sem.at[first_sem], has_up)
        arrived(ref.at[0:3, 160:192, :], halo_sem.at[first_sem + 1], has_down)
        arrived(ref.at[3:5, 16:32, :], halo_sem.at[first_sem + 2], pair_up)
        arrived(ref.at[3:5, 160:176, :], halo_sem.at[first_sem + 3], pair_down)

    stores = []

    def store(source, target, number):
        copy = pltpu.make_async_copy(source, target, store_sem.at[number])
        copy.start()
        stores.append(copy)

    kept = {}
    count_one = 3 * BAND * BANDS
    count_two = 2 * BAND * 2

    def prep():
        loads = []
        for number, (source, target) in enumerate(((exit_hbm, exit_w), (entry_hbm, entry_w))):
            for k in range(3):
                load = pltpu.make_async_copy(
                    source.at[:, k],
                    target.at[:, :, k * SLICE : (k + 1) * SLICE],
                    w_sem.at[number, k],
                )
                load.start()
                loads.append(load)
        kept["loads"] = loads
        own_x[0:FIRST] = x_one[...]
        own_x[FIRST:FRAMES] = x_two[...]
        own_g[0:FIRST] = g_one[...]
        own_g[FIRST:FRAMES] = g_two[...]
        for ref in (params, stat_c, stat_d, stat_f, smalls):
            ref[...] = jnp.zeros_like(ref)
        for ref in (band_x, long_g, long_m):
            for start in (0, 160):
                ref[:, start : start + 32, :] = jnp.zeros((FRAMES, 32, ref.shape[2]), BF16)
        for row, ref in enumerate((gain_one, shift_one, bias_one, gain_two, shift_two, bias_two)):
            params[n, row : row + 1, :] = ref[...].astype(F32)
        band_x[:, mine_long, :] = own_x[...]
        long_g[:, mine_long, :] = own_g[:, :, lanes_of(n)]

        barrier = pltpu.get_barrier_semaphore()
        for m in others:
            pl.semaphore_signal(barrier, inc=1, device_id=beside(m), device_id_type=MESH)
        for c in far:
            pl.semaphore_signal(barrier, inc=1, device_id=band_of(c), device_id_type=MESH)
        for sub, (start, stop) in enumerate(((0, FIRST), (FIRST, FRAMES))):
            values = own_x[start:stop].astype(F32).reshape((stop - start) * OWN, CHANNELS)
            total, square = moments(values)
            cuts = [slice(k * SLICE, (k + 1) * SLICE) for k in range(NARROW)]
            t, s = group_merge(
                jnp.concatenate([total[:, cut] for cut in cuts], axis=0),
                jnp.concatenate([square[:, cut] for cut in cuts], axis=0),
                float(values.shape[0]),
            )
            stat_a[n, 8 * sub : 8 * sub + 4, :] = t
            stat_a[n, 8 * sub + 4 : 8 * sub + 8, :] = s
        pl.semaphore_wait(barrier, NARROW - 1 + BANDS - 1)
        to_narrow(stat_a, 0)
        rims_out()
        for m in others:
            send(own_g.at[:, :, lanes_of(m)], long_g.at[:, mine_long, :], g_sem.at[n], beside(m))
            send(params.at[n], params.at[n], p_sem.at[n], beside(m))
        clear_pads(wide_one, wide_two)
        clear_pads(three_one, three_two)

    def xsend():
        for number, start in enumerate((0, three_one.shape[1] - 32)):
            rows = slice(start, start + 32)
            store(three_one.at[:, rows, :], wide_one_out.at[:, rows, :], 12 + number)
        for m in (opp, sib):
            send(own_x, band_x.at[:, mine_long, :], x_sem.at[n], beside(m))

    def st0():
        from_narrow(stat_a, 0)
        for sub, count in ((0, 3 * OWN * 16.0), (1, 2 * OWN * 16.0)):
            t, s = merge(
                [stat_a[m, 8 * sub : 8 * sub + 4, :] for m in range(NARROW)],
                [stat_a[m, 8 * sub + 4 : 8 * sub + 8, :] for m in range(NARROW)],
                count,
            )
            stat_b[b, 8 * sub : 8 * sub + 4, :] = t
            stat_b[b, 8 * sub + 4 : 8 * sub + 8, :] = s
        to_bands(stat_b, 1)

    def gown():
        for m in others:
            arrived(long_g.at[:, mine_long, :], g_sem.at[m])
        exchange_rims(long_g, 4)
        g_all[b] = long_g[:, 32:160, :]

    def rim_parts():
        return (
            (band_x.at[0:3, 0:32, :], 0, own_x.at[0:3], below, has_down, has_up, 3),
            (band_x.at[3:5, 16:32, :], 2, own_x.at[3:5, 16:32, :], beyond, pair_down, pair_up, 3),
            (band_x.at[0:3, 160:192, :], 1, own_x.at[0:3], above, has_up, has_down, 0),
            (band_x.at[3:5, 160:176, :], 3, own_x.at[3:5, 0:16, :], beyond, pair_up, pair_down, 0),
        )

    def rims_out():
        for ref, number, own, target, gives, _, owner in rim_parts():
            send(own, ref, halo_sem.at[number], band_of(target), both(gives, n == owner))

    def xh1():
        for ref, number, _, _, _, takes, owner in rim_parts():
            flag = both(takes, n == owner)
            arrived(ref, halo_sem.at[number], flag)
            send(ref, ref, halo_sem.at[number], beside(opp), flag)
            send(ref, ref, halo_sem.at[number], beside(sib), flag)

    def xh2():
        for ref, number, _, _, _, takes, owner in rim_parts():
            flag = both(takes, n == (owner + 2) % 4)
            arrived(ref, halo_sem.at[number], flag)
            send(ref, ref, halo_sem.at[number], beside(sib), flag)

    def xh3():
        for ref, number, _, _, _, takes, owner in rim_parts():
            arrived(ref, halo_sem.at[number], both(takes, n % 2 != owner % 2))

    def xown():
        arrived(band_x.at[:, mine_long, :], x_sem.at[opp])
        theirs = band_x.at[:, rows_of(opp, 32), :]
        send(theirs, theirs, x_sem.at[opp], beside(sib))
        arrived(band_x.at[:, mine_long, :], x_sem.at[sib])
        arrived(band_x.at[:, mine_long, :], x_sem.at[cross])

    def first_hidden(values, sub):
        normed = (values - kept["mean_one"][sub]) * kept["inv_one"][sub]
        return normed, normed * kept["gain_long"] + kept["shift_long"]

    def first_active(f, start, stop):
        _, hidden = first_hidden(band_x[f, start:stop].astype(F32), sub_of(f))
        return (hidden * sigmoid_of(hidden)).astype(BF16)

    def act():
        for m in others:
            arrived(params.at[n], p_sem.at[m])
        from_bands(stat_b, 1)
        one_total, one_square = merge(
            [stat_b[c, 0:4, :] for c in range(BANDS)],
            [stat_b[c, 4:8, :] for c in range(BANDS)],
            3 * BAND * 16.0,
        )
        two_total, two_square = merge(
            [stat_b[b, 8:12, :], stat_b[beyond, 8:12, :]],
            [stat_b[b, 12:16, :], stat_b[beyond, 12:16, :]],
            2 * BAND * 16.0,
        )
        kept["mean_one"] = [
            long_row(one_total / (16.0 * count_one), 0),
            long_row(two_total / (16.0 * count_two), 0),
        ]
        kept["inv_one"] = [
            long_row(lax.rsqrt(one_square / (16.0 * count_one) + EPS), 0),
            long_row(lax.rsqrt(two_square / (16.0 * count_two) + EPS), 0),
        ]
        kept["gain_long"] = jnp.concatenate([params[m, 0:1, :] for m in range(NARROW)], axis=1)
        kept["shift_long"] = jnp.concatenate([params[m, 1:2, :] for m in range(NARROW)], axis=1)
        for f in range(FRAMES):
            active = first_active(f, 32, 160)
            band_a[f, 32:160, :] = active
            for k in range(NARROW):
                cut = slice(k * SLICE, (k + 1) * SLICE)
                act_t1[b, f, lanes_of(place_of(k)), :] = active[:, cut].T

    def lay_out(long):
        for f in range(FRAMES):
            grad_three[f] = three_shifts(long[f], width_of(f))

    def t2():
        await_rims(long_g, 4)
        lay_out(long_g)
        for load in kept["loads"][:3]:
            load.wait()
        conv_backward(grad_three, exit_w, partial, 0)

    def t2c():
        conv_backward(grad_three, exit_w, partial, 2)
        part_send[0] = partial[:, :, lanes_of(sib)].astype(BF16)
        part_send[1] = partial[:, :, lanes_of(cross)].astype(BF16)
        for k in range(2):
            send(part_send.at[k], part_recv.at[k], rs_sem.at[0, k], beside(sib))

    def rs0():
        for k in range(2):
            arrived(part_recv.at[k], rs_sem.at[0, k])
        part_send[2] = (partial[:, :, lanes_of(opp)] + part_recv[1].astype(F32)).astype(BF16)
        send(part_send.at[2], part_recv.at[2], rs_sem.at[0, 2], beside(opp))

    def c1():
        xh3()
        for f in range(FRAMES):
            width = width_of(f)
            up, down = flags(f)
            row = first_active(f, 32 - width, 32)
            band_a[f, 32 - width : 32, :] = jnp.where(up, row, jnp.zeros_like(row))
            row = first_active(f, 160, 160 + width)
            band_a[f, 160 : 160 + width, :] = jnp.where(down, row, jnp.zeros_like(row))
        for load in kept["loads"][3:]:
            load.wait()
        conv_forward(band_a, entry_w, sums, 0)

    def c1c():
        conv_forward(band_a, entry_w, sums, 2)
        for f in range(FRAMES):
            mid[f] = conv_columns(sums, f, width_of(f)) + params[n, 2:3, :]
        for sub, (start, stop) in enumerate(((0, FIRST), (FIRST, FRAMES))):
            values = mid[start:stop].reshape((stop - start) * BAND, SLICE)
            total, square = moments(values)
            t, s = group_merge(total, square, float(values.shape[0]))
            stat_c[b, 2 * sub : 2 * sub + 1, :] = t
            stat_c[b, 2 * sub + 1 : 2 * sub + 2, :] = s
        to_bands(stat_c, 2)

    def s2():
        from_bands(stat_c, 2)
        one_total, one_square = merge(
            [stat_c[c, 0:1, :] for c in range(BANDS)],
            [stat_c[c, 1:2, :] for c in range(BANDS)],
            3 * BAND * 16.0,
        )
        two_total, two_square = merge(
            [stat_c[b, 2:3, :], stat_c[beyond, 2:3, :]],
            [stat_c[b, 3:4, :], stat_c[beyond, 3:4, :]],
            2 * BAND * 16.0,
        )
        mean_two = [one_total / (16.0 * count_one), two_total / (16.0 * count_two)]
        kept["inv_two"] = [
            lax.rsqrt(one_square / (16.0 * count_one) + EPS),
            lax.rsqrt(two_square / (16.0 * count_two) + EPS),
        ]
        kept["gain_own"], kept["shift_own"] = params[n, 3:4, :], params[n, 4:5, :]
        for f in range(FRAMES):
            normed = (mid[f] - mean_two[sub_of(f)]) * kept["inv_two"][sub_of(f)]
            mid[f] = normed
            hidden = normed * kept["gain_own"] + kept["shift_own"]
            act_t2[b, f, lanes_of(place_of(n)), :] = (hidden * sigmoid_of(hidden)).astype(BF16).T

    def gh2():
        arrived(part_recv.at[2], rs_sem.at[0, 2])
        rows_sum = [[0.0, 0.0], [0.0, 0.0]]
        for f in range(FRAMES):
            sub = sub_of(f)
            grad = partial[f, :, lanes_of(n)] + part_recv[0, f].astype(F32) + part_recv[2, f].astype(F32)
            hidden = mid[f] * kept["gain_own"] + kept["shift_own"]
            sigmoid = sigmoid_of(hidden)
            grad = grad * (sigmoid * (1.0 + hidden * (1.0 - sigmoid)))
            grad_two[f] = grad
            rows_sum[sub][0] += jnp.sum(grad, axis=0, keepdims=True)
            rows_sum[sub][1] += jnp.sum(grad * mid[f], axis=0, keepdims=True)
        for sub in range(2):
            stat_d[b, 2 * sub : 2 * sub + 1, :] = rows_sum[sub][0]
            stat_d[b, 2 * sub + 1 : 2 * sub + 2, :] = rows_sum[sub][1]
        own = g_all[b].astype(F32).reshape(FRAMES * BAND, SLICE)
        stat_d[b, 4:5, :] = jnp.sum(own, axis=0, keepdims=True)
        to_bands(stat_d, 3)

    def a2start():
        begin("a2")
        launch([to_opp("a2", b)])

    def a2own():
        o_step("a2", 0, 0)

    def s3():
        from_bands(stat_d, 3)
        gain_own = kept["gain_own"]
        all_rows = [
            functools.reduce(jnp.add, [stat_d[c, r : r + 1, :] for c in range(BANDS)]) for r in range(5)
        ]
        smalls[3:4, :] = all_rows[1] + all_rows[3]
        smalls[4:5, :] = all_rows[0] + all_rows[2]
        smalls[5:6, :] = all_rows[4]
        pair_rows = [stat_d[b, r : r + 1, :] + stat_d[beyond, r : r + 1, :] for r in range(4)]
        p_two = [
            group_sum(gain_own * all_rows[0]) / (16.0 * count_one),
            group_sum(gain_own * pair_rows[2]) / (16.0 * count_two),
        ]
        q_two = [
            group_sum(gain_own * all_rows[1]) / (16.0 * count_one),
            group_sum(gain_own * pair_rows[3]) / (16.0 * count_two),
        ]
        bias_sum = 0.0
        for f in range(FRAMES):
            sub = sub_of(f)
            grad = (grad_two[f] * gain_own - p_two[sub] - mid[f] * q_two[sub]) * kept["inv_two"][sub]
            grad = grad.astype(BF16)
            gm_all[b, f] = grad
            long_m[f, 32:160, :] = grad
            bias_sum = bias_sum + jnp.sum(grad.astype(F32), axis=0, keepdims=True)
        stat_f[b, 16:17, :] = bias_sum
        exchange_rims(long_m, 8)

    def t1():
        await_rims(long_m, 8)
        lay_out(long_m)
        conv_backward(grad_three, entry_w, partial, 0)

    def t1c():
        conv_backward(grad_three, entry_w, partial, 2)
        tail_send[0] = partial[:, rows_of(sib), :].astype(BF16)
        tail_send[1] = partial[:, rows_of(cross), :].astype(BF16)
        for k in range(2):
            send(tail_send.at[k], tail_recv.at[k], rs_sem.at[1, k], beside(sib))

    def rt():
        for k in range(2):
            arrived(tail_recv.at[k], rs_sem.at[1, k])
        tail_send[2] = (partial[:, rows_of(opp), :] + tail_recv[1].astype(F32)).astype(BF16)
        send(tail_send.at[2], tail_recv.at[2], rs_sem.at[1, 2], beside(opp))

    def gh1():
        arrived(tail_recv.at[2], rs_sem.at[1, 2])
        for sub, (start, stop) in enumerate(((0, FIRST), (FIRST, FRAMES))):
            first_sum, second_sum = 0.0, 0.0
            for f in range(start, stop):
                grad = partial[f, mine, :] + tail_recv[0, f].astype(F32) + tail_recv[2, f].astype(F32)
                normed, hidden = first_hidden(own_x[f].astype(F32), sub)
                sigmoid = sigmoid_of(hidden)
                grad = grad * (sigmoid * (1.0 + hidden * (1.0 - sigmoid)))
                grad_one[f] = grad
                first_sum = first_sum + jnp.sum(grad, axis=0, keepdims=True)
                second_sum = second_sum + jnp.sum(grad * normed, axis=0, keepdims=True)
            for k in range(NARROW):
                cut = slice(k * SLICE, (k + 1) * SLICE)
                stat_e[n, 8 * sub + k : 8 * sub + k + 1, :] = first_sum[:, cut]
                stat_e[n, 8 * sub + 4 + k : 8 * sub + 5 + k, :] = second_sum[:, cut]
        to_narrow(stat_e, 4)

    def s4():
        from_narrow(stat_e, 4)
        stat_f[b, 0:16, :] = stat_e[0] + stat_e[1] + stat_e[2] + stat_e[3]
        to_bands(stat_f, 5)

    def s5():
        from_bands(stat_f, 5)
        all_sums = functools.reduce(jnp.add, [stat_f[c] for c in range(BANDS)])
        pair_sums = stat_f[b] + stat_f[beyond]
        few[0, 0:4, :] = all_sums[0:4] + all_sums[8:12]
        few[1, 0:4, :] = all_sums[4:8] + all_sums[12:16]
        smalls[0:1, :] = few[1, pl.ds(n, 1), :]
        smalls[1:2, :] = few[0, pl.ds(n, 1), :]
        smalls[2:3, :] = all_sums[16:17]
        gain_rows = jnp.concatenate([params[m, 0:1, :] for m in range(NARROW)], axis=0)
        p_one = [
            long_row(group_sum(gain_rows * all_sums[0:4]) / (16.0 * count_one), 0),
            long_row(group_sum(gain_rows * pair_sums[8:12]) / (16.0 * count_two), 0),
        ]
        q_one = [
            long_row(group_sum(gain_rows * all_sums[4:8]) / (16.0 * count_one), 0),
            long_row(group_sum(gain_rows * pair_sums[12:16]) / (16.0 * count_two), 0),
        ]
        for f in range(FRAMES):
            sub = sub_of(f)
            normed, _ = first_hidden(own_x[f].astype(F32), sub)
            grad = grad_one[f] * kept["gain_long"] - p_one[sub] - normed * q_one[sub]
            grad = (own_g[f].astype(F32) + grad * kept["inv_one"][sub]).astype(BF16)
            if sub == 0:
                back_one[f] = grad
            else:
                back_two[f - FIRST] = grad

    def prepa(number):
        first = 2 * pairs_by_distance[number]
        await_sib("a2", first)
        await_sib("a2", first + 1)

    def pad(name, number, array, one, two):
        pair = pairs_by_distance[number]
        c = 2 * pair + 1 - y
        arrived(block(name, c, n), sem(name, c, 0))
        pad_pair(array, one, two, pair)

    def padg(number):
        pad("g", number, g_all, wide_one, wide_two)

    def c2():
        @pl.loop(0, NARROW)
        def _(k):
            cut = lanes_of(k)
            rows = lanes_of(place_of(k))
            for f in range(FRAMES):
                width = width_of(f)
                up, down = flags(f)
                band_a[f, 32:160, cut] = act_t2[b, f, rows, :].T
                row = act_t2[b - (b + 7) // 8, f, rows, :].T[BAND - width : BAND]
                band_a[f, 32 - width : 32, cut] = jnp.where(up, row, jnp.zeros_like(row))
                row = act_t2[b + (14 - b) // 8, f, rows, :].T[0:width]
                band_a[f, 160 : 160 + width, cut] = jnp.where(down, row, jnp.zeros_like(row))

        conv_forward(band_a, exit_w, sums, 0)

    def c2c():
        conv_forward(band_a, exit_w, sums, 2)
        for f in range(FRAMES):
            total = conv_columns(sums, f, width_of(f)) + params[n, 5:6, :]
            total = total + band_x[f, 32:160, lanes_of(n)].astype(F32)
            out_send[f] = total.astype(BF16)
        for m in others:
            send(out_send.at[0:3, rows_of(m), :], out_one.at[:, :, lanes_of(n)], o_sem.at[0, n], beside(m))
            send(out_send.at[3:5, rows_of(m), :], out_two.at[:, :, lanes_of(n)], o_sem.at[1, n], beside(m))
        out_one[:, :, lanes_of(n)] = out_send[0:3, mine, :]
        out_two[:, :, lanes_of(n)] = out_send[3:5, mine, :]

    def out():
        for m in others:
            arrived(out_one.at[:, :, lanes_of(m)], o_sem.at[0, m])
            arrived(out_two.at[:, :, lanes_of(m)], o_sem.at[1, m])

    def wx(number, place, group):
        i = PARTS[place]
        taps = TAP_GROUPS[group]
        pair = pairs_by_distance[number]
        pair_weight_terms(act_t2, wide_one, wide_two, pair, i, taps, exit_sum, number == 0)
        if number == 3 and group == len(TAP_GROUPS) - 1:
            cut = slice(9 * i, 9 * i + 9)
            store(exit_sum.at[cut], exit_grad.at[cut], 14 + i)

    def prepx(number):
        first = 2 * pairs_by_distance[number]
        if number == 0:
            await_sib("x", beyond)
        else:
            await_sib("x", first)
            await_sib("x", first + 1)
        store(act_t1.at[pl.ds(first, 2)], act_out.at[pl.ds(first, 2)], number)

    def padm(number):
        pad("m", number, gm_all, three_one, three_two)
        pair = pairs_by_distance[number]
        rows = pl.ds(pl.multiple_of(32 + pair * 2 * BAND, 32), 2 * BAND)
        store(three_one.at[:, rows, :], wide_one_out.at[:, rows, :], 4 + number)
        store(three_two.at[:, pair], wide_two_out.at[:, pair], 8 + number)

    def fin():
        reap(len(sends))
        for copy in stores:
            copy.wait()

    backward = lambda weights, part: lambda: conv_backward(grad_three, weights, partial, part)
    forward = lambda weights, part: lambda: conv_forward(band_a, weights, sums, part)
    steps = {
        "prep": prep, "xsend": xsend, "st0": st0, "gown": gown, "xown": xown, "xh1": xh1, "xh2": xh2, "act": act,
        "T2": t2, "T2b": backward(exit_w, 1), "T2c": t2c, "rs0": rs0,
        "C1": c1, "C1b": forward(entry_w, 1), "C1c": c1c,
        "S2": s2, "gh2": gh2, "a2start": a2start, "a2own": a2own, "S3": s3,
        "T1": t1, "T1b": backward(entry_w, 1), "T1c": t1c, "rt": rt, "gh1": gh1, "S4": s4, "S5": s5,
        "C2": c2, "C2b": forward(exit_w, 1), "C2c": c2c, "out": out,
        "padg": padg, "padm": padm, "fin": fin,
        "gstart": lambda: begin("g"),
        "mstart": lambda: begin("m"),
        "xbulk": lambda: begin("x"),
        "z": z_step, "y": y_step, "o": o_step, "wx": wx, "prepx": prepx, "prepa": prepa,
    }
    before = 0
    for number, item in enumerate(ORDER):
        if number in REAPS:
            count, before = before, len(sends) - before
            reap(count)
        word, *rest = item.split()
        steps[word](*[int(r) if r.isdigit() else r for r in rest])


def run_block(args):
    vmem = pl.BlockSpec(memory_space=pltpu.VMEM)
    hbm = pl.BlockSpec(memory_space=pl.ANY)
    dma = pltpu.SemaphoreType.DMA
    shape = jax.ShapeDtypeStruct
    everyone = (BANDS, FRAMES, CHANNELS, BAND)
    wide_one = (FIRST, 34 * 32, 3 * SLICE)
    wide_two = (FRAMES - FIRST, 4, 18 * 16, 3 * SLICE)
    return pl.pallas_call(
        block_kernel,
        out_shape=(
            shape((FIRST, OWN, CHANNELS), BF16),
            shape((FRAMES - FIRST, OWN, CHANNELS), BF16),
            shape((FIRST, OWN, CHANNELS), BF16),
            shape((FRAMES - FIRST, OWN, CHANNELS), BF16),
            shape((8, SLICE), F32),
            shape(everyone, BF16),
            shape(wide_one, BF16),
            shape(wide_two, BF16),
            shape((27, CHANNELS, SLICE), F32),
        ),
        in_specs=[vmem] * 10 + [hbm] * 2,
        out_specs=(vmem,) * 5 + (hbm,) * 4,
        scratch_shapes=[
            pltpu.VMEM(everyone, BF16),
            pltpu.VMEM(everyone, BF16),
            pltpu.VMEM((BANDS, FRAMES, BAND, SLICE), BF16),
            pltpu.VMEM((BANDS, FRAMES, BAND, SLICE), BF16),
            pltpu.VMEM(wide_one, BF16),
            pltpu.VMEM(wide_two, BF16),
            pltpu.VMEM(wide_one, BF16),
            pltpu.VMEM(wide_two, BF16),
            pltpu.VMEM((27, CHANNELS, SLICE), F32),
            pltpu.VMEM((9, CHANNELS, 3 * SLICE), BF16),
            pltpu.VMEM((9, CHANNELS, 3 * SLICE), BF16),
            pltpu.VMEM((FRAMES, OWN, CHANNELS), BF16),
            pltpu.VMEM((FRAMES, OWN, CHANNELS), BF16),
            pltpu.VMEM((FRAMES, LONG, CHANNELS), BF16),
            pltpu.VMEM((FRAMES, LONG, CHANNELS), BF16),
            pltpu.VMEM((FRAMES, LONG, SLICE), BF16),
            pltpu.VMEM((FRAMES, LONG, SLICE), BF16),
            pltpu.VMEM((NARROW, 8, SLICE), F32),
            pltpu.VMEM((NARROW, 16, SLICE), F32),
            pltpu.VMEM((BANDS, 16, SLICE), F32),
            pltpu.VMEM((BANDS, 8, SLICE), F32),
            pltpu.VMEM((BANDS, 8, SLICE), F32),
            pltpu.VMEM((NARROW, 16, SLICE), F32),
            pltpu.VMEM((BANDS, 24, SLICE), F32),
            pltpu.VMEM((2, 8, SLICE), F32),
            pltpu.VMEM((FRAMES, BAND, 3 * SLICE), F32),
            pltpu.VMEM((FRAMES, BAND, CHANNELS), F32),
            pltpu.VMEM((FRAMES, LONG, 3 * SLICE), BF16),
            pltpu.VMEM((FRAMES, BAND, SLICE), F32),
            pltpu.VMEM((FRAMES, BAND, SLICE), F32),
            pltpu.VMEM((FRAMES, OWN, CHANNELS), F32),
            pltpu.VMEM((3, FRAMES, BAND, SLICE), BF16),
            pltpu.VMEM((3, FRAMES, BAND, SLICE), BF16),
            pltpu.VMEM((3, FRAMES, OWN, CHANNELS), BF16),
            pltpu.VMEM((3, FRAMES, OWN, CHANNELS), BF16),
            pltpu.VMEM((FRAMES, BAND, SLICE), BF16),
            dma((2, 3)),
            dma((288,)),
            dma((NARROW,)),
            dma((NARROW,)),
            dma((NARROW,)),
            dma((12,)),
            dma((6, BANDS)),
            dma((BANDS,)),
            dma((BANDS,)),
            dma((BANDS, 3)),
            dma((BANDS, 3)),
            dma((2, 3)),
            dma((2, NARROW)),
            dma((17,)),
        ],
        compiler_params=pltpu.CompilerParams(
            collective_id=0, has_side_effects=True, vmem_limit_bytes=62 * 1024 * 1024
        ),
        cost_estimate=pl.CostEstimate(flops=20 * 10**9, bytes_accessed=3 * 10**7, transcendentals=0),
        name="block",
    )(*args)


def last_kernel(act_hbm, one_hbm, two_hbm, exit_hbm, smalls, *refs):
    rows, (entry_out, exit_out, *vectors), rest = refs[:4], refs[4:12], refs[12:]
    row_outs, (act_t, wide_one, wide_two, entry_sum, exit_sum, load_sem, store_sem) = rest[:4], rest[4:]

    loads = []
    for f in range(FRAMES):
        first = pltpu.make_async_copy(act_hbm.at[:, f], act_t.at[:, f], load_sem.at[f])
        if f < FIRST:
            second = pltpu.make_async_copy(one_hbm.at[f], wide_one.at[f], load_sem.at[FRAMES + f])
        else:
            place = f - FIRST
            second = pltpu.make_async_copy(two_hbm.at[place], wide_two.at[place], load_sem.at[FRAMES + f])
        first.start()
        second.start()
        loads.append((first, second))
    through = pltpu.make_async_copy(exit_hbm, exit_sum, load_sem.at[2 * FRAMES])
    through.start()
    for row, ref in enumerate(vectors):
        ref[...] = smalls[row : row + 1, :]
    for source, target in zip(rows, row_outs):
        target[...] = source[...]

    stores = []

    def store(source, target):
        copy = pltpu.make_async_copy(source, target, store_sem.at[len(stores)])
        copy.start()
        stores.append(copy)

    def terms(i, pairs, fresh, last):
        for group in TAP_GROUPS[:4]:
            weight_terms(act_t, wide_one, wide_two, i, pairs, group, entry_sum, fresh)
            if last:
                taps = slice(9 * i + group[0], 9 * i + group[-1] + 1)
                store(entry_sum.at[taps], entry_out.at[taps])

    for parts, pairs in ((loads[:2], PAIRS[1][:2]), (loads[2:], PAIRS[1][2:])):
        for first, second in parts:
            first.wait()
            second.wait()
        terms(1, pairs, pairs[0][0] == 0, pairs[-1][0] == FRAMES - 1)
    through.wait()
    store(exit_sum, exit_out)
    terms(0, PAIRS[0], True, True)
    seen = set()
    for s in range(FRAMES):
        meets = [(i, t) for i in range(3) for other, t in PAIRS[i] if other == s]
        right = jnp.concatenate([tap_rows(wide_one, wide_two, t, 8) for _, t in meets], axis=1)
        left = jnp.concatenate([act_t[c, s] for c in range(BANDS)], axis=1)
        result = jnp.dot(left, right, preferred_element_type=F32)
        for place, (i, _) in enumerate(meets):
            part = result[:, place * SLICE : (place + 1) * SLICE]
            store_taps(entry_sum, [9 * i + 8], part, i not in seen)
            seen.add(i)
    for i in range(3):
        store(entry_sum.at[9 * i + 8 : 9 * i + 9], entry_out.at[9 * i + 8 : 9 * i + 9])
    terms(2, PAIRS[2], True, True)
    for copy in stores:
        copy.wait()


def run_last(act, wide_one, wide_two, smalls, rows, exit_grad):
    vmem = pl.BlockSpec(memory_space=pltpu.VMEM)
    hbm = pl.BlockSpec(memory_space=pl.ANY)
    shape = jax.ShapeDtypeStruct
    taps = shape((27, CHANNELS, SLICE), F32)
    return pl.pallas_call(
        last_kernel,
        out_shape=(taps, taps, *[shape((1, SLICE), F32)] * 6, *[shape(r.shape, r.dtype) for r in rows]),
        in_specs=[hbm] * 4 + [vmem] * 5,
        out_specs=(hbm, hbm, *[vmem] * 10),
        scratch_shapes=[
            pltpu.VMEM(act.shape, BF16),
            pltpu.VMEM(wide_one.shape, BF16),
            pltpu.VMEM(wide_two.shape, BF16),
            pltpu.VMEM(taps.shape, F32),
            pltpu.VMEM(taps.shape, F32),
            pltpu.SemaphoreType.DMA((2 * FRAMES + 1,)),
            pltpu.SemaphoreType.DMA((16,)),
        ],
        compiler_params=pltpu.CompilerParams(vmem_limit_bytes=60 * 1024 * 1024),
        cost_estimate=pl.CostEstimate(flops=14 * 10**9, bytes_accessed=35 * 10**6, transcendentals=0),
        name="last",
    )(act, wide_one, wide_two, exit_grad, smalls, *rows)


def local(
    first_input,
    second_input,
    first_cotangent,
    second_cotangent,
    entry_gain,
    entry_shift,
    entry_kernel,
    entry_bias,
    exit_gain,
    exit_shift,
    exit_kernel,
    exit_bias,
):
    def rows(values):
        return values.reshape(values.shape[0], OWN, CHANNELS)

    vectors = [
        v.reshape(1, SLICE) for v in (entry_gain, entry_shift, entry_bias, exit_gain, exit_shift, exit_bias)
    ]
    taps = [k.reshape(9, 3, CHANNELS, SLICE) for k in (entry_kernel, exit_kernel)]
    *home, smalls, act_one, wide_one, wide_two, exit_grad = run_block(
        [
            rows(first_input),
            rows(second_input),
            rows(first_cotangent),
            rows(second_cotangent),
            *vectors,
            *taps,
        ]
    )
    entry_grad, exit_grad, *rest = run_last(act_one, wide_one, wide_two, smalls, home, exit_grad)
    small, (out_one, out_two, back_one, back_two) = rest[:6], rest[6:]
    totals = (*small, entry_grad, exit_grad)
    groups = lax.axis_size("wide") // BANDS
    if groups > 1:
        totals = tuple(lax.psum(t, "wide") / BANDS for t in totals)
    *small, entry_grad, exit_grad = totals
    small = [t.reshape(SLICE) for t in small]
    return (
        out_one.reshape(first_input.shape),
        out_two.reshape(second_input.shape),
        back_one.reshape(first_input.shape),
        back_two.reshape(second_input.shape),
        small[0],
        small[1],
        entry_grad,
        small[2],
        small[3],
        small[4],
        exit_grad,
        small[5],
    )


def solution(mesh):
    banded = P(None, ("wide", "narrow"), None, None)
    vector = P("narrow")
    kernel = P(None, None, "narrow")
    return jax.shard_map(
        local,
        mesh=mesh,
        in_specs=(banded,) * 4 + (vector, vector, kernel, vector) * 2,
        out_specs=(banded,) * 4 + (vector, vector, kernel, vector) * 2,
        check_vma=False,
    )
```

```python
import functools

import jax
import jax.numpy as jnp
from jax import lax
from jax.experimental import pallas as pl
from jax.experimental.pallas import tpu as pltpu
from jax.sharding import PartitionSpec as P

GROUPS = 32
HEIGHT_ONE = 32
HEIGHT_TWO = 16
CHANNELS = 512
NARROW = 4
BANDS = 8
SLICE = 128
FRAMES = 5
FIRST = 3
BAND = 128
OWN = 32
LONG = 192

EPS = 1e-06
F32 = jnp.float32
BF16 = jnp.bfloat16
MESH = pl.DeviceIdType.MESH

FORWARD = {
    1: ((0, 3, 0), (3, 5, 3)),
    0: ((0, 2, 1), (3, 4, 4)),
    2: ((1, 3, 0), (4, 5, 3)),
}
BACKWARD = {
    1: ((0, 3, 0), (3, 5, 3)),
    0: ((1, 3, 0), (4, 5, 3)),
    2: ((0, 2, 1), (3, 4, 4)),
}


TWO = {"x": True, "a2": False}
ORDER = (
    "prep",
    "st0",
    "xsend",
    "gown",
    "gstart",
    "xh1",
    "T2",
    "xown",
    "z g 1",
    "xh2",
    "act",
    "C1",
    "C1b",
    "C1c",
    "z g 2",
    "T2b",
    "S2",
    "a2start",
    "T2c",
    "rs0",
    "a2own",
    "z g 3",
    "xbulk",
    "y a2 0",
    "padg 0",
    "padg 1",
    "padg 2",
    "z a2 1",
    "o a2 0 1",
    "padg 3",
    "gh2",
    "prepa 0",
    "wx 0 0 0",
    "wx 0 0 1",
    "y a2 1",
    "z a2 2",
    "wx 0 0 2",
    "wx 0 0 3",
    "wx 0 0 4",
    "S3",
    "wx 0 1 0",
    "wx 0 1 1",
    "wx 0 1 2",
    "z x 1",
    "wx 0 1 3",
    "z a2 3",
    "o a2 1 0",
    "wx 0 1 4",
    "mstart",
    "wx 0 2 0",
    "wx 0 2 1",
    "wx 0 2 2",
    "wx 0 2 3",
    "wx 0 2 4",
    "y a2 2",
    "T1",
    "y x 0",
    "o a2 1 1",
    "T1b",
    "T1c",
    "prepa 1",
    "wx 1 0 0",
    "wx 1 0 1",
    "wx 1 0 2",
    "wx 1 0 3",
    "wx 1 0 4",
    "wx 1 1 0",
    "wx 1 1 1",
    "wx 1 1 2",
    "o a2 2 0",
    "wx 1 1 3",
    "wx 1 1 4",
    "z m 1",
    "o a2 2 1",
    "wx 1 2 0",
    "rt",
    "wx 1 2 1",
    "wx 1 2 2",
    "wx 1 2 3",
    "z x 2",
    "wx 1 2 4",
    "prepa 2",
    "wx 2 0 0",
    "wx 2 0 1",
    "wx 2 0 2",
    "o x 0 1",
    "wx 2 0 3",
    "wx 2 0 4",
    "y x 1",
    "C2",
    "y a2 3",
    "C2b",
    "o a2 3 0",
    "wx 2 1 0",
    "C2c",
    "wx 2 1 1",
    "z x 3",
    "gh1",
    "wx 2 1 2",
    "wx 2 1 3",
    "wx 2 1 4",
    "o a2 3 1",
    "y x 2",
    "z m 2",
    "wx 2 2 0",
    "wx 2 2 1",
    "wx 2 2 2",
    "wx 2 2 3",
    "padm 0",
    "padm 1",
    "wx 2 2 4",
    "S4",
    "o x 1 1",
    "y x 3",
    "prepa 3",
    "wx 3 0 0",
    "wx 3 0 1",
    "wx 3 0 2",
    "z m 3",
    "prepx 0",
    "wx 3 0 3",
    "prepx 1",
    "wx 3 0 4",
    "o x 2 1",
    "wx 3 1 0",
    "out",
    "wx 3 1 1",
    "wx 3 1 2",
    "wx 3 1 3",
    "o x 3 1",
    "wx 3 1 4",
    "wx 3 2 0",
    "wx 3 2 1",
    "wx 3 2 2",
    "prepx 2",
    "wx 3 2 3",
    "prepx 3",
    "wx 3 2 4",
    "padm 2",
    "padm 3",
    "S5",
    "fin",
)
REAPS = (47, 71, 94, 118, 136)


def sigmoid_of(values):
    return 0.5 * jnp.tanh(0.5 * values) + 0.5


def group_sum(tile):
    lanes = lax.broadcasted_iota(jnp.int32, tile.shape, 1)
    for step in (1, 2, 4, 8):
        up = pltpu.roll(tile, step, 1)
        down = pltpu.roll(tile, SLICE - step, 1)
        tile = tile + jnp.where((lanes & step) != 0, up, down)
    return tile


def column_ids(rows, width):
    return lax.broadcasted_iota(jnp.int32, (rows, SLICE), 0) % width


def shifted(values, width, k):
    if k == 1:
        return values
    rows = values.shape[0]
    cols = column_ids(rows, width)
    if k == 0:
        return jnp.where(cols == width - 1, 0.0, pltpu.roll(values, rows - 1, 0))
    return jnp.where(cols == 0, 0.0, pltpu.roll(values, 1, 0))


def three_shifts(values, width):
    wide = values.astype(F32)
    return jnp.concatenate([shifted(wide, width, k).astype(BF16) for k in range(3)], axis=1)


def taken(ref, spans, start_one, start_two):
    (a, b, _), (c, d, _) = spans
    one = ref[a:b, start_one : start_one + BAND, :]
    two = ref[c:d, start_two : start_two + BAND, :]
    lanes = ref.shape[2]
    return jnp.concatenate(
        [one.reshape((b - a) * BAND, lanes), two.reshape((d - c) * BAND, lanes)], axis=0
    )


def spread(out, spans, result, fresh):
    (a, b, o), (c, d, p) = spans
    cut = (b - a) * BAND
    one = result[:cut].reshape(b - a, BAND, -1)
    two = result[cut:].reshape(d - c, BAND, -1)
    if fresh:
        out[o : o + b - a] = one
        out[p : p + d - c] = two
    else:
        out[o : o + b - a] += one
        out[p : p + d - c] += two


PARTS = (1, 0, 2)


def conv_forward(act, weights, sums, part):
    i = PARTS[part]
    spans = FORWARD[i]
    rows = jnp.concatenate([taken(act, spans, 32 * j, 16 + 16 * j) for j in range(3)], axis=1)
    taps = weights[3 * i : 3 * i + 3].reshape(3 * CHANNELS, 3 * SLICE)
    spread(sums, spans, jnp.dot(rows, taps, preferred_element_type=F32), part == 0)


def conv_columns(sums, frame, width):
    total = sums[frame, :, SLICE : 2 * SLICE]
    total = total + shifted(sums[frame, :, 0:SLICE], width, 2)
    return total + shifted(sums[frame, :, 2 * SLICE : 3 * SLICE], width, 0)


def conv_backward(grads, weights, sums, part):
    i = PARTS[part]
    spans = BACKWARD[i]
    rows = jnp.concatenate(
        [taken(grads, spans, 64 - 32 * j, 48 - 16 * j) for j in range(3)], axis=1
    )
    taps = jnp.concatenate([weights[3 * i + j] for j in range(3)], axis=1)
    result = lax.dot_general(rows, taps, (((1,), (1,)), ((), ())), preferred_element_type=F32)
    spread(sums, spans, result, part == 0)


def moments(values):
    total = jnp.sum(values, axis=0, keepdims=True)
    off = values - total / values.shape[0]
    return total, jnp.sum(off * off, axis=0, keepdims=True)


def merge(totals, squares, count):
    total = functools.reduce(jnp.add, totals)
    mean = total / (count * len(totals))
    square = functools.reduce(jnp.add, squares)
    for part in totals:
        off = part / count - mean
        square = square + count * off * off
    return total, square


def group_merge(total, square, count):
    mean = total / count
    group_total = group_sum(total)
    off = mean - group_total / (16 * count)
    return group_total, group_sum(square + count * off * off)


def long_row(tile, row):
    return jnp.concatenate([tile[row + k : row + k + 1, :] for k in range(NARROW)], axis=1)


def lanes_of(m):
    if isinstance(m, int):
        return pl.ds(m * SLICE, SLICE)
    return pl.ds(pl.multiple_of(m * SLICE, SLICE), SLICE)


def place_of(k):
    return k % 2 * 2 + k // 2


def store_taps(out, taps, result, fresh):
    for number, tap in enumerate(taps):
        for k in range(NARROW):
            start = place_of(k) * SLICE
            piece = result[start : start + SLICE, number * SLICE : (number + 1) * SLICE]
            rows = slice(k * SLICE, (k + 1) * SLICE)
            if fresh:
                out[tap, rows, :] = piece
            else:
                out[tap, rows, :] += piece


def rows_of(m, offset=0):
    return pl.ds(pl.multiple_of(offset + m * OWN, OWN), OWN)


def clear_pads(three_one, three_two):
    for start in (0, three_one.shape[1] - 32):
        three_one[:, start : start + 32, :] = jnp.zeros((FIRST, 32, 3 * SLICE), BF16)
    for start in (0, three_two.shape[2] - 16):
        three_two[:, :, start : start + 16, :] = jnp.zeros((FRAMES - FIRST, 4, 16, 3 * SLICE), BF16)


def pad_pair(grad_ref, three_one, three_two, pair):
    @pl.loop(0, 2)
    def _(half):
        first = pl.multiple_of(half * BAND, BAND)

        @pl.loop(0, FIRST)
        def _(f):
            start = pl.multiple_of(32 + pair * 2 * BAND + first, 32)
            three_one[f, pl.ds(start, BAND), :] = three_shifts(grad_ref[2 * pair + half, f], 32)

        @pl.loop(0, FRAMES - FIRST)
        def _(f):
            start = pl.multiple_of(16 + first, 16)
            three_two[f, pair, pl.ds(start, BAND), :] = three_shifts(grad_ref[2 * pair + half, FIRST + f], 16)


PAIRS = {
    0: ((0, 1), (1, 2), (3, 4)),
    1: ((0, 0), (1, 1), (2, 2), (3, 3), (4, 4)),
    2: ((1, 0), (2, 1), (4, 3)),
}
TAP_GROUPS = ((0, 1), (2, 3), (4, 5), (6, 7), (8,))


def tap_rows(three_one, three_two, t, tap):
    j, k = tap // 3, tap % 3
    cut = slice(k * SLICE, (k + 1) * SLICE)
    if t < FIRST:
        return three_one[t, (2 - j) * 32 : (2 - j) * 32 + 1024, cut]
    return three_two[t - FIRST, :, (2 - j) * 16 : (2 - j) * 16 + 256, cut].reshape(1024, SLICE)


def weight_terms(act_t, three_one, three_two, i, pairs, group, out, fresh):
    left = jnp.concatenate([act_t[c, s] for s, _ in pairs for c in range(BANDS)], axis=1)
    right = jnp.concatenate(
        [
            jnp.concatenate([tap_rows(three_one, three_two, t, tap) for tap in group], axis=1)
            for _, t in pairs
        ],
        axis=0,
    )
    result = jnp.dot(left, right, preferred_element_type=F32)
    store_taps(out, [9 * i + tap for tap in group], result, fresh)


def pair_weight_terms(act_t, three_one, three_two, pair, i, group, out, fresh):
    def rows(t, tap):
        j, cut = tap // 3, slice(tap % 3 * SLICE, (tap % 3 + 1) * SLICE)
        if t < FIRST:
            start = pl.multiple_of((2 - j) * 32 + pair * 2 * BAND, 32)
            return three_one[t, pl.ds(start, 2 * BAND), cut]
        return three_two[t - FIRST, pair, (2 - j) * 16 : (2 - j) * 16 + 2 * BAND, cut]

    left = jnp.concatenate([act_t[2 * pair + half, s] for s, _ in PAIRS[i] for half in range(2)], axis=1)
    right = jnp.concatenate(
        [jnp.concatenate([rows(t, tap) for tap in group], axis=1) for _, t in PAIRS[i]], axis=0
    )
    result = jnp.dot(left, right, preferred_element_type=F32)
    store_taps(out, [9 * i + tap for tap in group], result, fresh)


def block_kernel(
    x_one, x_two, g_one, g_two, gain_one, shift_one, bias_one, gain_two, shift_two, bias_two,
    entry_hbm, exit_hbm,
    out_one, out_two, back_one, back_two, smalls, act_out, wide_one_out, wide_two_out, exit_grad,
    act_t1, act_t2, g_all, gm_all, three_one, three_two, wide_one, wide_two, exit_sum,
    entry_w, exit_w, own_x, own_g, band_x, band_a, long_g, long_m, params,
    stat_a, stat_b, stat_c, stat_d, stat_e, stat_f, few,
    sums, partial, grad_three, mid, grad_two, grad_one, part_send, part_recv, tail_send, tail_recv, out_send,
    w_sem, send_sem, x_sem, g_sem, p_sem, halo_sem, stat_sem, ga_sem, gm_sem, a1_sem, a2_sem, rs_sem, o_sem, store_sem,
):
    w = lax.axis_index("wide")
    n = lax.axis_index("narrow")
    base = w // BANDS * BANDS
    b = w - base
    z, y = b // 2, b % 2
    has_up, has_down = b > 0, b < BANDS - 1
    pair_up, pair_down = y == 1, y == 0
    flags = lambda f: (has_up, has_down) if f < FIRST else (pair_up, pair_down)
    width_of = lambda f: 32 if f < FIRST else 16
    sub_of = lambda f: 0 if f < FIRST else 1

    sends = []
    used = [0]

    def both(first, second):
        if first is None or second is None:
            return second if first is None else first
        return jnp.logical_and(first, second)

    def under(flag, act):
        if flag is None:
            act()
        else:
            pl.when(flag)(act)

    def make(src, dst, recv, device):
        used[0] += 1
        return pltpu.make_async_remote_copy(
            src_ref=src,
            dst_ref=dst,
            send_sem=send_sem.at[used[0] - 1],
            recv_sem=recv,
            device_id=device,
            device_id_type=MESH,
        )

    def start(copies):
        for copy in copies:
            copy.start()

    def launch(copies, flag=None):
        under(flag, lambda: start(copies))
        sends.append((flag, copies))

    def send(src, dst, recv, device, flag=None):
        launch([make(src, dst, recv, device)], flag)

    def reap(count):
        for flag, copies in sends[:count]:

            def wait_all(copies=copies):
                for copy in copies:
                    copy.wait_send()

            under(flag, wait_all)
        del sends[:count]

    def arrived(dst, recv, flag=None):
        wait = pltpu.make_async_remote_copy(
            src_ref=dst,
            dst_ref=dst,
            send_sem=send_sem.at[0],
            recv_sem=recv,
            device_id=(w, n),
            device_id_type=MESH,
        ).wait_recv
        under(flag, wait)

    def beside(m):
        return (w, m)

    def band_of(c):
        return (base + c, n)

    others = [lax.rem(n + d, NARROW) for d in (1, 2, 3)]
    far = [lax.rem(b + d, BANDS) for d in range(1, BANDS)]
    sib, opp, cross = n ^ 1, n ^ 2, n ^ 3
    beyond = b + 1 - 2 * y
    slant = b - 1 + 2 * y
    above = lax.rem(b + BANDS - 1, BANDS)
    below = lax.rem(b + 1, BANDS)
    up_chip = lax.rem(b + BANDS - 2, BANDS)
    down_chip = lax.rem(b + 2, BANDS)
    pairs_by_distance = [z, z + 1 - 2 * (z % 2), 2 - z // 2, 3 - 3 * (z // 2)]
    mine, mine_long = rows_of(n), rows_of(n, 32)

    sem_of = {"x": a1_sem, "a2": a2_sem, "g": ga_sem, "m": gm_sem}
    array_of = {"x": act_t1, "a2": act_t2, "g": g_all, "m": gm_all}

    def block(name, c, k):
        if name in ("g", "m"):
            return array_of[name].at[c]
        return array_of[name].at[c, :, lanes_of(place_of(k)), :]

    def couple(name, c, k):
        rows = pl.ds(pl.multiple_of(k % 2 * 2 * SLICE, 2 * SLICE), 2 * SLICE)
        return array_of[name].at[c, :, rows, :]

    def sem(name, c, kind):
        return sem_of[name].at[c] if name in ("g", "m") else sem_of[name].at[c, kind]

    def own(name, c):
        return couple(name, c, n) if TWO.get(name) else block(name, c, n)

    def to(ref, name, c, kind, device):
        return make(ref, ref, sem(name, c, kind), device)

    def to_opp(name, c):
        return to(block(name, c, n), name, c, 1, beside(opp))

    def to_sib(name, c):
        return to(couple(name, c, n), name, c, 2, beside(sib))

    def to_beyond(name, c):
        return to(block(name, c, n), name, c, 0, band_of(beyond))

    def at_distance(step, line):
        for sign in (-1, 1) if step else (1,):
            there = None if step == 0 else (z >= step if sign < 0 else z + step <= 3)
            c = lax.rem(b + 2 * sign * step + BANDS, BANDS)
            yield sign, there, c if line == 0 else c + 1 - 2 * y

    def z_step(name, step):
        for sign, there, c in at_distance(step, 0):
            arrived(own(name, c), sem(name, c, 0), there)
            copies = [to_beyond(name, c)]
            if name in ("x", "a2"):
                copies.append(to_sib(name, c) if TWO[name] else to_opp(name, c))
            if step < 3:
                onward, target = (z < 3, down_chip) if sign < 0 else (z > 0, up_chip)
                launch([to(own(name, c), name, c, 0, band_of(target))], both(there, onward))
            launch(copies, there)

    def y_step(name, step):
        for _, there, c in at_distance(step, 1):
            arrived(block(name, c, n), sem(name, c, 0), there)
            launch([to_opp(name, c)], there)

    def o_step(name, step, line):
        for _, there, c in at_distance(step, line):
            arrived(block(name, c, opp), sem(name, c, 1), there)
            launch([to_sib(name, c)], there)

    def begin(name):
        launch([to(own(name, b), name, b, 0, band_of(down_chip))], z < 3)
        launch([to(own(name, b), name, b, 0, band_of(up_chip))], z > 0)
        launch([to_beyond(name, b)])

    def await_sib(name, c):
        arrived(couple(name, c, sib), sem(name, c, 2))

    def to_bands(stat, number):
        for c in far:
            send(stat.at[b], stat.at[b], stat_sem.at[number, b], band_of(c))

    def from_bands(stat, number):
        for c in far:
            arrived(stat.at[b], stat_sem.at[number, c])

    def to_narrow(stat, number):
        for m in others:
            send(stat.at[n], stat.at[n], stat_sem.at[number, n], beside(m))

    def from_narrow(stat, number):
        for m in others:
            arrived(stat.at[n], stat_sem.at[number, m])

    def exchange_rims(ref, first_sem):
        send(ref.at[0:3, 128:160, :], ref.at[0:3, 0:32, :], halo_sem.at[first_sem], band_of(below), has_down)
        send(ref.at[0:3, 32:64, :], ref.at[0:3, 160:192, :], halo_sem.at[first_sem + 1], band_of(above), has_up)
        send(ref.at[3:5, 144:160, :], ref.at[3:5, 16:32, :], halo_sem.at[first_sem + 2], band_of(beyond), pair_down)
        send(ref.at[3:5, 32:48, :], ref.at[3:5, 160:176, :], halo_sem.at[first_sem + 3], band_of(beyond), pair_up)

    def await_rims(ref, first_sem):
        arrived(ref.at[0:3, 0:32, :], halo_sem.at[first_sem], has_up)
        arrived(ref.at[0:3, 160:192, :], halo_sem.at[first_sem + 1], has_down)
        arrived(ref.at[3:5, 16:32, :], halo_sem.at[first_sem + 2], pair_up)
        arrived(ref.at[3:5, 160:176, :], halo_sem.at[first_sem + 3], pair_down)

    stores = []

    def store(source, target, number):
        copy = pltpu.make_async_copy(source, target, store_sem.at[number])
        copy.start()
        stores.append(copy)

    kept = {}
    count_one = 3 * BAND * BANDS
    count_two = 2 * BAND * 2

    def prep():
        loads = []
        for number, (source, target) in enumerate(((exit_hbm, exit_w), (entry_hbm, entry_w))):
            for k in range(3):
                load = pltpu.make_async_copy(
                    source.at[:, k],
                    target.at[:, :, k * SLICE : (k + 1) * SLICE],
                    w_sem.at[number, k],
                )
                load.start()
                loads.append(load)
        kept["loads"] = loads
        own_x[0:FIRST] = x_one[...]
        own_x[FIRST:FRAMES] = x_two[...]
        own_g[0:FIRST] = g_one[...]
        own_g[FIRST:FRAMES] = g_two[...]
        for ref in (params, stat_c, stat_d, stat_f, smalls):
            ref[...] = jnp.zeros_like(ref)
        for ref in (band_x, long_g, long_m):
            for start in (0, 160):
                ref[:, start : start + 32, :] = jnp.zeros((FRAMES, 32, ref.shape[2]), BF16)
        for row, ref in enumerate((gain_one, shift_one, bias_one, gain_two, shift_two, bias_two)):
            params[n, row : row + 1, :] = ref[...].astype(F32)
        band_x[:, mine_long, :] = own_x[...]
        long_g[:, mine_long, :] = own_g[:, :, lanes_of(n)]

        barrier = pltpu.get_barrier_semaphore()
        for m in others:
            pl.semaphore_signal(barrier, inc=1, device_id=beside(m), device_id_type=MESH)
        for c in far:
            pl.semaphore_signal(barrier, inc=1, device_id=band_of(c), device_id_type=MESH)
        for sub, (start, stop) in enumerate(((0, FIRST), (FIRST, FRAMES))):
            values = own_x[start:stop].astype(F32).reshape((stop - start) * OWN, CHANNELS)
            total, square = moments(values)
            cuts = [slice(k * SLICE, (k + 1) * SLICE) for k in range(NARROW)]
            t, s = group_merge(
                jnp.concatenate([total[:, cut] for cut in cuts], axis=0),
                jnp.concatenate([square[:, cut] for cut in cuts], axis=0),
                float(values.shape[0]),
            )
            stat_a[n, 8 * sub : 8 * sub + 4, :] = t
            stat_a[n, 8 * sub + 4 : 8 * sub + 8, :] = s
        pl.semaphore_wait(barrier, NARROW - 1 + BANDS - 1)
        to_narrow(stat_a, 0)
        rims_out()
        for m in others:
            send(own_g.at[:, :, lanes_of(m)], long_g.at[:, mine_long, :], g_sem.at[n], beside(m))
            send(params.at[n], params.at[n], p_sem.at[n], beside(m))
        clear_pads(wide_one, wide_two)
        clear_pads(three_one, three_two)

    def xsend():
        for number, start in enumerate((0, three_one.shape[1] - 32)):
            rows = slice(start, start + 32)
            store(three_one.at[:, rows, :], wide_one_out.at[:, rows, :], 12 + number)
        for m in (opp, sib):
            send(own_x, band_x.at[:, mine_long, :], x_sem.at[n], beside(m))

    def st0():
        from_narrow(stat_a, 0)
        for sub, count in ((0, 3 * OWN * 16.0), (1, 2 * OWN * 16.0)):
            t, s = merge(
                [stat_a[m, 8 * sub : 8 * sub + 4, :] for m in range(NARROW)],
                [stat_a[m, 8 * sub + 4 : 8 * sub + 8, :] for m in range(NARROW)],
                count,
            )
            stat_b[b, 8 * sub : 8 * sub + 4, :] = t
            stat_b[b, 8 * sub + 4 : 8 * sub + 8, :] = s
        to_bands(stat_b, 1)

    def gown():
        for m in others:
            arrived(long_g.at[:, mine_long, :], g_sem.at[m])
        exchange_rims(long_g, 4)
        g_all[b] = long_g[:, 32:160, :]

    def rim_parts():
        return (
            (band_x.at[0:3, 0:32, :], 0, own_x.at[0:3], below, has_down, has_up, 3),
            (band_x.at[3:5, 16:32, :], 2, own_x.at[3:5, 16:32, :], beyond, pair_down, pair_up, 3),
            (band_x.at[0:3, 160:192, :], 1, own_x.at[0:3], above, has_up, has_down, 0),
            (band_x.at[3:5, 160:176, :], 3, own_x.at[3:5, 0:16, :], beyond, pair_up, pair_down, 0),
        )

    def rims_out():
        for ref, number, own, target, gives, _, owner in rim_parts():
            send(own, ref, halo_sem.at[number], band_of(target), both(gives, n == owner))

    def xh1():
        for ref, number, _, _, _, takes, owner in rim_parts():
            flag = both(takes, n == owner)
            arrived(ref, halo_sem.at[number], flag)
            send(ref, ref, halo_sem.at[number], beside(opp), flag)
            send(ref, ref, halo_sem.at[number], beside(sib), flag)

    def xh2():
        for ref, number, _, _, _, takes, owner in rim_parts():
            flag = both(takes, n == (owner + 2) % 4)
            arrived(ref, halo_sem.at[number], flag)
            send(ref, ref, halo_sem.at[number], beside(sib), flag)

    def xh3():
        for ref, number, _, _, _, takes, owner in rim_parts():
            arrived(ref, halo_sem.at[number], both(takes, n % 2 != owner % 2))

    def xown():
        arrived(band_x.at[:, mine_long, :], x_sem.at[opp])
        theirs = band_x.at[:, rows_of(opp, 32), :]
        send(theirs, theirs, x_sem.at[opp], beside(sib))
        arrived(band_x.at[:, mine_long, :], x_sem.at[sib])
        arrived(band_x.at[:, mine_long, :], x_sem.at[cross])

    def first_hidden(values, sub):
        normed = (values - kept["mean_one"][sub]) * kept["inv_one"][sub]
        return normed, normed * kept["gain_long"] + kept["shift_long"]

    def first_active(f, start, stop):
        _, hidden = first_hidden(band_x[f, start:stop].astype(F32), sub_of(f))
        return (hidden * sigmoid_of(hidden)).astype(BF16)

    def act():
        for m in others:
            arrived(params.at[n], p_sem.at[m])
        from_bands(stat_b, 1)
        one_total, one_square = merge(
            [stat_b[c, 0:4, :] for c in range(BANDS)],
            [stat_b[c, 4:8, :] for c in range(BANDS)],
            3 * BAND * 16.0,
        )
        two_total, two_square = merge(
            [stat_b[b, 8:12, :], stat_b[beyond, 8:12, :]],
            [stat_b[b, 12:16, :], stat_b[beyond, 12:16, :]],
            2 * BAND * 16.0,
        )
        kept["mean_one"] = [
            long_row(one_total / (16.0 * count_one), 0),
            long_row(two_total / (16.0 * count_two), 0),
        ]
        kept["inv_one"] = [
            long_row(lax.rsqrt(one_square / (16.0 * count_one) + EPS), 0),
            long_row(lax.rsqrt(two_square / (16.0 * count_two) + EPS), 0),
        ]
        kept["gain_long"] = jnp.concatenate([params[m, 0:1, :] for m in range(NARROW)], axis=1)
        kept["shift_long"] = jnp.concatenate([params[m, 1:2, :] for m in range(NARROW)], axis=1)
        for f in range(FRAMES):
            active = first_active(f, 32, 160)
            band_a[f, 32:160, :] = active
            for k in range(NARROW):
                cut = slice(k * SLICE, (k + 1) * SLICE)
                act_t1[b, f, lanes_of(place_of(k)), :] = active[:, cut].T

    def lay_out(long):
        for f in range(FRAMES):
            grad_three[f] = three_shifts(long[f], width_of(f))

    def t2():
        await_rims(long_g, 4)
        lay_out(long_g)
        for load in kept["loads"][:3]:
            load.wait()
        conv_backward(grad_three, exit_w, partial, 0)

    def t2c():
        conv_backward(grad_three, exit_w, partial, 2)
        part_send[0] = partial[:, :, lanes_of(sib)].astype(BF16)
        part_send[1] = partial[:, :, lanes_of(cross)].astype(BF16)
        for k in range(2):
            send(part_send.at[k], part_recv.at[k], rs_sem.at[0, k], beside(sib))

    def rs0():
        for k in range(2):
            arrived(part_recv.at[k], rs_sem.at[0, k])
        part_send[2] = (partial[:, :, lanes_of(opp)] + part_recv[1].astype(F32)).astype(BF16)
        send(part_send.at[2], part_recv.at[2], rs_sem.at[0, 2], beside(opp))

    def c1():
        xh3()
        for f in range(FRAMES):
            width = width_of(f)
            up, down = flags(f)
            row = first_active(f, 32 - width, 32)
            band_a[f, 32 - width : 32, :] = jnp.where(up, row, jnp.zeros_like(row))
            row = first_active(f, 160, 160 + width)
            band_a[f, 160 : 160 + width, :] = jnp.where(down, row, jnp.zeros_like(row))
        for load in kept["loads"][3:]:
            load.wait()
        conv_forward(band_a, entry_w, sums, 0)

    def c1c():
        conv_forward(band_a, entry_w, sums, 2)
        for f in range(FRAMES):
            mid[f] = conv_columns(sums, f, width_of(f)) + params[n, 2:3, :]
        for sub, (start, stop) in enumerate(((0, FIRST), (FIRST, FRAMES))):
            values = mid[start:stop].reshape((stop - start) * BAND, SLICE)
            total, square = moments(values)
            t, s = group_merge(total, square, float(values.shape[0]))
            stat_c[b, 2 * sub : 2 * sub + 1, :] = t
            stat_c[b, 2 * sub + 1 : 2 * sub + 2, :] = s
        to_bands(stat_c, 2)

    def s2():
        from_bands(stat_c, 2)
        one_total, one_square = merge(
            [stat_c[c, 0:1, :] for c in range(BANDS)],
            [stat_c[c, 1:2, :] for c in range(BANDS)],
            3 * BAND * 16.0,
        )
        two_total, two_square = merge(
            [stat_c[b, 2:3, :], stat_c[beyond, 2:3, :]],
            [stat_c[b, 3:4, :], stat_c[beyond, 3:4, :]],
            2 * BAND * 16.0,
        )
        mean_two = [one_total / (16.0 * count_one), two_total / (16.0 * count_two)]
        kept["inv_two"] = [
            lax.rsqrt(one_square / (16.0 * count_one) + EPS),
            lax.rsqrt(two_square / (16.0 * count_two) + EPS),
        ]
        kept["gain_own"], kept["shift_own"] = params[n, 3:4, :], params[n, 4:5, :]
        for f in range(FRAMES):
            normed = (mid[f] - mean_two[sub_of(f)]) * kept["inv_two"][sub_of(f)]
            mid[f] = normed
            hidden = normed * kept["gain_own"] + kept["shift_own"]
            act_t2[b, f, lanes_of(place_of(n)), :] = (hidden * sigmoid_of(hidden)).astype(BF16).T

    def gh2():
        arrived(part_recv.at[2], rs_sem.at[0, 2])
        rows_sum = [[0.0, 0.0], [0.0, 0.0]]
        for f in range(FRAMES):
            sub = sub_of(f)
            grad = partial[f, :, lanes_of(n)] + part_recv[0, f].astype(F32) + part_recv[2, f].astype(F32)
            hidden = mid[f] * kept["gain_own"] + kept["shift_own"]
            sigmoid = sigmoid_of(hidden)
            grad = grad * (sigmoid * (1.0 + hidden * (1.0 - sigmoid)))
            grad_two[f] = grad
            rows_sum[sub][0] += jnp.sum(grad, axis=0, keepdims=True)
            rows_sum[sub][1] += jnp.sum(grad * mid[f], axis=0, keepdims=True)
        for sub in range(2):
            stat_d[b, 2 * sub : 2 * sub + 1, :] = rows_sum[sub][0]
            stat_d[b, 2 * sub + 1 : 2 * sub + 2, :] = rows_sum[sub][1]
        own = g_all[b].astype(F32).reshape(FRAMES * BAND, SLICE)
        stat_d[b, 4:5, :] = jnp.sum(own, axis=0, keepdims=True)
        to_bands(stat_d, 3)

    def a2start():
        begin("a2")
        launch([to_opp("a2", b)])

    def a2own():
        o_step("a2", 0, 0)

    def s3():
        from_bands(stat_d, 3)
        gain_own = kept["gain_own"]
        all_rows = [
            functools.reduce(jnp.add, [stat_d[c, r : r + 1, :] for c in range(BANDS)]) for r in range(5)
        ]
        smalls[3:4, :] = all_rows[1] + all_rows[3]
        smalls[4:5, :] = all_rows[0] + all_rows[2]
        smalls[5:6, :] = all_rows[4]
        pair_rows = [stat_d[b, r : r + 1, :] + stat_d[beyond, r : r + 1, :] for r in range(4)]
        p_two = [
            group_sum(gain_own * all_rows[0]) / (16.0 * count_one),
            group_sum(gain_own * pair_rows[2]) / (16.0 * count_two),
        ]
        q_two = [
            group_sum(gain_own * all_rows[1]) / (16.0 * count_one),
            group_sum(gain_own * pair_rows[3]) / (16.0 * count_two),
        ]
        bias_sum = 0.0
        for f in range(FRAMES):
            sub = sub_of(f)
            grad = (grad_two[f] * gain_own - p_two[sub] - mid[f] * q_two[sub]) * kept["inv_two"][sub]
            grad = grad.astype(BF16)
            gm_all[b, f] = grad
            long_m[f, 32:160, :] = grad
            bias_sum = bias_sum + jnp.sum(grad.astype(F32), axis=0, keepdims=True)
        stat_f[b, 16:17, :] = bias_sum
        exchange_rims(long_m, 8)

    def t1():
        await_rims(long_m, 8)
        lay_out(long_m)
        conv_backward(grad_three, entry_w, partial, 0)

    def t1c():
        conv_backward(grad_three, entry_w, partial, 2)
        tail_send[0] = partial[:, rows_of(sib), :].astype(BF16)
        tail_send[1] = partial[:, rows_of(cross), :].astype(BF16)
        for k in range(2):
            send(tail_send.at[k], tail_recv.at[k], rs_sem.at[1, k], beside(sib))

    def rt():
        for k in range(2):
            arrived(tail_recv.at[k], rs_sem.at[1, k])
        tail_send[2] = (partial[:, rows_of(opp), :] + tail_recv[1].astype(F32)).astype(BF16)
        send(tail_send.at[2], tail_recv.at[2], rs_sem.at[1, 2], beside(opp))

    def gh1():
        arrived(tail_recv.at[2], rs_sem.at[1, 2])
        for sub, (start, stop) in enumerate(((0, FIRST), (FIRST, FRAMES))):
            first_sum, second_sum = 0.0, 0.0
            for f in range(start, stop):
                grad = partial[f, mine, :] + tail_recv[0, f].astype(F32) + tail_recv[2, f].astype(F32)
                normed, hidden = first_hidden(own_x[f].astype(F32), sub)
                sigmoid = sigmoid_of(hidden)
                grad = grad * (sigmoid * (1.0 + hidden * (1.0 - sigmoid)))
                grad_one[f] = grad
                first_sum = first_sum + jnp.sum(grad, axis=0, keepdims=True)
                second_sum = second_sum + jnp.sum(grad * normed, axis=0, keepdims=True)
            for k in range(NARROW):
                cut = slice(k * SLICE, (k + 1) * SLICE)
                stat_e[n, 8 * sub + k : 8 * sub + k + 1, :] = first_sum[:, cut]
                stat_e[n, 8 * sub + 4 + k : 8 * sub + 5 + k, :] = second_sum[:, cut]
        to_narrow(stat_e, 4)

    def s4():
        from_narrow(stat_e, 4)
        stat_f[b, 0:16, :] = stat_e[0] + stat_e[1] + stat_e[2] + stat_e[3]
        to_bands(stat_f, 5)

    def s5():
        from_bands(stat_f, 5)
        all_sums = functools.reduce(jnp.add, [stat_f[c] for c in range(BANDS)])
        pair_sums = stat_f[b] + stat_f[beyond]
        few[0, 0:4, :] = all_sums[0:4] + all_sums[8:12]
        few[1, 0:4, :] = all_sums[4:8] + all_sums[12:16]
        smalls[0:1, :] = few[1, pl.ds(n, 1), :]
        smalls[1:2, :] = few[0, pl.ds(n, 1), :]
        smalls[2:3, :] = all_sums[16:17]
        gain_rows = jnp.concatenate([params[m, 0:1, :] for m in range(NARROW)], axis=0)
        p_one = [
            long_row(group_sum(gain_rows * all_sums[0:4]) / (16.0 * count_one), 0),
            long_row(group_sum(gain_rows * pair_sums[8:12]) / (16.0 * count_two), 0),
        ]
        q_one = [
            long_row(group_sum(gain_rows * all_sums[4:8]) / (16.0 * count_one), 0),
            long_row(group_sum(gain_rows * pair_sums[12:16]) / (16.0 * count_two), 0),
        ]
        for f in range(FRAMES):
            sub = sub_of(f)
            normed, _ = first_hidden(own_x[f].astype(F32), sub)
            grad = grad_one[f] * kept["gain_long"] - p_one[sub] - normed * q_one[sub]
            grad = (own_g[f].astype(F32) + grad * kept["inv_one"][sub]).astype(BF16)
            if sub == 0:
                back_one[f] = grad
            else:
                back_two[f - FIRST] = grad

    def prepa(number):
        first = 2 * pairs_by_distance[number]
        await_sib("a2", first)
        await_sib("a2", first + 1)

    def pad(name, number, array, one, two):
        pair = pairs_by_distance[number]
        c = 2 * pair + 1 - y
        arrived(block(name, c, n), sem(name, c, 0))
        pad_pair(array, one, two, pair)

    def padg(number):
        pad("g", number, g_all, wide_one, wide_two)

    def c2():
        @pl.loop(0, NARROW)
        def _(k):
            cut = lanes_of(k)
            rows = lanes_of(place_of(k))
            for f in range(FRAMES):
                width = width_of(f)
                up, down = flags(f)
                band_a[f, 32:160, cut] = act_t2[b, f, rows, :].T
                row = act_t2[b - (b + 7) // 8, f, rows, :].T[BAND - width : BAND]
                band_a[f, 32 - width : 32, cut] = jnp.where(up, row, jnp.zeros_like(row))
                row = act_t2[b + (14 - b) // 8, f, rows, :].T[0:width]
                band_a[f, 160 : 160 + width, cut] = jnp.where(down, row, jnp.zeros_like(row))

        conv_forward(band_a, exit_w, sums, 0)

    def c2c():
        conv_forward(band_a, exit_w, sums, 2)
        for f in range(FRAMES):
            total = conv_columns(sums, f, width_of(f)) + params[n, 5:6, :]
            total = total + band_x[f, 32:160, lanes_of(n)].astype(F32)
            out_send[f] = total.astype(BF16)
        for m in others:
            send(out_send.at[0:3, rows_of(m), :], out_one.at[:, :, lanes_of(n)], o_sem.at[0, n], beside(m))
            send(out_send.at[3:5, rows_of(m), :], out_two.at[:, :, lanes_of(n)], o_sem.at[1, n], beside(m))
        out_one[:, :, lanes_of(n)] = out_send[0:3, mine, :]
        out_two[:, :, lanes_of(n)] = out_send[3:5, mine, :]

    def out():
        for m in others:
            arrived(out_one.at[:, :, lanes_of(m)], o_sem.at[0, m])
            arrived(out_two.at[:, :, lanes_of(m)], o_sem.at[1, m])

    def wx(number, place, group):
        i = PARTS[place]
        taps = TAP_GROUPS[group]
        pair = pairs_by_distance[number]
        pair_weight_terms(act_t2, wide_one, wide_two, pair, i, taps, exit_sum, number == 0)
        if number == 3 and group == len(TAP_GROUPS) - 1:
            cut = slice(9 * i, 9 * i + 9)
            store(exit_sum.at[cut], exit_grad.at[cut], 14 + i)

    def prepx(number):
        first = 2 * pairs_by_distance[number]
        if number == 0:
            await_sib("x", beyond)
        else:
            await_sib("x", first)
            await_sib("x", first + 1)
        store(act_t1.at[pl.ds(first, 2)], act_out.at[pl.ds(first, 2)], number)

    def padm(number):
        pad("m", number, gm_all, three_one, three_two)
        pair = pairs_by_distance[number]
        rows = pl.ds(pl.multiple_of(32 + pair * 2 * BAND, 32), 2 * BAND)
        store(three_one.at[:, rows, :], wide_one_out.at[:, rows, :], 4 + number)
        store(three_two.at[:, pair], wide_two_out.at[:, pair], 8 + number)

    def fin():
        reap(len(sends))
        for copy in stores:
            copy.wait()

    backward = lambda weights, part: lambda: conv_backward(grad_three, weights, partial, part)
    forward = lambda weights, part: lambda: conv_forward(band_a, weights, sums, part)
    steps = {
        "prep": prep, "xsend": xsend, "st0": st0, "gown": gown, "xown": xown, "xh1": xh1, "xh2": xh2, "act": act,
        "T2": t2, "T2b": backward(exit_w, 1), "T2c": t2c, "rs0": rs0,
        "C1": c1, "C1b": forward(entry_w, 1), "C1c": c1c,
        "S2": s2, "gh2": gh2, "a2start": a2start, "a2own": a2own, "S3": s3,
        "T1": t1, "T1b": backward(entry_w, 1), "T1c": t1c, "rt": rt, "gh1": gh1, "S4": s4, "S5": s5,
        "C2": c2, "C2b": forward(exit_w, 1), "C2c": c2c, "out": out,
        "padg": padg, "padm": padm, "fin": fin,
        "gstart": lambda: begin("g"),
        "mstart": lambda: begin("m"),
        "xbulk": lambda: begin("x"),
        "z": z_step, "y": y_step, "o": o_step, "wx": wx, "prepx": prepx, "prepa": prepa,
    }
    before = 0
    for number, item in enumerate(ORDER):
        if number in REAPS:
            count, before = before, len(sends) - before
            reap(count)
        word, *rest = item.split()
        steps[word](*[int(r) if r.isdigit() else r for r in rest])


def run_block(args):
    vmem = pl.BlockSpec(memory_space=pltpu.VMEM)
    hbm = pl.BlockSpec(memory_space=pl.ANY)
    dma = pltpu.SemaphoreType.DMA
    shape = jax.ShapeDtypeStruct
    everyone = (BANDS, FRAMES, CHANNELS, BAND)
    wide_one = (FIRST, 34 * 32, 3 * SLICE)
    wide_two = (FRAMES - FIRST, 4, 18 * 16, 3 * SLICE)
    return pl.pallas_call(
        block_kernel,
        out_shape=(
            shape((FIRST, OWN, CHANNELS), BF16),
            shape((FRAMES - FIRST, OWN, CHANNELS), BF16),
            shape((FIRST, OWN, CHANNELS), BF16),
            shape((FRAMES - FIRST, OWN, CHANNELS), BF16),
            shape((8, SLICE), F32),
            shape(everyone, BF16),
            shape(wide_one, BF16),
            shape(wide_two, BF16),
            shape((27, CHANNELS, SLICE), F32),
        ),
        in_specs=[vmem] * 10 + [hbm] * 2,
        out_specs=(vmem,) * 5 + (hbm,) * 4,
        scratch_shapes=[
            pltpu.VMEM(everyone, BF16),
            pltpu.VMEM(everyone, BF16),
            pltpu.VMEM((BANDS, FRAMES, BAND, SLICE), BF16),
            pltpu.VMEM((BANDS, FRAMES, BAND, SLICE), BF16),
            pltpu.VMEM(wide_one, BF16),
            pltpu.VMEM(wide_two, BF16),
            pltpu.VMEM(wide_one, BF16),
            pltpu.VMEM(wide_two, BF16),
            pltpu.VMEM((27, CHANNELS, SLICE), F32),
            pltpu.VMEM((9, CHANNELS, 3 * SLICE), BF16),
            pltpu.VMEM((9, CHANNELS, 3 * SLICE), BF16),
            pltpu.VMEM((FRAMES, OWN, CHANNELS), BF16),
            pltpu.VMEM((FRAMES, OWN, CHANNELS), BF16),
            pltpu.VMEM((FRAMES, LONG, CHANNELS), BF16),
            pltpu.VMEM((FRAMES, LONG, CHANNELS), BF16),
            pltpu.VMEM((FRAMES, LONG, SLICE), BF16),
            pltpu.VMEM((FRAMES, LONG, SLICE), BF16),
            pltpu.VMEM((NARROW, 8, SLICE), F32),
            pltpu.VMEM((NARROW, 16, SLICE), F32),
            pltpu.VMEM((BANDS, 16, SLICE), F32),
            pltpu.VMEM((BANDS, 8, SLICE), F32),
            pltpu.VMEM((BANDS, 8, SLICE), F32),
            pltpu.VMEM((NARROW, 16, SLICE), F32),
            pltpu.VMEM((BANDS, 24, SLICE), F32),
            pltpu.VMEM((2, 8, SLICE), F32),
            pltpu.VMEM((FRAMES, BAND, 3 * SLICE), F32),
            pltpu.VMEM((FRAMES, BAND, CHANNELS), F32),
            pltpu.VMEM((FRAMES, LONG, 3 * SLICE), BF16),
            pltpu.VMEM((FRAMES, BAND, SLICE), F32),
            pltpu.VMEM((FRAMES, BAND, SLICE), F32),
            pltpu.VMEM((FRAMES, OWN, CHANNELS), F32),
            pltpu.VMEM((3, FRAMES, BAND, SLICE), BF16),
            pltpu.VMEM((3, FRAMES, BAND, SLICE), BF16),
            pltpu.VMEM((3, FRAMES, OWN, CHANNELS), BF16),
            pltpu.VMEM((3, FRAMES, OWN, CHANNELS), BF16),
            pltpu.VMEM((FRAMES, BAND, SLICE), BF16),
            dma((2, 3)),
            dma((288,)),
            dma((NARROW,)),
            dma((NARROW,)),
            dma((NARROW,)),
            dma((12,)),
            dma((6, BANDS)),
            dma((BANDS,)),
            dma((BANDS,)),
            dma((BANDS, 3)),
            dma((BANDS, 3)),
            dma((2, 3)),
            dma((2, NARROW)),
            dma((17,)),
        ],
        compiler_params=pltpu.CompilerParams(
            collective_id=0, has_side_effects=True, vmem_limit_bytes=62 * 1024 * 1024
        ),
        cost_estimate=pl.CostEstimate(flops=20 * 10**9, bytes_accessed=3 * 10**7, transcendentals=0),
        name="block",
    )(*args)


def last_kernel(act_hbm, one_hbm, two_hbm, exit_hbm, smalls, *refs):
    rows, (entry_out, exit_out, *vectors), rest = refs[:4], refs[4:12], refs[12:]
    row_outs, (act_t, wide_one, wide_two, entry_sum, exit_sum, load_sem, store_sem) = rest[:4], rest[4:]

    loads = []
    for f in range(FRAMES):
        first = pltpu.make_async_copy(act_hbm.at[:, f], act_t.at[:, f], load_sem.at[f])
        if f < FIRST:
            second = pltpu.make_async_copy(one_hbm.at[f], wide_one.at[f], load_sem.at[FRAMES + f])
        else:
            place = f - FIRST
            second = pltpu.make_async_copy(two_hbm.at[place], wide_two.at[place], load_sem.at[FRAMES + f])
        first.start()
        second.start()
        loads.append((first, second))
    through = pltpu.make_async_copy(exit_hbm, exit_sum, load_sem.at[2 * FRAMES])
    through.start()
    for row, ref in enumerate(vectors):
        ref[...] = smalls[row : row + 1, :]
    for source, target in zip(rows, row_outs):
        target[...] = source[...]

    stores = []

    def store(source, target):
        copy = pltpu.make_async_copy(source, target, store_sem.at[len(stores)])
        copy.start()
        stores.append(copy)

    def terms(i, pairs, fresh, last):
        for group in TAP_GROUPS[:4]:
            weight_terms(act_t, wide_one, wide_two, i, pairs, group, entry_sum, fresh)
            if last:
                taps = slice(9 * i + group[0], 9 * i + group[-1] + 1)
                store(entry_sum.at[taps], entry_out.at[taps])

    for parts, pairs in ((loads[:2], PAIRS[1][:2]), (loads[2:], PAIRS[1][2:])):
        for first, second in parts:
            first.wait()
            second.wait()
        terms(1, pairs, pairs[0][0] == 0, pairs[-1][0] == FRAMES - 1)
    through.wait()
    store(exit_sum, exit_out)
    terms(0, PAIRS[0], True, True)
    seen = set()
    for s in range(FRAMES):
        meets = [(i, t) for i in range(3) for other, t in PAIRS[i] if other == s]
        right = jnp.concatenate([tap_rows(wide_one, wide_two, t, 8) for _, t in meets], axis=1)
        left = jnp.concatenate([act_t[c, s] for c in range(BANDS)], axis=1)
        result = jnp.dot(left, right, preferred_element_type=F32)
        for place, (i, _) in enumerate(meets):
            part = result[:, place * SLICE : (place + 1) * SLICE]
            store_taps(entry_sum, [9 * i + 8], part, i not in seen)
            seen.add(i)
    for i in range(3):
        store(entry_sum.at[9 * i + 8 : 9 * i + 9], entry_out.at[9 * i + 8 : 9 * i + 9])
    terms(2, PAIRS[2], True, True)
    for copy in stores:
        copy.wait()


def run_last(act, wide_one, wide_two, smalls, rows, exit_grad):
    vmem = pl.BlockSpec(memory_space=pltpu.VMEM)
    hbm = pl.BlockSpec(memory_space=pl.ANY)
    shape = jax.ShapeDtypeStruct
    taps = shape((27, CHANNELS, SLICE), F32)
    return pl.pallas_call(
        last_kernel,
        out_shape=(taps, taps, *[shape((1, SLICE), F32)] * 6, *[shape(r.shape, r.dtype) for r in rows]),
        in_specs=[hbm] * 4 + [vmem] * 5,
        out_specs=(hbm, hbm, *[vmem] * 10),
        scratch_shapes=[
            pltpu.VMEM(act.shape, BF16),
            pltpu.VMEM(wide_one.shape, BF16),
            pltpu.VMEM(wide_two.shape, BF16),
            pltpu.VMEM(taps.shape, F32),
            pltpu.VMEM(taps.shape, F32),
            pltpu.SemaphoreType.DMA((2 * FRAMES + 1,)),
            pltpu.SemaphoreType.DMA((16,)),
        ],
        compiler_params=pltpu.CompilerParams(vmem_limit_bytes=60 * 1024 * 1024),
        cost_estimate=pl.CostEstimate(flops=14 * 10**9, bytes_accessed=35 * 10**6, transcendentals=0),
        name="last",
    )(act, wide_one, wide_two, exit_grad, smalls, *rows)


def local(
    first_input,
    second_input,
    first_cotangent,
    second_cotangent,
    entry_gain,
    entry_shift,
    entry_kernel,
    entry_bias,
    exit_gain,
    exit_shift,
    exit_kernel,
    exit_bias,
):
    def rows(values):
        return values.reshape(values.shape[0], OWN, CHANNELS)

    vectors = [
        v.reshape(1, SLICE) for v in (entry_gain, entry_shift, entry_bias, exit_gain, exit_shift, exit_bias)
    ]
    taps = [k.reshape(9, 3, CHANNELS, SLICE) for k in (entry_kernel, exit_kernel)]
    *home, smalls, act_one, wide_one, wide_two, exit_grad = run_block(
        [
            rows(first_input),
            rows(second_input),
            rows(first_cotangent),
            rows(second_cotangent),
            *vectors,
            *taps,
        ]
    )
    entry_grad, exit_grad, *rest = run_last(act_one, wide_one, wide_two, smalls, home, exit_grad)
    small, (out_one, out_two, back_one, back_two) = rest[:6], rest[6:]
    totals = (*small, entry_grad, exit_grad)
    groups = lax.axis_size("wide") // BANDS
    if groups > 1:
        totals = tuple(lax.psum(t, "wide") / BANDS for t in totals)
    *small, entry_grad, exit_grad = totals
    small = [t.reshape(SLICE) for t in small]
    return (
        out_one.reshape(first_input.shape),
        out_two.reshape(second_input.shape),
        back_one.reshape(first_input.shape),
        back_two.reshape(second_input.shape),
        small[0],
        small[1],
        entry_grad,
        small[2],
        small[3],
        small[4],
        exit_grad,
        small[5],
    )


def solution(mesh):
    banded = P(None, ("wide", "narrow"), None, None)
    vector = P("narrow")
    kernel = P(None, None, "narrow")
    return jax.shard_map(
        local,
        mesh=mesh,
        in_specs=(banded,) * 4 + (vector, vector, kernel, vector) * 2,
        out_specs=(banded,) * 4 + (vector, vector, kernel, vector) * 2,
        check_vma=False,
    )
```
